256 devices in a mesh: space: 8 (over x_hi, y), tm: 32 (over x_lo, z, core).
Axes of the slice: x: 4 (x_hi: 2, x_lo: 2; x = x_hi * 2 + x_lo), y: 4, z: 8, core: 2. Of those that a mesh axis runs over, the one named last changes fastest.
Arguments:
- initial_guess: float32 [4, 256, 64, 4, 128], P(None, 'tm', 'space'), may hold values from -6 to 6
- forcing: float32 [4, 256, 64, 4, 128], P(None, 'tm', 'space'), may hold values from -6 to 6
- visc_table: float32 [8], replicated, may hold values from 0.05 to 0.5
- visc_class: int32 [64, 4, 128], P('space'), may hold values from 0 to 7
- inverse_bank: bfloat16 [4, 32, 32], replicated, may hold values from -0.125 to 0.125
- patch_kind: int32 [32, 2, 64], P('space'), may hold values from 0 to 3
Outputs:
- smoothed: float32 [4, 256, 64, 4, 128], P(None, 'tm', 'space')
- coarse: float32 [4, 8, 32768], P(None, None, ('space', 'tm'))
The draws below stay inside these ranges and needn't reach their ends.
All inputs are finite; a program needn't handle non-finite values.
Results may differ from the reference program's by a relative error of at most 0.00096.
Values sent between devices are 32-bit elements; how exact they have to be, the bound alone decides.
A program may use at most 64 MiB of HBM per device.

```python
import math
import jax
import jax.numpy as jnp
from jax import lax

NY = 4
NZ = 128
TS = 8
SWEEPS = 2
LEVELS = 5
KCLASS = 8
KINDS = 4
NX = 64
NT = 256


def set_ends(result, stream_key, least, high):
    longest = result.shape.index(max(result.shape))
    spots = []
    for shift in (0, 1):
        where = [jax.random.randint(jax.random.fold_in(stream_key, axis), (), 0, length) for axis, length in enumerate(result.shape)]
        where[longest] = (where[longest] + shift) % result.shape[longest]
        spots.append(tuple(where))
    return result.at[spots[0]].set(least).at[spots[1]].set(high)


def block_levels(rng, shape, shards, smallest, largest):
    def one(axis_at, shards_of):
        draws = jax.random.uniform(jax.random.fold_in(jax.random.fold_in(rng, 6), axis_at), (shards_of,), jnp.float32, smallest / len(shards), largest / len(shards))
        return jnp.repeat(jnp.exp(draws), shape[axis_at] // shards_of).reshape((-1,) + (1,) * (len(shape) - axis_at - 1))

    factor_of = one(*shards[0])
    for cut in shards[1:]:
        factor_of = factor_of * one(*cut)
    return factor_of


def normal_values(stream_key, extent, scale, most, shards=(), kind=jnp.bfloat16):
    values = scale * jax.random.normal(stream_key, extent, jnp.float32)
    if shards:
        values = values * block_levels(stream_key, extent, shards, -0.22, 0.18)
    return jnp.clip(values, -most, most).astype(kind)


def setup_inputs(seed: int = 0) -> dict:
    key_list = jax.random.split(jax.random.key(seed), 7)
    initial_guess = normal_values(key_list[0], (4, NT, NX, NY, NZ), 1.0, 6.0, ((1, 32), (2, 8)), jnp.float32)
    forcing = normal_values(key_list[1], (4, NT, NX, NY, NZ), 1.0, 6.0, ((1, 32), (2, 8)), jnp.float32)
    visc_table = jnp.clip(jnp.exp(jax.random.uniform(key_list[2], (KCLASS,), jnp.float32, math.log(0.05), math.log(0.5))), 0.05, 0.5)
    visc_class = set_ends(jax.random.randint(key_list[3], (NX, NY, NZ), 0, KCLASS), jax.random.fold_in(key_list[3], 1), 0, KCLASS - 1).astype(jnp.int32)
    inverse_bank = normal_values(key_list[4], (KINDS, 32, 32), 2048 ** -0.5, 0.125)
    patch_kind = set_ends(jax.random.randint(key_list[5], (NX // 2, NY // 2, NZ // 2), 0, KINDS), jax.random.fold_in(key_list[5], 1), 0, KINDS - 1).astype(jnp.int32)
    return dict(initial_guess=initial_guess, forcing=forcing, visc_table=visc_table, visc_class=visc_class, inverse_bank=inverse_bank, patch_kind=patch_kind)


damping = 0.8
mass_weight = 1.0
stabilize = 0.1


def neighbour(array, offset):
    size_x = array.shape[-3] - 2
    size_y = array.shape[-2] - 2
    size_z = array.shape[-1] - 2
    return array[..., 1 + offset[0]:1 + offset[0] + size_x, 1 + offset[1]:1 + offset[1] + size_y, 1 + offset[2]:1 + offset[2] + size_z]


def operate(padded, earlier, visc_pad):
    extended = jnp.pad(padded, ((0, 0), (0, 0), (0, 0), (1, 1), (1, 1)))
    viscous = jnp.pad(visc_pad, ((0, 0), (1, 1), (1, 1)))
    centre = (0, 0, 0)
    centre_visc = neighbour(viscous, centre)
    velocity = neighbour(extended[:3], centre)
    pressure = neighbour(extended[3], centre)
    units = ((1, 0, 0), (0, 1, 0), (0, 0, 1))
    diffusion = jnp.zeros_like(velocity)
    pressure_sum = jnp.zeros_like(pressure)
    gradient = []
    divergence = jnp.zeros_like(pressure)
    for number in range(3):
        unit = units[number]
        minus = (-unit[0], -unit[1], -unit[2])
        for offset in (unit, minus):
            kappa = 0.5 * (centre_visc + neighbour(viscous, offset))
            diffusion = diffusion + kappa * (velocity - neighbour(extended[:3], offset))
            pressure_sum = pressure_sum + neighbour(extended[3], offset)
        gradient.append(0.5 * (neighbour(extended[3], unit) - neighbour(extended[3], minus)))
        divergence = divergence + 0.5 * (neighbour(extended[number], unit) - neighbour(extended[number], minus))
    previous = jnp.concatenate([earlier[:, None], velocity[:, :-1]], axis=1)
    momentum = mass_weight * (velocity - previous) + diffusion + jnp.stack(gradient)
    continuity = stabilize * (6.0 * pressure - pressure_sum) - divergence
    return jnp.concatenate([momentum, continuity[None]], axis=0)


def lookup(classes, table):
    labels = jnp.arange(table.shape[0], dtype=jnp.int32).reshape(-1, 1, 1, 1)
    return jnp.sum(jnp.where(classes[None] == labels, table.reshape(-1, 1, 1, 1), 0.0), axis=0)


def vanka_patches(resid, inverse_bank, patch_kind):
    kinds_count = inverse_bank.shape[0]
    comps, steps, size_x, size_y, size_z = resid.shape
    grouped = resid.reshape(comps, steps, size_x // 2, 2, size_y // 2, 2, size_z // 2, 2)
    grouped = grouped.transpose(0, 3, 5, 7, 1, 2, 4, 6).reshape(8 * comps, -1).astype(jnp.bfloat16)
    products = jnp.dot(inverse_bank.reshape(-1, 8 * comps), grouped, preferred_element_type=jnp.float32)
    products = products.reshape(kinds_count, 8 * comps, steps, size_x // 2, size_y // 2, size_z // 2)
    labels = jnp.arange(kinds_count, dtype=jnp.int32).reshape(-1, 1, 1, 1, 1, 1)
    chosen = jnp.sum(jnp.where(patch_kind[None, None, None] == labels, products, 0.0), axis=0)
    placed = (damping * chosen).reshape(comps, 2, 2, 2, steps, size_x // 2, size_y // 2, size_z // 2)
    return placed.transpose(0, 4, 5, 1, 6, 2, 7, 3).reshape(comps, steps, size_x, size_y, size_z)


def coarsen(level_now, before_step):
    even_steps = level_now[:, 0::2]
    odd_steps = level_now[:, 1::2]
    shifted = jnp.concatenate([before_step[:, None], odd_steps[:, :-1]], axis=1)
    return 0.25 * shifted + 0.5 * even_steps + 0.25 * odd_steps


def reference(initial_guess, forcing, visc_table, visc_class, inverse_bank, patch_kind):
    viscosity = lookup(visc_class, visc_table)
    visc_pad = jnp.pad(viscosity, ((1, 1), (0, 0), (0, 0)))

    def blockwise(iterate, finish):
        def one_block(index):
            start = index * TS
            current = lax.dynamic_slice_in_dim(iterate, start, TS, 1)
            earlier = lax.dynamic_slice_in_dim(iterate, jnp.maximum(start - 1, 0), 1, 1)[:3, 0]
            earlier = jnp.where(index > 0, earlier, jnp.zeros_like(earlier))
            padded = jnp.pad(current, ((0, 0), (0, 0), (1, 1), (0, 0), (0, 0)))
            resid = lax.dynamic_slice_in_dim(forcing, start, TS, 1) - operate(padded, earlier, visc_pad)
            if finish:
                return resid
            return current + vanka_patches(resid, inverse_bank, patch_kind)

        blocks = lax.map(one_block, jnp.arange(NT // TS, dtype=jnp.int32))
        return jnp.moveaxis(blocks, 0, 1).reshape(4, NT, NX, NY, NZ)

    iterate = initial_guess
    for sweep_index in range(SWEEPS):
        iterate = blockwise(iterate, False)
    final = blockwise(iterate, True).reshape(4, NT, NX * NY * NZ)
    coarse = final
    for level_index in range(LEVELS):
        coarse = coarsen(coarse, jnp.zeros_like(coarse[:, 0]))
    return iterate, coarse
```

```python
import functools

import jax
import jax.numpy as jnp
from jax import lax
from jax.experimental import pallas as pl
from jax.experimental.pallas import tpu as pltpu
from jax.sharding import PartitionSpec as P

MESH = pl.DeviceIdType.MESH
F32 = jnp.float32
BF16 = jnp.bfloat16
DAMPING = 0.8
STABILIZE = 0.1


def iota(shape, dim):
    return lax.broadcasted_iota(jnp.int32, shape, dim)


def cell_index(q):
    return (q // 8) * 8 + (q // 4 % 2) * 4 + (q % 2) * 2


def build_bank(bank_ref, lhs_ref):
    j = iota((32, 64), 0)
    q = iota((32, 64), 1)
    spread = (j == cell_index(q % 32) + q // 32).astype(BF16)
    p = iota((64, 32), 0)
    i = iota((64, 32), 1)
    gather = (i == cell_index(p % 32) + p // 32).astype(BF16)
    same = (iota((64, 64), 0) // 2 % 2) == (iota((64, 64), 1) // 2 % 2)
    wide = jnp.dot(bank_ref[...].reshape(128, 32), spread, preferred_element_type=F32).astype(BF16)
    parts = []
    for kind in range(4):
        part = jnp.dot(gather, wide[32 * kind : 32 * kind + 32], preferred_element_type=F32)
        parts.append(jnp.where(same, part, 0.0).astype(BF16))
    lhs_ref[...] = jnp.concatenate(parts, axis=1)


def build_kinds(kind_ref, mask_ref):
    upper = iota((8, 64), 0) // 2 % 2 == 0
    double = (iota((64, 128), 0) == iota((64, 128), 1) // 2).astype(BF16)
    for g in range(4):
        pair = kind_ref[g].astype(F32)
        rows = jnp.where(upper, pair[0:1], pair[1:2]).astype(BF16)
        kinds = jnp.dot(rows, double, preferred_element_type=F32)
        for kind in range(4):
            mask = (kinds == float(kind)).astype(F32)
            mask_ref[g, kind] = jnp.concatenate([mask, mask], axis=0).astype(BF16)


def shift_x(values, left, right):
    first = jnp.concatenate([left, values[0, 0:4]], axis=0)
    last = jnp.concatenate([values[3, 4:8], right], axis=0)
    low = iota((3, 8, 128), 1) < 4
    inner = pltpu.roll(jnp.where(low, values[1:4], values[0:3]), 4, 1)
    return (
        jnp.concatenate([first[None], inner], axis=0),
        jnp.concatenate([inner, last[None]], axis=0),
    )


def shifts_yz(values):
    return (
        pltpu.roll(values, 1, 1),
        pltpu.roll(values, 7, 1),
        pltpu.roll(values, 1, 2),
        pltpu.roll(values, 127, 2),
    )


def edge_masks():
    y = iota((4, 8, 128), 1) % 4
    z = iota((4, 8, 128), 2)
    return y != 0, y != 3, z != 0, z != 127


def build_coefficients(viscosity, left, right, coef_ref):
    xm, xp = shift_x(viscosity, left, right)
    ym, yp, zm, zp = shifts_yz(viscosity)
    total = jnp.ones_like(viscosity)
    for n, (near, mask) in enumerate(zip((xm, xp, ym, yp, zm, zp), (None, None) + edge_masks())):
        if mask is not None:
            near = jnp.where(mask, near, 0.0)
        kappa = 0.5 * (viscosity + near)
        total = total + kappa
        if mask is not None:
            kappa = jnp.where(mask, kappa, 0.0)
        coef_ref[1 + n] = kappa
    coef_ref[0] = total


def residual(t, cur, left, right, forcing, coef_ref):
    mym, myp, mzm, mzp = edge_masks()
    pressure = cur[3, t + 1]
    pxm, pxp = shift_x(pressure, left[3, t], right[3, t])
    pym, pyp, pzm, pzp = shifts_yz(pressure)
    pym = jnp.where(mym, pym, 0.0)
    pyp = jnp.where(myp, pyp, 0.0)
    pzm = jnp.where(mzm, pzm, 0.0)
    pzp = jnp.where(mzp, pzp, 0.0)
    gradients = (pxp - pxm, pyp - pym, pzp - pzm)
    out = []
    divergence = None
    for c in range(3):
        value = cur[c, t + 1]
        xm, xp = shift_x(value, left[c, t], right[c, t])
        ym, yp, zm, zp = shifts_yz(value)
        flow = coef_ref[1] * xm + coef_ref[2] * xp
        flow = flow + (coef_ref[3] * ym + coef_ref[4] * yp)
        flow = flow + (coef_ref[5] * zm + coef_ref[6] * zp)
        out.append(
            forcing[c, t] + cur[c, t] - coef_ref[0] * value + flow - 0.5 * gradients[c]
        )
        if c == 0:
            divergence = xp - xm
        elif c == 1:
            divergence = divergence + (jnp.where(myp, yp, 0.0) - jnp.where(mym, ym, 0.0))
        else:
            divergence = divergence + (jnp.where(mzp, zp, 0.0) - jnp.where(mzm, zm, 0.0))
    around = (pxm + pxp) + (pym + pyp) + (pzm + pzp)
    out.append(
        forcing[3, t] - STABILIZE * (6.0 * pressure - around) + 0.5 * divergence
    )
    return out


def smooth(t, cur, left, right, forcing, coef_ref, lhs_ref, mask_ref, nxt, send_left, send_right):
    resid = residual(t, cur, left, right, forcing, coef_ref)
    even = iota((4, 8, 128), 2) % 2 == 0
    evens = []
    odds = []
    for value in resid:
        evens.append(jnp.where(even, value, pltpu.roll(value, 1, 2)))
        odds.append(jnp.where(even, pltpu.roll(value, 127, 2), value))
    columns = []
    for g in range(4):
        stack = jnp.concatenate([v[g] for v in evens] + [v[g] for v in odds], axis=0)
        stack = stack.astype(BF16).reshape(4, 16, 128)
        masked = [(stack * mask_ref[g, kind]).reshape(64, 128) for kind in range(4)]
        columns.append(jnp.concatenate(masked, axis=0))
    product = jnp.dot(
        lhs_ref[...], jnp.concatenate(columns, axis=1), preferred_element_type=F32
    )
    even = even[0]
    for g in range(4):
        for c in range(4):
            part = product[8 * c : 8 * c + 8, 128 * g : 128 * g + 128]
            other = product[32 + 8 * c : 40 + 8 * c, 128 * g : 128 * g + 128]
            value = cur[c, t + 1, g] + DAMPING * jnp.where(even, part, other)
            nxt[c, t + 1, g] = value
            if g == 0:
                send_left[c, t] = value[0:4]
            if g == 3:
                send_right[c, t] = value[4:8]


def kernel(
    init5, init, forc, table, vclass, bank, kind,
    smoothed, coarse,
    buf0, buf1, buf2, forcing, lefts, rights, outl, outr, vout, vin, coef, lhs, mask, acc, parts, recv,
    load_sem, send_sem, recv_sem, vsend_sem, vrecv_sem, psend_sem, precv_sem,
):
    sx = lax.axis_index("space")
    tb = lax.axis_index("tm")
    bufs = (buf0, buf1, buf2)
    has_left, has_right = sx > 0, sx < 7
    has_before, has_after = tb > 0, tb < 31

    barrier = pltpu.get_barrier_semaphore()

    def greet(step, carry):
        peer = lax.rem(tb + step, 32)
        pl.semaphore_signal(barrier, inc=1, device_id={"tm": peer}, device_id_type=MESH)
        return carry

    lax.fori_loop(1, 32, greet, 0)

    @pl.when(has_left)
    def _():
        pl.semaphore_signal(barrier, inc=1, device_id={"space": sx - 1}, device_id_type=MESH)

    @pl.when(has_right)
    def _():
        pl.semaphore_signal(barrier, inc=1, device_id={"space": sx + 1}, device_id_type=MESH)

    load_a = pltpu.make_async_copy(init, buf0.at[:, 1:9], load_sem.at[0])
    load_b = pltpu.make_async_copy(forc, forcing, load_sem.at[1])
    load_a.start()
    load_b.start()

    pl.semaphore_wait(barrier, 31 + has_left.astype(jnp.int32) + has_right.astype(jnp.int32))

    def exchange(s):
        if s == 0:
            from_left, from_right, last = init5.at[:, :, 0], init5.at[:, :, 7], init.at[0:3, 7]
        else:
            from_left, from_right, last = outl.at[s - 1], outr.at[s - 1], bufs[s].at[0:3, 8]
        to_left = pltpu.make_async_remote_copy(
            from_left, rights.at[s], send_sem.at[s, 0], recv_sem.at[s, 1],
            device_id={"space": sx - 1}, device_id_type=MESH,
        )
        to_right = pltpu.make_async_remote_copy(
            from_right, lefts.at[s], send_sem.at[s, 1], recv_sem.at[s, 0],
            device_id={"space": sx + 1}, device_id_type=MESH,
        )
        to_after = pltpu.make_async_remote_copy(
            last, bufs[s].at[0:3, 0], send_sem.at[s, 2], recv_sem.at[s, 2],
            device_id={"tm": tb + 1}, device_id_type=MESH,
        )
        return to_left, to_right, to_after

    def start(s):
        to_left, to_right, to_after = exchange(s)
        pl.when(has_left)(to_left.start)
        pl.when(has_right)(to_right.start)
        pl.when(has_after)(to_after.start)

    def arrive(s):
        to_left, to_right, to_after = exchange(s)
        pl.when(has_left)(to_right.wait_recv)
        pl.when(has_right)(to_left.wait_recv)
        pl.when(has_before)(to_after.wait_recv)

    def sent(s):
        to_left, to_right, to_after = exchange(s)
        pl.when(has_left)(to_left.wait_send)
        pl.when(has_right)(to_right.wait_send)
        pl.when(has_after)(to_after.wait_send)

    start(0)

    viscosity = jnp.zeros((4, 8, 128), F32)
    for label in range(8):
        viscosity = jnp.where(vclass[...] == label, table[label], viscosity)
    vout[0] = viscosity[0, 0:4]
    vout[1] = viscosity[3, 4:8]
    v_left = pltpu.make_async_remote_copy(
        vout.at[0], vin.at[1], vsend_sem.at[0], vrecv_sem.at[1],
        device_id={"space": sx - 1}, device_id_type=MESH,
    )
    v_right = pltpu.make_async_remote_copy(
        vout.at[1], vin.at[0], vsend_sem.at[1], vrecv_sem.at[0],
        device_id={"space": sx + 1}, device_id_type=MESH,
    )
    pl.when(has_left)(v_left.start)
    pl.when(has_right)(v_right.start)

    @pl.when(sx == 0)
    def _():
        vin[0] = jnp.zeros((4, 128), F32)
        for s in range(3):
            lefts[s] = jnp.zeros((4, 8, 4, 128), F32)

    @pl.when(sx == 7)
    def _():
        vin[1] = jnp.zeros((4, 128), F32)
        for s in range(3):
            rights[s] = jnp.zeros((4, 8, 4, 128), F32)

    @pl.when(tb == 0)
    def _():
        for buf in bufs:
            buf[0:3, 0] = jnp.zeros((3, 4, 8, 128), F32)

    build_bank(bank, lhs)
    build_kinds(kind, mask)
    acc[...] = jnp.zeros_like(acc)

    pl.when(has_left)(v_right.wait_recv)
    pl.when(has_right)(v_left.wait_recv)
    build_coefficients(viscosity, vin[0], vin[1], coef)
    load_a.wait()
    load_b.wait()

    for s in range(2):
        arrive(s)

        def sweep(t, carry, s=s):
            smooth(
                t, bufs[s], lefts.at[s], rights.at[s], forcing, coef, lhs, mask,
                bufs[s + 1], outl.at[s], outr.at[s],
            )
            return carry

        lax.fori_loop(0, 8, sweep, 0)
        start(s + 1)

    store = pltpu.make_async_copy(buf2.at[:, 1:9], smoothed, load_sem.at[2])
    store.start()
    arrive(2)

    def finish(t, carry):
        resid = residual(t, buf2, lefts.at[2], rights.at[2], forcing, coef)
        j = lax.rem(tb, 4) * 8 + t
        near = (32 - j).astype(F32) * (1.0 / 1024.0)
        far = j.astype(F32) * (1.0 / 1024.0)
        for c in range(4):
            acc[0, c] += near * resid[c]
            acc[1, c] += far * resid[c]
        return carry

    lax.fori_loop(0, 8, finish, 0)
    for half in range(2):
        for c in range(4):
            for g in range(4):
                parts[pl.ds(64 * g + 4 * half + c, 8, stride=8), :] = acc[half, c, g]

    def piece(step):
        peer = lax.rem(tb + step, 32)
        return pltpu.make_async_remote_copy(
            parts.at[pl.ds(pl.multiple_of(peer * 8, 8), 8)], recv.at[tb], psend_sem.at[step], precv_sem.at[tb],
            device_id={"tm": peer}, device_id_type=MESH,
        )

    def send(step, carry):
        piece(step).start()
        return carry

    lax.fori_loop(1, 32, send, 0)
    recv[tb] = parts[pl.ds(pl.multiple_of(tb * 8, 8), 8), :]

    def take(step, carry):
        source = lax.rem(tb + step, 32)
        pltpu.make_async_remote_copy(
            parts.at[0:8], recv.at[source], psend_sem.at[step], precv_sem.at[source],
            device_id={"tm": source}, device_id_type=MESH,
        ).wait_recv()
        return carry

    lax.fori_loop(1, 32, take, 0)
    before = jnp.zeros((4, 128), F32)
    for k in range(8):
        block = (recv[4 * k] + recv[4 * k + 1]) + (recv[4 * k + 2] + recv[4 * k + 3])
        level = block[0:4] + before
        before = block[4:8]
        for c in range(4):
            coarse[c, k : k + 1, :] = level[c : c + 1]

    def drain(step, carry):
        piece(step).wait_send()
        return carry

    lax.fori_loop(1, 32, drain, 0)
    for s in range(3):
        sent(s)
    pl.when(has_left)(v_left.wait_send)
    pl.when(has_right)(v_right.wait_send)
    store.wait()


def per_device(initial_guess, forcing, visc_table, visc_class, inverse_bank, patch_kind):
    hbm = pl.BlockSpec(memory_space=pl.ANY)
    vmem = pl.BlockSpec(memory_space=pltpu.VMEM)
    smem = pl.BlockSpec(memory_space=pltpu.SMEM)
    dma = pltpu.SemaphoreType.DMA
    smoothed, coarse = pl.pallas_call(
        kernel,
        out_shape=(
            jax.ShapeDtypeStruct((4, 8, 4, 8, 128), F32),
            jax.ShapeDtypeStruct((4, 8, 128), F32),
        ),
        in_specs=[hbm, hbm, hbm, smem, vmem, vmem, vmem],
        out_specs=(hbm, vmem),
        scratch_shapes=[
            pltpu.VMEM((4, 9, 4, 8, 128), F32),
            pltpu.VMEM((4, 9, 4, 8, 128), F32),
            pltpu.VMEM((4, 9, 4, 8, 128), F32),
            pltpu.VMEM((4, 8, 4, 8, 128), F32),
            pltpu.VMEM((3, 4, 8, 4, 128), F32),
            pltpu.VMEM((3, 4, 8, 4, 128), F32),
            pltpu.VMEM((2, 4, 8, 4, 128), F32),
            pltpu.VMEM((2, 4, 8, 4, 128), F32),
            pltpu.VMEM((2, 4, 128), F32),
            pltpu.VMEM((2, 4, 128), F32),
            pltpu.VMEM((7, 4, 8, 128), F32),
            pltpu.VMEM((64, 256), BF16),
            pltpu.VMEM((4, 4, 16, 128), BF16),
            pltpu.VMEM((2, 4, 4, 8, 128), F32),
            pltpu.VMEM((256, 128), F32),
            pltpu.VMEM((32, 8, 128), F32),
            dma((3,)),
            dma((3, 3)),
            dma((3, 3)),
            dma((2,)),
            dma((2,)),
            dma((32,)),
            dma((32,)),
        ],
        compiler_params=pltpu.CompilerParams(
            collective_id=0, has_side_effects=True, vmem_limit_bytes=24 * 1024 * 1024
        ),
    )(
        initial_guess,
        initial_guess.reshape(4, 8, 4, 8, 128),
        forcing.reshape(4, 8, 4, 8, 128),
        visc_table,
        visc_class.reshape(4, 8, 128),
        inverse_bank,
        patch_kind,
    )
    return smoothed.reshape(4, 8, 8, 4, 128), coarse


def solution(mesh):
    return jax.shard_map(
        per_device,
        mesh=mesh,
        in_specs=(
            P(None, "tm", "space", None, None),
            P(None, "tm", "space", None, None),
            P(),
            P("space", None, None),
            P(),
            P("space", None, None),
        ),
        out_specs=(P(None, "tm", "space", None, None), P(None, None, ("space", "tm"))),
        check_vma=False,
    )
```

```python
import functools

import jax
import jax.numpy as jnp
from jax import lax
from jax.experimental import pallas as pl
from jax.experimental.pallas import tpu as pltpu
from jax.sharding import PartitionSpec as P

MESH = pl.DeviceIdType.MESH
F32 = jnp.float32
BF16 = jnp.bfloat16
DAMPING = 0.8
STABILIZE = 0.1


def iota(shape, dim):
    return lax.broadcasted_iota(jnp.int32, shape, dim)


def cell_index(q):
    return (q // 8) * 8 + (q // 4 % 2) * 4 + (q % 2) * 2


def build_bank(bank_ref, lhs_ref):
    j = iota((32, 64), 0)
    q = iota((32, 64), 1)
    spread = (j == cell_index(q % 32) + q // 32).astype(BF16)
    p = iota((64, 32), 0)
    i = iota((64, 32), 1)
    gather = (i == cell_index(p % 32) + p // 32).astype(BF16)
    same = (iota((64, 64), 0) // 2 % 2) == (iota((64, 64), 1) // 2 % 2)
    wide = jnp.dot(bank_ref[...].reshape(128, 32), spread, preferred_element_type=F32).astype(BF16)
    parts = []
    for kind in range(4):
        part = jnp.dot(gather, wide[32 * kind : 32 * kind + 32], preferred_element_type=F32)
        parts.append(jnp.where(same, part, 0.0).astype(BF16))
    lhs_ref[...] = jnp.concatenate(parts, axis=1)


def build_kinds(kind_ref, mask_ref):
    upper = iota((8, 64), 0) // 2 % 2 == 0
    double = (iota((64, 128), 0) == iota((64, 128), 1) // 2).astype(BF16)
    for g in range(4):
        pair = kind_ref[g].astype(F32)
        rows = jnp.where(upper, pair[0:1], pair[1:2]).astype(BF16)
        kinds = jnp.dot(rows, double, preferred_element_type=F32)
        for kind in range(4):
            mask = (kinds == float(kind)).astype(F32)
            mask_ref[g, kind] = jnp.concatenate([mask, mask], axis=0).astype(BF16)


def shift_x(values, left, right):
    first = jnp.concatenate([left, values[0, 0:4]], axis=0)
    last = jnp.concatenate([values[3, 4:8], right], axis=0)
    low = iota((3, 8, 128), 1) < 4
    inner = pltpu.roll(jnp.where(low, values[1:4], values[0:3]), 4, 1)
    return (
        jnp.concatenate([first[None], inner], axis=0),
        jnp.concatenate([inner, last[None]], axis=0),
    )


def shifts_yz(values):
    return (
        pltpu.roll(values, 1, 1),
        pltpu.roll(values, 7, 1),
        pltpu.roll(values, 1, 2),
        pltpu.roll(values, 127, 2),
    )


def edge_masks():
    y = iota((4, 8, 128), 1) % 4
    z = iota((4, 8, 128), 2)
    return y != 0, y != 3, z != 0, z != 127


def build_coefficients(viscosity, left, right, coef_ref):
    xm, xp = shift_x(viscosity, left, right)
    ym, yp, zm, zp = shifts_yz(viscosity)
    total = jnp.zeros_like(viscosity)
    for n, (near, mask) in enumerate(zip((xm, xp, ym, yp, zm, zp), (None, None) + edge_masks())):
        if mask is not None:
            near = jnp.where(mask, near, 0.0)
        kappa = 0.5 * (viscosity + near)
        total = total + kappa
        if mask is not None:
            kappa = jnp.where(mask, kappa, 0.0)
        coef_ref[1 + n] = kappa
    coef_ref[0] = total + 1.0
    coef_ref[7] = total


def residual(now, left, right, base, diagonal, coef_ref):
    mym, myp, mzm, mzp = edge_masks()
    pressure = now[3]
    pxm, pxp = shift_x(pressure, left[3], right[3])
    pym, pyp, pzm, pzp = shifts_yz(pressure)
    pym = jnp.where(mym, pym, 0.0)
    pyp = jnp.where(myp, pyp, 0.0)
    pzm = jnp.where(mzm, pzm, 0.0)
    pzp = jnp.where(mzp, pzp, 0.0)
    gradients = (pxp - pxm, pyp - pym, pzp - pzm)
    out = []
    divergence = None
    for c in range(3):
        value = now[c]
        xm, xp = shift_x(value, left[c], right[c])
        ym, yp, zm, zp = shifts_yz(value)
        flow = coef_ref[1] * xm + coef_ref[2] * xp
        flow = flow + (coef_ref[3] * ym + coef_ref[4] * yp)
        flow = flow + (coef_ref[5] * zm + coef_ref[6] * zp)
        out.append(base[c] - diagonal * value + flow - 0.5 * gradients[c])
        if c == 0:
            divergence = xp - xm
        elif c == 1:
            divergence = divergence + (jnp.where(myp, yp, 0.0) - jnp.where(mym, ym, 0.0))
        else:
            divergence = divergence + (jnp.where(mzp, zp, 0.0) - jnp.where(mzm, zm, 0.0))
    around = (pxm + pxp) + (pym + pyp) + (pzm + pzp)
    out.append(base[3] - STABILIZE * (6.0 * pressure - around) + 0.5 * divergence)
    return out


def corrections(resid, lhs_ref, mask_ref):
    even = iota((4, 8, 128), 2) % 2 == 0
    evens = []
    odds = []
    for value in resid:
        evens.append(jnp.where(even, value, pltpu.roll(value, 1, 2)))
        odds.append(jnp.where(even, pltpu.roll(value, 127, 2), value))
    columns = []
    for g in range(4):
        stack = jnp.concatenate([v[g] for v in evens] + [v[g] for v in odds], axis=0)
        stack = stack.astype(BF16).reshape(4, 16, 128)
        masked = [(stack * mask_ref[g, kind]).reshape(64, 128) for kind in range(4)]
        columns.append(jnp.concatenate(masked, axis=0))
    product = jnp.dot(
        lhs_ref[...], jnp.concatenate(columns, axis=1), preferred_element_type=F32
    )
    even = even[0]
    out = []
    for g in range(4):
        across = slice(128 * g, 128 * g + 128)
        out.append(
            [
                DAMPING
                * jnp.where(even, product[8 * c : 8 * c + 8, across], product[32 + 8 * c : 40 + 8 * c, across])
                for c in range(4)
            ]
        )
    return out


def time_sums(load):
    plain = load(0)
    ramp = None
    for t in range(1, 8):
        value = load(t)
        plain = plain + value
        ramp = value * float(t) if ramp is None else ramp + value * float(t)
    return plain, ramp


def kernel(
    init5, init, forc, table_in, vclass_in, bank_in, kind_in,
    smoothed, coarse, table, vclass, bank, kind,
    buf0, buf1, forcing, lefts, rights, outl, outr, vout, vin, coef, lhs, mask,
    weighted, weighted_f, gout, gin, parts, edge, recv,
    load_sem, send_sem, recv_sem, tsend_sem, trecv_sem, vsend_sem, vrecv_sem, gsend_sem, grecv_sem, psend_sem, precv_sem,
):
    sx = lax.axis_index("space")
    tb = lax.axis_index("tm")
    has_left, has_right = sx > 0, sx < 7
    has_before, has_after = tb > 0, tb < 31
    to_left, to_right, to_after = {"space": sx - 1}, {"space": sx + 1}, {"tm": tb + 1}

    barrier = pltpu.get_barrier_semaphore()

    @pl.when(has_left)
    def _():
        pl.semaphore_signal(barrier, inc=1, device_id=to_left, device_id_type=MESH)

    @pl.when(has_right)
    def _():
        pl.semaphore_signal(barrier, inc=1, device_id=to_right, device_id_type=MESH)

    def greet(step, carry):
        peer = lax.rem(tb + step, 32)
        pl.semaphore_signal(barrier, inc=1, device_id={"tm": peer}, device_id_type=MESH)
        return carry

    lax.fori_loop(1, 32, greet, 0)

    loads = [
        pltpu.make_async_copy(table_in, table, load_sem.at[0]),
        pltpu.make_async_copy(vclass_in, vclass, load_sem.at[1]),
        pltpu.make_async_copy(bank_in, bank, load_sem.at[2]),
        pltpu.make_async_copy(kind_in, kind, load_sem.at[3]),
        pltpu.make_async_copy(init, buf0.at[:, 1:9], load_sem.at[4]),
        pltpu.make_async_copy(forc, forcing, load_sem.at[5]),
    ]
    for copy in loads:
        copy.start()

    pl.semaphore_wait(barrier, 31 + has_left.astype(jnp.int32) + has_right.astype(jnp.int32))

    def remote(source, target, send, receive, device):
        return pltpu.make_async_remote_copy(
            source, target, send, receive, device_id=device, device_id_type=MESH
        )

    def chunk_copies(s, i):
        if s == 0:
            steps = pl.ds(6 - 2 * i, 2)
            from_left, from_right = init5.at[:, steps, 0], init5.at[:, steps, 7]
        else:
            from_left, from_right = outl.at[i], outr.at[i]
        return (
            remote(from_left, rights.at[s, i], send_sem.at[0], recv_sem.at[s, 1, i], to_left),
            remote(from_right, lefts.at[s, i], send_sem.at[1], recv_sem.at[s, 0, i], to_right),
        )

    def start_chunk(s, i):
        leftward, rightward = chunk_copies(s, i)
        pl.when(has_left)(leftward.start)
        pl.when(has_right)(rightward.start)

    def arrive_chunk(s, i):
        leftward, rightward = chunk_copies(s, i)
        pl.when(has_left)(rightward.wait_recv)
        pl.when(has_right)(leftward.wait_recv)

    later = [
        remote(init.at[0:3, 7], buf0.at[0:3, 0], tsend_sem.at[0], trecv_sem.at[0], to_after),
        remote(buf1.at[0:3, 8], buf1.at[0:3, 0], tsend_sem.at[1], trecv_sem.at[1], to_after),
    ]

    start_chunk(0, 0)
    start_chunk(0, 1)
    pl.when(has_after)(later[0].start)
    start_chunk(0, 2)
    start_chunk(0, 3)

    loads[0].wait()
    loads[1].wait()
    viscosity = jnp.zeros((4, 8, 128), F32)
    for label in range(8):
        viscosity = jnp.where(vclass[...] == label, table[label], viscosity)
    vout[0] = viscosity[0, 0:4]
    vout[1] = viscosity[3, 4:8]
    v_left = remote(vout.at[0], vin.at[1], vsend_sem.at[0], vrecv_sem.at[1], to_left)
    v_right = remote(vout.at[1], vin.at[0], vsend_sem.at[1], vrecv_sem.at[0], to_right)
    pl.when(has_left)(v_left.start)
    pl.when(has_right)(v_right.start)

    @pl.when(sx == 0)
    def _():
        vin[0] = jnp.zeros((4, 128), F32)
        lefts[...] = jnp.zeros_like(lefts)

    @pl.when(sx == 7)
    def _():
        vin[1] = jnp.zeros((4, 128), F32)
        rights[...] = jnp.zeros_like(rights)

    @pl.when(tb == 0)
    def _():
        for buf in (buf0, buf1):
            buf[0:3, 0] = jnp.zeros((3, 4, 8, 128), F32)

    loads[2].wait()
    build_bank(bank, lhs)
    loads[3].wait()
    build_kinds(kind, mask)

    first = (lax.rem(tb, 4) * 8).astype(F32) * (1.0 / 1024.0)

    def weigh(plain, ramp):
        far = first * plain + ramp * (1.0 / 1024.0)
        return plain * (1.0 / 32.0) - far, far

    loads[5].wait()
    for c in range(4):
        near, far = weigh(*time_sums(lambda t, c=c: forcing[c, t]))
        weighted_f[0, c] = near
        weighted_f[1, c] = far

    pl.when(has_left)(v_right.wait_recv)
    pl.when(has_right)(v_left.wait_recv)
    build_coefficients(viscosity, vin[0], vin[1], coef)
    loads[4].wait()

    for s in range(2):
        cur = (buf0, buf1)[s]

        def sweep(i, carry, s=s, cur=cur):
            arrive_chunk(s, i)

            @pl.when(jnp.logical_and(i == 3, has_before))
            def _():
                later[s].wait_recv()

            for part in range(2):
                t = 6 - 2 * i + part
                now = [cur[c, t + 1] for c in range(4)]
                base = [forcing[c, t] + cur[c, t] for c in range(3)] + [forcing[3, t]]
                resid = residual(
                    now,
                    [lefts[s, i, c, part] for c in range(4)],
                    [rights[s, i, c, part] for c in range(4)],
                    base,
                    coef[0],
                    coef,
                )
                change = corrections(resid, lhs, mask)
                for g in range(4):
                    for c in range(4):
                        value = now[c][g] + change[g][c]
                        if s == 1:
                            smoothed[c, t, g] = value
                            continue
                        buf1[c, t + 1, g] = value
                        if g == 0:
                            outl[i, c, part] = value[0:4]
                        if g == 3:
                            outr[i, c, part] = value[4:8]
            if s == 0:
                start_chunk(1, i)

                @pl.when(jnp.logical_and(i == 0, has_after))
                def _():
                    later[1].start()

            return carry

        lax.fori_loop(0, 4, sweep, 0)

    plains = []
    for c in range(4):
        plain, ramp = time_sums(lambda t, c=c: smoothed[c, t])
        near, far = weigh(plain, ramp)
        plains.append(plain * (1.0 / 1024.0))
        for half, value in enumerate((near, far)):
            weighted[half, c] = value
            gout[0, half, c] = value[0, 0:4]
            gout[1, half, c] = value[3, 4:8]
    g_left = remote(gout.at[0], gin.at[1], gsend_sem.at[0], grecv_sem.at[1], to_left)
    g_right = remote(gout.at[1], gin.at[0], gsend_sem.at[1], grecv_sem.at[0], to_right)
    pl.when(has_left)(g_left.start)
    pl.when(has_right)(g_right.start)

    nothing = [jnp.zeros((4, 128), F32)] * 4
    for half in range(2):
        now = [weighted[half, c] for c in range(4)]
        mass = [-p for p in plains] if half == 0 else plains
        base = [weighted_f[half, c] + (mass[c] if c < 3 else 0.0) for c in range(4)]
        resid = residual(now, nothing, nothing, base, coef[7], coef)
        for c in range(4):
            row = 4 * half + c
            for g in range(4):
                parts[pl.ds(64 * g + row, 8, stride=8), :] = resid[c][g]
            edge[pl.ds(row, 4, stride=8), :] = resid[c][0, 0:4]
            edge[pl.ds(32 + row, 4, stride=8), :] = resid[c][3, 4:8]

    def tile(ref, row):
        return ref.at[pl.ds(pl.multiple_of(row * 8, 8), 8)]

    def piece(ref, row, peer):
        return remote(tile(ref, row), recv.at[tb], psend_sem, precv_sem, {"tm": peer})

    def send_inner(step, carry):
        peer = 4 + lax.rem(tb + step, 24)
        pl.when(peer != tb)(piece(parts, peer, peer).start)
        return carry

    lax.fori_loop(0, 24, send_inner, 0)

    @pl.when(jnp.logical_and(tb >= 4, tb < 28))
    def _():
        recv[tb] = tile(parts, tb)[...]

    def add_edge(side, at, coefs, g, rows, sign):
        for half in range(2):
            near = [gin[side, half, c] for c in range(4)]
            for c in range(4):
                if c < 3:
                    extra = coef[coefs, g][rows] * near[c]
                    if c == 0:
                        extra = extra - sign * 0.5 * near[3]
                else:
                    extra = STABILIZE * near[3] + sign * 0.5 * near[0]
                where = pl.ds(at + 4 * half + c, 4, stride=8)
                edge[where, :] = edge[where, :] + extra

    @pl.when(has_left)
    def _():
        g_right.wait_recv()
        add_edge(0, 0, 1, 0, slice(0, 4), -1.0)

    @pl.when(has_right)
    def _():
        g_left.wait_recv()
        add_edge(1, 32, 2, 3, slice(4, 8), 1.0)

    def send_edge(step, carry):
        place = lax.rem(tb + step, 8)
        peer = place + 24 * (place // 4)
        pl.when(peer != tb)(piece(edge, place, peer).start)
        return carry

    lax.fori_loop(0, 8, send_edge, 0)

    @pl.when(tb < 4)
    def _():
        recv[tb] = tile(edge, tb)[...]

    @pl.when(tb >= 28)
    def _():
        recv[tb] = tile(edge, tb - 24)[...]

    @pl.when(has_left)
    def _():
        remote(rights, rights, send_sem.at[0], recv_sem.at[0, 1, 0], to_left).wait_send()
        v_left.wait_send()
        g_left.wait_send()

    @pl.when(has_right)
    def _():
        remote(lefts, lefts, send_sem.at[1], recv_sem.at[0, 0, 0], to_right).wait_send()
        v_right.wait_send()
        g_right.wait_send()

    @pl.when(has_after)
    def _():
        later[0].wait_send()
        later[1].wait_send()

    pieces = remote(recv.at[0:31], recv.at[0:31], psend_sem, precv_sem, {"tm": tb})
    pieces.wait_send()
    pieces.wait_recv()
    before = jnp.zeros((4, 128), F32)
    for k in range(8):
        block = (recv[4 * k] + recv[4 * k + 1]) + (recv[4 * k + 2] + recv[4 * k + 3])
        level = block[0:4] + before
        before = block[4:8]
        for c in range(4):
            coarse[c, k : k + 1, :] = level[c : c + 1]


def per_device(initial_guess, forcing, visc_table, visc_class, inverse_bank, patch_kind):
    hbm = pl.BlockSpec(memory_space=pltpu.HBM)
    vmem = pl.BlockSpec(memory_space=pltpu.VMEM)
    dma = pltpu.SemaphoreType.DMA
    smoothed, coarse = pl.pallas_call(
        kernel,
        out_shape=(
            pltpu.VMEM((4, 8, 4, 8, 128), F32),
            pltpu.VMEM((4, 8, 128), F32),
        ),
        in_specs=[hbm] * 7,
        out_specs=(vmem, vmem),
        scratch_shapes=[
            pltpu.SMEM((8,), F32),
            pltpu.VMEM((4, 8, 128), jnp.int32),
            pltpu.VMEM((4, 32, 32), BF16),
            pltpu.VMEM((4, 2, 64), jnp.int32),
            pltpu.VMEM((4, 9, 4, 8, 128), F32),
            pltpu.VMEM((4, 9, 4, 8, 128), F32),
            pltpu.VMEM((4, 8, 4, 8, 128), F32),
            pltpu.VMEM((2, 4, 4, 2, 4, 128), F32),
            pltpu.VMEM((2, 4, 4, 2, 4, 128), F32),
            pltpu.VMEM((4, 4, 2, 4, 128), F32),
            pltpu.VMEM((4, 4, 2, 4, 128), F32),
            pltpu.VMEM((2, 4, 128), F32),
            pltpu.VMEM((2, 4, 128), F32),
            pltpu.VMEM((8, 4, 8, 128), F32),
            pltpu.VMEM((64, 256), BF16),
            pltpu.VMEM((4, 4, 16, 128), BF16),
            pltpu.VMEM((2, 4, 4, 8, 128), F32),
            pltpu.VMEM((2, 4, 4, 8, 128), F32),
            pltpu.VMEM((2, 2, 4, 4, 128), F32),
            pltpu.VMEM((2, 2, 4, 4, 128), F32),
            pltpu.VMEM((256, 128), F32),
            pltpu.VMEM((64, 128), F32),
            pltpu.VMEM((32, 8, 128), F32),
            dma((6,)),
            dma((2,)),
            dma((2, 2, 4)),
            dma((2,)),
            dma((2,)),
            dma((2,)),
            dma((2,)),
            dma((2,)),
            dma((2,)),
            dma,
            dma,
        ],
        compiler_params=pltpu.CompilerParams(
            collective_id=0, has_side_effects=True, vmem_limit_bytes=60 * 1024 * 1024
        ),
    )(
        initial_guess,
        initial_guess.reshape(4, 8, 4, 8, 128),
        forcing.reshape(4, 8, 4, 8, 128),
        visc_table,
        visc_class.reshape(4, 8, 128),
        inverse_bank,
        patch_kind,
    )
    return smoothed.reshape(4, 8, 8, 4, 128), coarse


def solution(mesh):
    return jax.shard_map(
        per_device,
        mesh=mesh,
        in_specs=(
            P(None, "tm", "space", None, None),
            P(None, "tm", "space", None, None),
            P(),
            P("space", None, None),
            P(),
            P("space", None, None),
        ),
        out_specs=(P(None, "tm", "space", None, None), P(None, None, ("space", "tm"))),
        check_vma=False,
    )
```

```python
import functools

import jax
import jax.numpy as jnp
from jax import lax
from jax.experimental import pallas as pl
from jax.experimental.pallas import tpu as pltpu
from jax.sharding import PartitionSpec as P

MESH = pl.DeviceIdType.MESH
F32 = jnp.float32
BF16 = jnp.bfloat16
DAMPING = 0.8
STABILIZE = 0.1


def iota(shape, dim):
    return lax.broadcasted_iota(jnp.int32, shape, dim)


def cell_index(q):
    return (q // 8) * 8 + (q // 4 % 2) * 4 + (q % 2) * 2


def build_bank(bank_ref, lhs_ref):
    j = iota((32, 64), 0)
    q = iota((32, 64), 1)
    spread = (j == cell_index(q % 32) + q // 32).astype(BF16)
    p = iota((64, 32), 0)
    i = iota((64, 32), 1)
    gather = (i == cell_index(p % 32) + p // 32).astype(BF16)
    same = (iota((64, 64), 0) // 2 % 2) == (iota((64, 64), 1) // 2 % 2)
    wide = jnp.dot(bank_ref[...].reshape(128, 32), spread, preferred_element_type=F32).astype(BF16)
    parts = []
    for kind in range(4):
        part = jnp.dot(gather, wide[32 * kind : 32 * kind + 32], preferred_element_type=F32)
        parts.append(jnp.where(same, part, 0.0).astype(BF16))
    lhs_ref[...] = jnp.concatenate(parts, axis=1)


def kind_maps(kind_ref):
    upper = iota((8, 64), 0) // 2 % 2 == 0
    double = (iota((64, 128), 0) == iota((64, 128), 1) // 2).astype(BF16)
    maps = []
    for g in range(4):
        pair = kind_ref[g].astype(F32)
        rows = jnp.where(upper, pair[0:1], pair[1:2]).astype(BF16)
        maps.append(jnp.dot(rows, double, preferred_element_type=F32))
    return maps


def store_mask(kinds, mask_ref, at):
    for kind in range(4):
        mask = (kinds == float(kind)).astype(F32)
        mask_ref[at, kind] = jnp.concatenate([mask, mask], axis=0).astype(BF16)


def shift_x(values, left, right):
    first = jnp.concatenate([left, values[0, 0:4]], axis=0)
    last = jnp.concatenate([values[3, 4:8], right], axis=0)
    low = iota((3, 8, 128), 1) < 4
    inner = pltpu.roll(jnp.where(low, values[1:4], values[0:3]), 4, 1)
    return (
        jnp.concatenate([first[None], inner], axis=0),
        jnp.concatenate([inner, last[None]], axis=0),
    )


def shifts_yz(values):
    return (
        pltpu.roll(values, 1, 1),
        pltpu.roll(values, 7, 1),
        pltpu.roll(values, 1, 2),
        pltpu.roll(values, 127, 2),
    )


def edge_masks():
    y = iota((4, 8, 128), 1) % 4
    z = iota((4, 8, 128), 2)
    return y != 0, y != 3, z != 0, z != 127


def build_coefficients(viscosity, coef_ref):
    none = jnp.zeros((4, 128), F32)
    xm, xp = shift_x(viscosity, none, none)
    ym, yp, zm, zp = shifts_yz(viscosity)
    g, row = iota((4, 8, 128), 0), iota((4, 8, 128), 1)
    has_xm = jnp.logical_or(g > 0, row >= 4)
    has_xp = jnp.logical_or(g < 3, row < 4)
    total = jnp.zeros_like(viscosity)
    for n, (near, mask) in enumerate(zip((xm, xp, ym, yp, zm, zp), (has_xm, has_xp) + edge_masks())):
        near = jnp.where(mask, near, 0.0)
        kappa = 0.5 * (viscosity + near)
        inner = jnp.where(mask, kappa, 0.0)
        total = total + (inner if n < 2 else kappa)
        coef_ref[1 + n] = inner
    coef_ref[0] = total + 1.0
    coef_ref[7] = total


def residual(now, left, right, base, diagonal, coef_ref):
    mym, myp, mzm, mzp = edge_masks()
    pressure = now[3]
    pxm, pxp = shift_x(pressure, left[3], right[3])
    pym, pyp, pzm, pzp = shifts_yz(pressure)
    pym = jnp.where(mym, pym, 0.0)
    pyp = jnp.where(myp, pyp, 0.0)
    pzm = jnp.where(mzm, pzm, 0.0)
    pzp = jnp.where(mzp, pzp, 0.0)
    gradients = (pxp - pxm, pyp - pym, pzp - pzm)
    out = []
    divergence = None
    for c in range(3):
        value = now[c]
        xm, xp = shift_x(value, left[c], right[c])
        ym, yp, zm, zp = shifts_yz(value)
        flow = coef_ref[1] * xm + coef_ref[2] * xp
        flow = flow + (coef_ref[3] * ym + coef_ref[4] * yp)
        flow = flow + (coef_ref[5] * zm + coef_ref[6] * zp)
        out.append(base[c] - diagonal * value + flow - 0.5 * gradients[c])
        if c == 0:
            divergence = xp - xm
        elif c == 1:
            divergence = divergence + (jnp.where(myp, yp, 0.0) - jnp.where(mym, ym, 0.0))
        else:
            divergence = divergence + (jnp.where(mzp, zp, 0.0) - jnp.where(mzm, zm, 0.0))
    around = (pxm + pxp) + (pym + pyp) + (pzm + pzp)
    out.append(base[3] - STABILIZE * (6.0 * pressure - around) + 0.5 * divergence)
    return out


def face(near, own, kappa, sign):
    out = []
    for c in range(3):
        out.append(kappa * (near[c] if own is None else near[c] - own[c]))
    out[0] = out[0] - (0.5 * sign) * near[3]
    out.append(STABILIZE * near[3] + (0.5 * sign) * near[0])
    return out


def low(rows):
    return jnp.concatenate([rows, jnp.zeros((4, 128), F32)], axis=0)


def high(rows):
    return jnp.concatenate([jnp.zeros((4, 128), F32), rows], axis=0)


def corrections(units, at, lhs_ref, mask_ref):
    even = iota((8, 128), 1) % 2 == 0
    columns = []
    for unit, place in zip(units, at):
        evens = [jnp.where(even, v, pltpu.roll(v, 1, 1)) for v in unit]
        odds = [jnp.where(even, pltpu.roll(v, 127, 1), v) for v in unit]
        stack = jnp.concatenate(evens + odds, axis=0).astype(BF16).reshape(4, 16, 128)
        masked = [(stack * mask_ref[place, kind]).reshape(64, 128) for kind in range(4)]
        columns.append(jnp.concatenate(masked, axis=0))
    product = jnp.dot(
        lhs_ref[...], jnp.concatenate(columns, axis=1), preferred_element_type=F32
    )
    out = []
    for n in range(len(units)):
        across = slice(128 * n, 128 * n + 128)
        out.append(
            [
                DAMPING
                * jnp.where(even, product[8 * c : 8 * c + 8, across], product[32 + 8 * c : 40 + 8 * c, across])
                for c in range(4)
            ]
        )
    return out


def time_sums(load):
    plain = load(0)
    ramp = None
    for t in range(1, 8):
        value = load(t)
        plain = plain + value
        ramp = value * float(t) if ramp is None else ramp + value * float(t)
    return plain, ramp


def steps(body):
    def several(i, carry):
        for j in range(4):
            body(4 * i + j, i, j)
        return carry

    lax.fori_loop(0, 2, several, 0)


def kernel(
    init5, init, forc, table_in, vclass_in, bank_in, kind_in,
    smoothed, coarse, table, vclass, bank, kind,
    f0, f1, forcing, part, part2, e0, e1, lp, rp, lp2, rp2, lres, rres, ares, lcor, rcor, vk_out, vk_in,
    faces, coef, lhs, mask, weighted_f, parts, edges, recv, recv_e,
    load_sem, send_sem, recv_sem, psend_sem, precv_sem, esend_sem, erecv_sem,
):
    sx = lax.axis_index("space")
    tb = lax.axis_index("tm")
    has_left, has_right = sx > 0, sx < 7
    has_before, has_after = tb > 0, tb < 31
    is_edge = jnp.logical_or(jnp.logical_and(tb < 4, has_left), jnp.logical_and(tb >= 28, has_right))
    to_left, to_right, to_after = {"space": sx - 1}, {"space": sx + 1}, {"tm": tb + 1}
    left_after, right_after = {"space": sx - 1, "tm": tb + 1}, {"space": sx + 1, "tm": tb + 1}
    left_before, right_before = {"space": sx - 1, "tm": tb - 1}, {"space": sx + 1, "tm": tb - 1}
    both = jnp.logical_and

    barrier = pltpu.get_barrier_semaphore()

    def greet(condition, device):
        @pl.when(condition)
        def _():
            pl.semaphore_signal(barrier, inc=1, device_id=device, device_id_type=MESH)

    greet(has_left, to_left)
    greet(has_right, to_right)
    greet(both(has_left, has_before), left_before)
    greet(both(has_right, has_before), right_before)

    def greet_peer(step, carry):
        greet(True, {"tm": lax.rem(tb + step, 32)})
        return carry

    lax.fori_loop(1, 32, greet_peer, 0)

    def greet_edge(step, carry):
        peer = lax.rem(tb + step, 32)
        greet(both(tb < 4, has_left), {"space": sx - 1, "tm": peer})
        greet(both(tb >= 28, has_right), {"space": sx + 1, "tm": peer})
        return carry

    lax.fori_loop(0, 32, greet_edge, 0)

    loads = [
        pltpu.make_async_copy(table_in, table, load_sem.at[0]),
        pltpu.make_async_copy(vclass_in, vclass, load_sem.at[1]),
        pltpu.make_async_copy(kind_in, kind, load_sem.at[2]),
        pltpu.make_async_copy(init, f0, load_sem.at[3]),
        pltpu.make_async_copy(forc, forcing, load_sem.at[4]),
        pltpu.make_async_copy(bank_in, bank, load_sem.at[5]),
    ]
    for copy in loads:
        copy.start()

    @pl.when(sx == 0)
    def _():
        vk_in[0] = jnp.zeros((16, 128), F32)
        lp[...] = jnp.zeros_like(lp)
        lres[...] = jnp.zeros_like(lres)

    @pl.when(sx == 7)
    def _():
        vk_in[1] = jnp.zeros((16, 128), F32)
        rp[...] = jnp.zeros_like(rp)
        rres[...] = jnp.zeros_like(rres)

    @pl.when(tb == 0)
    def _():
        e0[...] = jnp.zeros_like(e0)
        ares[...] = jnp.zeros_like(ares)

    @pl.when(jnp.logical_or(tb == 0, sx == 0))
    def _():
        lcor[...] = jnp.zeros_like(lcor)

    @pl.when(jnp.logical_or(tb == 0, sx == 7))
    def _():
        rcor[...] = jnp.zeros_like(rcor)

    @pl.when(jnp.logical_not(is_edge))
    def _():
        recv_e[...] = jnp.zeros_like(recv_e)

    loads[0].wait()
    loads[1].wait()
    viscosity = jnp.zeros((4, 8, 128), F32)
    for label in range(8):
        viscosity = jnp.where(vclass[...] == label, table[label], viscosity)
    build_coefficients(viscosity, coef)
    loads[2].wait()
    maps = kind_maps(kind)
    vk_out[0, 0:4] = viscosity[0, 0:4]
    vk_out[1, 0:4] = viscosity[3, 4:8]
    vk_out[0, 4:8] = jnp.zeros((4, 128), F32)
    vk_out[1, 4:8] = jnp.zeros((4, 128), F32)
    vk_out[0, 8:16] = maps[0]
    vk_out[1, 8:16] = maps[3]
    for g in range(4):
        store_mask(maps[g], mask, g + 1)
    loads[3].wait()
    loads[4].wait()

    nothing = [jnp.zeros((4, 128), F32)] * 4

    def local(t, i, j):
        now = [f0[c, t] for c in range(4)]
        base = [forcing[c, t] for c in range(4)]
        for c in range(3):
            base[c] = base[c] + (f0[c, t - 1] if j else jnp.where(i > 0, f0[c, jnp.maximum(t - 1, 0)], 0.0))
        for c, value in enumerate(residual(now, nothing, nothing, base, coef[0], coef)):
            part[c, t] = value

    steps(local)

    one = lambda condition: condition.astype(jnp.int32)
    pl.semaphore_wait(
        barrier,
        31 + 5 * one(has_left) + 5 * one(has_right)
        + one(both(has_left, has_after)) + one(both(has_right, has_after)),
    )

    def remote(condition, awaited, source, target, n, device):
        copy = pltpu.make_async_remote_copy(
            source, target, send_sem.at[n], recv_sem.at[n], device_id=device, device_id_type=MESH
        )
        return condition, awaited, copy

    round_one = [
        remote(has_left, has_right, vk_out.at[0], vk_in.at[1], 0, to_left),
        remote(has_right, has_left, vk_out.at[1], vk_in.at[0], 1, to_right),
        remote(has_left, has_right, init5.at[:, :, 0], rp, 2, to_left),
        remote(has_right, has_left, init5.at[:, :, 7], lp, 3, to_right),
        remote(has_after, has_before, init.at[0:3, 7], e0, 4, to_after),
        remote(has_after, has_before, part.at[:, 7], ares, 5, to_after),
        remote(both(has_left, has_after), both(has_right, has_before), init.at[:, 7, 0], rcor, 6, left_after),
        remote(both(has_right, has_after), both(has_left, has_before), init.at[:, 7, 3], lcor, 7, right_after),
        remote(has_left, has_right, part.at[:, 0:4, 0], rres.at[:, 0:4], 8, to_left),
        remote(has_right, has_left, part.at[:, 0:4, 3], lres.at[:, 0:4], 9, to_right),
        remote(has_left, has_right, part.at[:, 4:8, 0], rres.at[:, 4:8], 10, to_left),
        remote(has_right, has_left, part.at[:, 4:8, 3], lres.at[:, 4:8], 11, to_right),
    ]
    for condition, _, copy in round_one:
        pl.when(condition)(copy.start)

    def arrive(first, last):
        for _, awaited, copy in round_one[first:last]:
            pl.when(awaited)(copy.wait_recv)

    loads[5].wait()
    build_bank(bank, lhs)
    first = (lax.rem(tb, 4) * 8).astype(F32) * (1.0 / 1024.0)

    def weigh(plain, ramp):
        far = first * plain + ramp * (1.0 / 1024.0)
        return plain * (1.0 / 32.0) - far, far

    for c in range(4):
        near, far = weigh(*time_sums(lambda t, c=c: forcing[c, t]))
        weighted_f[0, c] = near
        weighted_f[1, c] = far

    for pair in ((1, 2), (3, 4), (5, 6), (7,)):
        where = [(t, g) for t in pair for g in (1, 2)]
        units = [[part[c, t, g] for c in range(4)] for t, g in where]
        for (t, g), change in zip(where, corrections(units, [g + 1 for _, g in where], lhs, mask)):
            for c in range(4):
                f1[c, t, g] = f0[c, t, g] + change[c]

    arrive(0, 2)
    faces[0] = 0.5 * (viscosity[0, 0:4] + vk_in[0, 0:4])
    faces[1] = 0.5 * (viscosity[3, 4:8] + vk_in[1, 0:4])
    store_mask(vk_in[0, 8:16], mask, 0)
    store_mask(vk_in[1, 8:16], mask, 5)
    arrive(2, 5)

    units = [[part[c, 0, g] + (e0[c, g] if c < 3 else 0.0) for c in range(4)] for g in (1, 2)]
    for g, change in zip((1, 2), corrections(units, [2, 3], lhs, mask)):
        for c in range(4):
            f1[c, 0, g] = f0[c, 0, g] + change[c]

    def plane(ref, t, side):
        if side == 0:
            return [ref[c, t, 0, 0:4] for c in range(4)]
        return [ref[c, t, 3, 4:8] for c in range(4)]

    def outer(t, i, j):
        units = []
        for side, g, near, sign, place in ((0, 0, lp, -1.0, low), (1, 3, rp, 1.0, high)):
            extra = face([near[c, t] for c in range(4)], plane(f0, t, side), faces[side], sign)
            unit = [part[c, t, g] + place(extra[c]) for c in range(4)]
            if j == 0:
                unit = [unit[c] + jnp.where(i == 0, e0[c, g], 0.0) for c in range(3)] + unit[3:]
            units.append(unit)
        for g, change in zip((0, 3), corrections(units, [1, 4], lhs, mask)):
            for c in range(4):
                f1[c, t, g] = f0[c, t, g] + change[c]

    steps(outer)

    arrive(5, 8)
    units = [[ares[c, g] for c in range(4)] for g in range(4)]
    old = [e0[c, 0, 0:4] for c in range(3)]
    extra = face([lcor[c, 4:8] for c in range(4)], old, faces[0], -1.0)
    units[0] = [units[0][c] + low(extra[c]) for c in range(4)]
    old = [e0[c, 3, 4:8] for c in range(3)]
    extra = face([rcor[c, 0:4] for c in range(4)], old, faces[1], 1.0)
    units[3] = [units[3][c] + high(extra[c]) for c in range(4)]
    for g, change in enumerate(corrections(units, [1, 2, 3, 4], lhs, mask)):
        for c in range(3):
            e1[c, g] = e0[c, g] + change[c]

    def middle(t, i, j):
        now = [f1[c, t] for c in range(4)]
        base = [forcing[c, t] for c in range(4)]
        for c in range(3):
            if j:
                base[c] = base[c] + f1[c, t - 1]
            else:
                base[c] = base[c] + jnp.where(i > 0, f1[c, jnp.maximum(t - 1, 0)], e1[c])
        resid = residual(now, nothing, nothing, base, coef[0], coef)
        for c in range(4):
            part2[c, t] = resid[c]
        units = [[resid[c][g] for c in range(4)] for g in (1, 2)]
        for g, change in zip((1, 2), corrections(units, [2, 3], lhs, mask)):
            for c in range(4):
                smoothed[c, t, g] = now[c][g] + change[c]

    steps(middle)

    arrive(8, 12)
    for c in range(3):
        lres[c, 0] = lres[c, 0] + lcor[c]
        rres[c, 0] = rres[c, 0] + rcor[c]

    def beside(t, i, j):
        lold = [lp[c, t] for c in range(4)]
        rold = [rp[c, t] for c in range(4)]
        extra = face(plane(f0, t, 0), lold, faces[0], 1.0)
        lunit = [lres[c, t] + high(extra[c]) for c in range(4)]
        extra = face(plane(f0, t, 1), rold, faces[1], -1.0)
        runit = [rres[c, t] + low(extra[c]) for c in range(4)]
        lchange, rchange = corrections([lunit, runit], [0, 5], lhs, mask)
        for c in range(4):
            lp2[c, t] = jnp.where(has_left, lold[c] + lchange[c][4:8], 0.0)
            rp2[c, t] = jnp.where(has_right, rold[c] + rchange[c][0:4], 0.0)

    steps(beside)

    def ends(t, i, j):
        units = []
        for side, g, near, sign, place in ((0, 0, lp2, -1.0, low), (1, 3, rp2, 1.0, high)):
            extra = face([near[c, t] for c in range(4)], plane(f1, t, side), faces[side], sign)
            units.append([part2[c, t, g] + place(extra[c]) for c in range(4)])
        for g, change in zip((0, 3), corrections(units, [1, 4], lhs, mask)):
            for c in range(4):
                smoothed[c, t, g] = f1[c, t, g] + change[c]

    steps(ends)

    fields = ([], [])
    mass = []
    for c in range(4):
        plain, ramp = time_sums(lambda t, c=c: smoothed[c, t])
        near, far = weigh(plain, ramp)
        fields[0].append(near)
        fields[1].append(far)
        mass.append(plain * (1.0 / 1024.0))
    for half in range(2):
        now = fields[half]
        for side, g, sign in ((0, 0, 1.0), (1, 3, -1.0)):
            rows = slice(4 * side, 4 * side + 4)
            for c, value in enumerate(face([v[g, rows] for v in now], None, faces[side], sign)):
                edges[side, pl.ds(4 * half + c, 4, stride=8), :] = value
    for half in range(2):
        now = fields[half]
        base = [weighted_f[half, c] for c in range(4)]
        for c in range(3):
            base[c] = base[c] - mass[c] if half == 0 else base[c] + mass[c]
        resid = residual(now, nothing, nothing, base, coef[7], coef)
        for c in range(4):
            row = 4 * half + c
            for g in range(4):
                value = resid[c][g]
                if c < 3 and g == 0:
                    value = value - low(faces[0] * now[c][0, 0:4])
                if c < 3 and g == 3:
                    value = value - high(faces[1] * now[c][3, 4:8])
                parts[pl.ds(64 * g + row, 8, stride=8), :] = value

    def tile(ref, row):
        return ref.at[pl.ds(pl.multiple_of(row * 8, 8), 8)]

    def edge_piece(side, y, device):
        return pltpu.make_async_remote_copy(
            edges.at[side, pl.ds(8 * y, 8)], recv_e.at[tb], esend_sem.at[side], erecv_sem,
            device_id=device, device_id_type=MESH,
        )

    @pl.when(has_left)
    def _():
        for y in range(4):
            edge_piece(0, y, {"space": sx - 1, "tm": 28 + y}).start()

    @pl.when(has_right)
    def _():
        for y in range(4):
            edge_piece(1, y, {"space": sx + 1, "tm": y}).start()

    def send(step, carry):
        k = step // 4
        odd = lax.rem(k, 2)
        dz = 4 + (k // 2) * (1 - odd) - ((k + 1) // 2) * odd
        column = lax.rem(lax.rem(tb, 16) + 2 * dz, 16)
        column = column // 2 * 2 + lax.rem(tb + step, 2)
        peer = lax.rem(tb // 16 + 1 + lax.rem(step // 2, 2), 2) * 16 + column

        @pl.when(peer != tb)
        def _():
            pltpu.make_async_remote_copy(
                tile(parts, peer), recv.at[tb], psend_sem, precv_sem,
                device_id={"tm": peer}, device_id_type=MESH,
            ).start()

        return carry

    lax.fori_loop(0, 32, send, 0)
    recv[tb] = tile(parts, tb)[...]

    for condition, _, copy in round_one:
        pl.when(condition)(copy.wait_send)

    def sent_edges(side, device):
        pltpu.make_async_remote_copy(
            edges.at[side], edges.at[side], esend_sem.at[side], erecv_sem,
            device_id=device, device_id_type=MESH,
        ).wait_send()

    pl.when(has_left)(lambda: sent_edges(0, to_left))
    pl.when(has_right)(lambda: sent_edges(1, to_right))
    pieces = pltpu.make_async_remote_copy(
        recv.at[0:31], recv.at[0:31], psend_sem, precv_sem, device_id=to_after, device_id_type=MESH
    )
    pieces.wait_send()
    pieces.wait_recv()

    @pl.when(is_edge)
    def _():
        pltpu.make_async_remote_copy(
            recv_e, recv_e, psend_sem, erecv_sem, device_id=to_after, device_id_type=MESH
        ).wait_recv()

    before = jnp.zeros((4, 128), F32)
    for k in range(8):
        block = (recv[4 * k] + recv[4 * k + 1]) + (recv[4 * k + 2] + recv[4 * k + 3])
        block = block + (
            (recv_e[4 * k] + recv_e[4 * k + 1]) + (recv_e[4 * k + 2] + recv_e[4 * k + 3])
        )
        level = block[0:4] + before
        before = block[4:8]
        for c in range(4):
            coarse[c, k : k + 1, :] = level[c : c + 1]


def per_device(initial_guess, forcing, visc_table, visc_class, inverse_bank, patch_kind):
    hbm = pl.BlockSpec(memory_space=pltpu.HBM)
    vmem = pl.BlockSpec(memory_space=pltpu.VMEM)
    dma = pltpu.SemaphoreType.DMA
    smoothed, coarse = pl.pallas_call(
        kernel,
        out_shape=(
            pltpu.VMEM((4, 8, 4, 8, 128), F32),
            pltpu.VMEM((4, 8, 128), F32),
        ),
        in_specs=[hbm] * 7,
        out_specs=(vmem, vmem),
        scratch_shapes=[
            pltpu.SMEM((8,), F32),
            pltpu.VMEM((4, 8, 128), jnp.int32),
            pltpu.VMEM((4, 32, 32), BF16),
            pltpu.VMEM((4, 2, 64), jnp.int32),
            pltpu.VMEM((4, 8, 4, 8, 128), F32),
            pltpu.VMEM((4, 8, 4, 8, 128), F32),
            pltpu.VMEM((4, 8, 4, 8, 128), F32),
            pltpu.VMEM((4, 8, 4, 8, 128), F32),
            pltpu.VMEM((4, 8, 4, 8, 128), F32),
            pltpu.VMEM((3, 4, 8, 128), F32),
            pltpu.VMEM((3, 4, 8, 128), F32),
            pltpu.VMEM((4, 8, 4, 128), F32),
            pltpu.VMEM((4, 8, 4, 128), F32),
            pltpu.VMEM((4, 8, 4, 128), F32),
            pltpu.VMEM((4, 8, 4, 128), F32),
            pltpu.VMEM((4, 8, 8, 128), F32),
            pltpu.VMEM((4, 8, 8, 128), F32),
            pltpu.VMEM((4, 4, 8, 128), F32),
            pltpu.VMEM((4, 8, 128), F32),
            pltpu.VMEM((4, 8, 128), F32),
            pltpu.VMEM((2, 16, 128), F32),
            pltpu.VMEM((2, 16, 128), F32),
            pltpu.VMEM((2, 4, 128), F32),
            pltpu.VMEM((8, 4, 8, 128), F32),
            pltpu.VMEM((64, 256), BF16),
            pltpu.VMEM((6, 4, 16, 128), BF16),
            pltpu.VMEM((2, 4, 4, 8, 128), F32),
            pltpu.VMEM((256, 128), F32),
            pltpu.VMEM((2, 32, 128), F32),
            pltpu.VMEM((32, 8, 128), F32),
            pltpu.VMEM((32, 8, 128), F32),
            dma((6,)),
            dma((12,)),
            dma((12,)),
            dma,
            dma,
            dma((2,)),
            dma,
        ],
        compiler_params=pltpu.CompilerParams(
            collective_id=0, has_side_effects=True, vmem_limit_bytes=60 * 1024 * 1024
        ),
    )(
        initial_guess,
        initial_guess.reshape(4, 8, 4, 8, 128),
        forcing.reshape(4, 8, 4, 8, 128),
        visc_table,
        visc_class.reshape(4, 8, 128),
        inverse_bank,
        patch_kind,
    )
    return smoothed.reshape(4, 8, 8, 4, 128), coarse


def solution(mesh):
    return jax.shard_map(
        per_device,
        mesh=mesh,
        in_specs=(
            P(None, "tm", "space", None, None),
            P(None, "tm", "space", None, None),
            P(),
            P("space", None, None),
            P(),
            P("space", None, None),
        ),
        out_specs=(P(None, "tm", "space", None, None), P(None, None, ("space", "tm"))),
        check_vma=False,
    )
```

```python
import functools

import jax
import jax.numpy as jnp
from jax import lax
from jax.experimental import pallas as pl
from jax.experimental.pallas import tpu as pltpu
from jax.sharding import PartitionSpec as P

MESH = pl.DeviceIdType.MESH
F32 = jnp.float32
BF16 = jnp.bfloat16
DAMPING = 0.8
STABILIZE = 0.1


def iota(shape, dim):
    return lax.broadcasted_iota(jnp.int32, shape, dim)


def cell_index(q):
    return (q // 8) * 8 + (q // 4 % 2) * 4 + (q % 2) * 2


def build_bank(bank_ref, lhs_ref):
    j = iota((32, 64), 0)
    q = iota((32, 64), 1)
    spread = (j == cell_index(q % 32) + q // 32).astype(BF16)
    p = iota((64, 32), 0)
    i = iota((64, 32), 1)
    gather = (i == cell_index(p % 32) + p // 32).astype(BF16)
    same = (iota((64, 64), 0) // 2 % 2) == (iota((64, 64), 1) // 2 % 2)
    wide = jnp.dot(bank_ref[...].reshape(128, 32), spread, preferred_element_type=F32).astype(BF16)
    parts = []
    for kind in range(4):
        part = jnp.dot(gather, wide[32 * kind : 32 * kind + 32], preferred_element_type=F32)
        parts.append(jnp.where(same, part, 0.0).astype(BF16))
    lhs_ref[...] = jnp.concatenate(parts, axis=1)


def kind_maps(kind_ref):
    upper = iota((8, 64), 0) // 2 % 2 == 0
    double = (iota((64, 128), 0) == iota((64, 128), 1) // 2).astype(BF16)
    maps = []
    for g in range(4):
        pair = kind_ref[g].astype(F32)
        rows = jnp.where(upper, pair[0:1], pair[1:2]).astype(BF16)
        maps.append(jnp.dot(rows, double, preferred_element_type=F32))
    return maps


def store_mask(kinds, mask_ref, at):
    for kind in range(4):
        mask = (kinds == float(kind)).astype(F32)
        mask_ref[at, kind] = jnp.concatenate([mask, mask], axis=0).astype(BF16)


def shift_x(values, left, right):
    first = jnp.concatenate([left, values[0, 0:4]], axis=0)
    last = jnp.concatenate([values[3, 4:8], right], axis=0)
    low = iota((3, 8, 128), 1) < 4
    inner = pltpu.roll(jnp.where(low, values[1:4], values[0:3]), 4, 1)
    return (
        jnp.concatenate([first[None], inner], axis=0),
        jnp.concatenate([inner, last[None]], axis=0),
    )


def shifts_yz(values):
    return (
        pltpu.roll(values, 1, 1),
        pltpu.roll(values, 7, 1),
        pltpu.roll(values, 1, 2),
        pltpu.roll(values, 127, 2),
    )


def edge_masks():
    y = iota((4, 8, 128), 1) % 4
    z = iota((4, 8, 128), 2)
    return y != 0, y != 3, z != 0, z != 127


def build_coefficients(viscosity, coef_ref):
    none = jnp.zeros((4, 128), F32)
    xm, xp = shift_x(viscosity, none, none)
    ym, yp, zm, zp = shifts_yz(viscosity)
    g, row = iota((4, 8, 128), 0), iota((4, 8, 128), 1)
    has_xm = jnp.logical_or(g > 0, row >= 4)
    has_xp = jnp.logical_or(g < 3, row < 4)
    total = jnp.zeros_like(viscosity)
    for n, (near, mask) in enumerate(zip((xm, xp, ym, yp, zm, zp), (has_xm, has_xp) + edge_masks())):
        near = jnp.where(mask, near, 0.0)
        kappa = 0.5 * (viscosity + near)
        inner = jnp.where(mask, kappa, 0.0)
        total = total + (inner if n < 2 else kappa)
        coef_ref[1 + n] = inner
    coef_ref[0] = total + 1.0
    coef_ref[7] = total


def residual(now, left, right, base, diagonal, coef_ref):
    mym, myp, mzm, mzp = edge_masks()
    pressure = now[3]
    pxm, pxp = shift_x(pressure, left[3], right[3])
    pym, pyp, pzm, pzp = shifts_yz(pressure)
    pym = jnp.where(mym, pym, 0.0)
    pyp = jnp.where(myp, pyp, 0.0)
    pzm = jnp.where(mzm, pzm, 0.0)
    pzp = jnp.where(mzp, pzp, 0.0)
    gradients = (pxp - pxm, pyp - pym, pzp - pzm)
    out = []
    divergence = None
    for c in range(3):
        value = now[c]
        xm, xp = shift_x(value, left[c], right[c])
        ym, yp, zm, zp = shifts_yz(value)
        flow = coef_ref[1] * xm + coef_ref[2] * xp
        flow = flow + (coef_ref[3] * ym + coef_ref[4] * yp)
        flow = flow + (coef_ref[5] * zm + coef_ref[6] * zp)
        out.append(base[c] - diagonal * value + flow - 0.5 * gradients[c])
        if c == 0:
            divergence = xp - xm
        elif c == 1:
            divergence = divergence + (jnp.where(myp, yp, 0.0) - jnp.where(mym, ym, 0.0))
        else:
            divergence = divergence + (jnp.where(mzp, zp, 0.0) - jnp.where(mzm, zm, 0.0))
    around = (pxm + pxp) + (pym + pyp) + (pzm + pzp)
    out.append(base[3] - STABILIZE * (6.0 * pressure - around) + 0.5 * divergence)
    return out


def face(near, own, kappa, sign):
    out = []
    for c in range(3):
        out.append(kappa * (near[c] if own is None else near[c] - own[c]))
    out[0] = out[0] - (0.5 * sign) * near[3]
    out.append(STABILIZE * near[3] + (0.5 * sign) * near[0])
    return out


def low(rows):
    return jnp.concatenate([rows, jnp.zeros((4, 128), F32)], axis=0)


def high(rows):
    return jnp.concatenate([jnp.zeros((4, 128), F32), rows], axis=0)


def corrections(units, at, lhs_ref, mask_ref):
    even = iota((8, 128), 1) % 2 == 0
    columns = []
    for unit, place in zip(units, at):
        evens = [jnp.where(even, v, pltpu.roll(v, 1, 1)) for v in unit]
        odds = [jnp.where(even, pltpu.roll(v, 127, 1), v) for v in unit]
        stack = jnp.concatenate(evens + odds, axis=0).astype(BF16).reshape(4, 16, 128)
        masked = [(stack * mask_ref[place, kind]).reshape(64, 128) for kind in range(4)]
        columns.append(jnp.concatenate(masked, axis=0))
    product = jnp.dot(
        lhs_ref[...], jnp.concatenate(columns, axis=1), preferred_element_type=F32
    )
    out = []
    for n in range(len(units)):
        across = slice(128 * n, 128 * n + 128)
        out.append(
            [
                DAMPING
                * jnp.where(even, product[8 * c : 8 * c + 8, across], product[32 + 8 * c : 40 + 8 * c, across])
                for c in range(4)
            ]
        )
    return out


def time_sums(load):
    plain = load(0)
    ramp = None
    for t in range(1, 8):
        value = load(t)
        plain = plain + value
        ramp = value * float(t) if ramp is None else ramp + value * float(t)
    return plain, ramp


def steps(body):
    def several(i, carry):
        for j in range(4):
            body(4 * i + j, i, j)
        return carry

    lax.fori_loop(0, 2, several, 0)


def kernel(
    init5, init, forc, table_in, vclass_in, bank_in, kind_in,
    smoothed, coarse, table, vclass, bank, kind,
    f0, f1, forcing, part, part2, e0, e1, lp, rp, lp2, rp2, lres, rres, ares, lcor, rcor, vk_out, vk_in,
    faces, coef, lhs, mask, weighted_f, parts, edges, recv, recv_e,
    load_sem, send_sem, recv_sem, psend_sem, precv_sem, esend_sem, erecv_sem, token_sem,
):
    sx = lax.axis_index("space")
    tb = lax.axis_index("tm")
    has_left, has_right = sx > 0, sx < 7
    has_before, has_after = tb > 0, tb < 31
    is_edge = jnp.logical_or(jnp.logical_and(tb < 4, has_left), jnp.logical_and(tb >= 28, has_right))
    to_left, to_right, to_after = {"space": sx - 1}, {"space": sx + 1}, {"tm": tb + 1}
    left_after, right_after = {"space": sx - 1, "tm": tb + 1}, {"space": sx + 1, "tm": tb + 1}
    left_before, right_before = {"space": sx - 1, "tm": tb - 1}, {"space": sx + 1, "tm": tb - 1}
    both = jnp.logical_and

    barrier = pltpu.get_barrier_semaphore()

    def greet(condition, device):
        @pl.when(condition)
        def _():
            pl.semaphore_signal(barrier, inc=1, device_id=device, device_id_type=MESH)

    column, row = lax.rem(tb, 16), tb // 16
    ring = [{"tm": row * 16 + lax.rem(column + step, 16)} for step in (2, 14)]
    across = {"tm": lax.rem(tb + 16, 32)}
    partner = {"tm": tb + 1 - 2 * lax.rem(tb, 2)}
    greet(has_left, to_left)
    greet(has_right, to_right)
    greet(has_before, {"tm": tb - 1})
    greet(has_after, to_after)
    greet(both(has_left, has_before), left_before)
    greet(both(has_right, has_before), right_before)
    for device in ring + [across]:
        greet(True, device)

    def tell(n, devices):
        for condition, device in devices:

            @pl.when(condition)
            def _(device=device):
                pl.semaphore_signal(token_sem.at[n], inc=1, device_id=device, device_id_type=MESH)

    circles = [[(True, device) for device in ring]] * 3
    circles += [[(True, across)], [(True, partner)], [(has_left, to_left), (has_right, to_right)]]
    counts = [2, 2, 2, 1, 1, has_left.astype(jnp.int32) + has_right.astype(jnp.int32)]

    def pass_on(n):
        if n > 0:
            pl.semaphore_wait(token_sem.at[n - 1], counts[n - 1])
        if n < 6:
            tell(n, circles[n])

    loads = [
        pltpu.make_async_copy(table_in, table, load_sem.at[0]),
        pltpu.make_async_copy(vclass_in, vclass, load_sem.at[1]),
        pltpu.make_async_copy(kind_in, kind, load_sem.at[2]),
        pltpu.make_async_copy(init, f0, load_sem.at[3]),
        pltpu.make_async_copy(forc, forcing, load_sem.at[4]),
        pltpu.make_async_copy(bank_in, bank, load_sem.at[5]),
    ]
    for copy in loads:
        copy.start()

    @pl.when(sx == 0)
    def _():
        vk_in[0] = jnp.zeros((16, 128), F32)
        lp[...] = jnp.zeros_like(lp)
        lres[...] = jnp.zeros_like(lres)

    @pl.when(sx == 7)
    def _():
        vk_in[1] = jnp.zeros((16, 128), F32)
        rp[...] = jnp.zeros_like(rp)
        rres[...] = jnp.zeros_like(rres)

    @pl.when(tb == 0)
    def _():
        e0[...] = jnp.zeros_like(e0)
        ares[...] = jnp.zeros_like(ares)

    @pl.when(jnp.logical_or(tb == 0, sx == 0))
    def _():
        lcor[...] = jnp.zeros_like(lcor)

    @pl.when(jnp.logical_or(tb == 0, sx == 7))
    def _():
        rcor[...] = jnp.zeros_like(rcor)

    @pl.when(jnp.logical_not(is_edge))
    def _():
        recv_e[...] = jnp.zeros_like(recv_e)

    loads[0].wait()
    loads[1].wait()
    viscosity = jnp.zeros((4, 8, 128), F32)
    for label in range(8):
        viscosity = jnp.where(vclass[...] == label, table[label], viscosity)
    build_coefficients(viscosity, coef)
    loads[2].wait()
    maps = kind_maps(kind)
    vk_out[0, 0:4] = viscosity[0, 0:4]
    vk_out[1, 0:4] = viscosity[3, 4:8]
    vk_out[0, 4:8] = jnp.zeros((4, 128), F32)
    vk_out[1, 4:8] = jnp.zeros((4, 128), F32)
    vk_out[0, 8:16] = maps[0]
    vk_out[1, 8:16] = maps[3]
    for g in range(4):
        store_mask(maps[g], mask, g + 1)
    loads[3].wait()
    loads[4].wait()

    nothing = [jnp.zeros((4, 128), F32)] * 4

    def local(t, i, j):
        now = [f0[c, t] for c in range(4)]
        base = [forcing[c, t] for c in range(4)]
        for c in range(3):
            base[c] = base[c] + (f0[c, t - 1] if j else jnp.where(i > 0, f0[c, jnp.maximum(t - 1, 0)], 0.0))
        for c, value in enumerate(residual(now, nothing, nothing, base, coef[0], coef)):
            part[c, t] = value

    steps(local)

    one = lambda condition: condition.astype(jnp.int32)
    pl.semaphore_wait(
        barrier,
        3 + one(has_left) + one(has_right) + one(has_before) + one(has_after)
        + one(both(has_left, has_after)) + one(both(has_right, has_after)),
    )

    def remote(condition, awaited, source, target, n, device):
        copy = pltpu.make_async_remote_copy(
            source, target, send_sem.at[n], recv_sem.at[n], device_id=device, device_id_type=MESH
        )
        return condition, awaited, copy

    round_one = [
        remote(has_left, has_right, vk_out.at[0], vk_in.at[1], 0, to_left),
        remote(has_right, has_left, vk_out.at[1], vk_in.at[0], 1, to_right),
        remote(has_left, has_right, init5.at[:, :, 0], rp, 2, to_left),
        remote(has_right, has_left, init5.at[:, :, 7], lp, 3, to_right),
        remote(has_after, has_before, init.at[0:3, 7], e0, 4, to_after),
        remote(has_after, has_before, part.at[:, 7], ares, 5, to_after),
        remote(both(has_left, has_after), both(has_right, has_before), init.at[:, 7, 0], rcor, 6, left_after),
        remote(both(has_right, has_after), both(has_left, has_before), init.at[:, 7, 3], lcor, 7, right_after),
        remote(has_left, has_right, part.at[:, 0:4, 0], rres.at[:, 0:4], 8, to_left),
        remote(has_right, has_left, part.at[:, 0:4, 3], lres.at[:, 0:4], 9, to_right),
        remote(has_left, has_right, part.at[:, 4:8, 0], rres.at[:, 4:8], 10, to_left),
        remote(has_right, has_left, part.at[:, 4:8, 3], lres.at[:, 4:8], 11, to_right),
    ]
    for condition, _, copy in round_one:
        pl.when(condition)(copy.start)
    pass_on(0)

    def arrive(first, last):
        for _, awaited, copy in round_one[first:last]:
            pl.when(awaited)(copy.wait_recv)

    loads[5].wait()
    build_bank(bank, lhs)
    first = (lax.rem(tb, 4) * 8).astype(F32) * (1.0 / 1024.0)

    def weigh(plain, ramp):
        far = first * plain + ramp * (1.0 / 1024.0)
        return plain * (1.0 / 32.0) - far, far

    for c in range(4):
        near, far = weigh(*time_sums(lambda t, c=c: forcing[c, t]))
        weighted_f[0, c] = near
        weighted_f[1, c] = far

    pass_on(1)

    for pair in ((1, 2), (3, 4), (5, 6), (7,)):
        where = [(t, g) for t in pair for g in (1, 2)]
        units = [[part[c, t, g] for c in range(4)] for t, g in where]
        for (t, g), change in zip(where, corrections(units, [g + 1 for _, g in where], lhs, mask)):
            for c in range(4):
                f1[c, t, g] = f0[c, t, g] + change[c]

    pass_on(2)
    arrive(0, 2)
    faces[0] = 0.5 * (viscosity[0, 0:4] + vk_in[0, 0:4])
    faces[1] = 0.5 * (viscosity[3, 4:8] + vk_in[1, 0:4])
    store_mask(vk_in[0, 8:16], mask, 0)
    store_mask(vk_in[1, 8:16], mask, 5)
    arrive(2, 5)
    pass_on(3)

    units = [[part[c, 0, g] + (e0[c, g] if c < 3 else 0.0) for c in range(4)] for g in (1, 2)]
    for g, change in zip((1, 2), corrections(units, [2, 3], lhs, mask)):
        for c in range(4):
            f1[c, 0, g] = f0[c, 0, g] + change[c]

    def plane(ref, t, side):
        if side == 0:
            return [ref[c, t, 0, 0:4] for c in range(4)]
        return [ref[c, t, 3, 4:8] for c in range(4)]

    def outer(t, i, j):
        units = []
        for side, g, near, sign, place in ((0, 0, lp, -1.0, low), (1, 3, rp, 1.0, high)):
            extra = face([near[c, t] for c in range(4)], plane(f0, t, side), faces[side], sign)
            unit = [part[c, t, g] + place(extra[c]) for c in range(4)]
            if j == 0:
                unit = [unit[c] + jnp.where(i == 0, e0[c, g], 0.0) for c in range(3)] + unit[3:]
            units.append(unit)
        for g, change in zip((0, 3), corrections(units, [1, 4], lhs, mask)):
            for c in range(4):
                f1[c, t, g] = f0[c, t, g] + change[c]

    steps(outer)

    pass_on(4)

    arrive(5, 8)
    units = [[ares[c, g] for c in range(4)] for g in range(4)]
    old = [e0[c, 0, 0:4] for c in range(3)]
    extra = face([lcor[c, 4:8] for c in range(4)], old, faces[0], -1.0)
    units[0] = [units[0][c] + low(extra[c]) for c in range(4)]
    old = [e0[c, 3, 4:8] for c in range(3)]
    extra = face([rcor[c, 0:4] for c in range(4)], old, faces[1], 1.0)
    units[3] = [units[3][c] + high(extra[c]) for c in range(4)]
    for g, change in enumerate(corrections(units, [1, 2, 3, 4], lhs, mask)):
        for c in range(3):
            e1[c, g] = e0[c, g] + change[c]

    def middle(t, i, j):
        now = [f1[c, t] for c in range(4)]
        base = [forcing[c, t] for c in range(4)]
        for c in range(3):
            if j:
                base[c] = base[c] + f1[c, t - 1]
            else:
                base[c] = base[c] + jnp.where(i > 0, f1[c, jnp.maximum(t - 1, 0)], e1[c])
        resid = residual(now, nothing, nothing, base, coef[0], coef)
        for c in range(4):
            part2[c, t] = resid[c]
        units = [[resid[c][g] for c in range(4)] for g in (1, 2)]
        for g, change in zip((1, 2), corrections(units, [2, 3], lhs, mask)):
            for c in range(4):
                smoothed[c, t, g] = now[c][g] + change[c]

    steps(middle)

    pass_on(5)

    arrive(8, 12)
    for c in range(3):
        lres[c, 0] = lres[c, 0] + lcor[c]
        rres[c, 0] = rres[c, 0] + rcor[c]

    def beside(t, i, j):
        lold = [lp[c, t] for c in range(4)]
        rold = [rp[c, t] for c in range(4)]
        extra = face(plane(f0, t, 0), lold, faces[0], 1.0)
        lunit = [lres[c, t] + high(extra[c]) for c in range(4)]
        extra = face(plane(f0, t, 1), rold, faces[1], -1.0)
        runit = [rres[c, t] + low(extra[c]) for c in range(4)]
        lchange, rchange = corrections([lunit, runit], [0, 5], lhs, mask)
        for c in range(4):
            lp2[c, t] = jnp.where(has_left, lold[c] + lchange[c][4:8], 0.0)
            rp2[c, t] = jnp.where(has_right, rold[c] + rchange[c][0:4], 0.0)

    steps(beside)

    def ends(t, i, j):
        units = []
        for side, g, near, sign, place in ((0, 0, lp2, -1.0, low), (1, 3, rp2, 1.0, high)):
            extra = face([near[c, t] for c in range(4)], plane(f1, t, side), faces[side], sign)
            units.append([part2[c, t, g] + place(extra[c]) for c in range(4)])
        for g, change in zip((0, 3), corrections(units, [1, 4], lhs, mask)):
            for c in range(4):
                smoothed[c, t, g] = f1[c, t, g] + change[c]

    steps(ends)

    fields = ([], [])
    mass = []
    for c in range(4):
        plain, ramp = time_sums(lambda t, c=c: smoothed[c, t])
        near, far = weigh(plain, ramp)
        fields[0].append(near)
        fields[1].append(far)
        mass.append(plain * (1.0 / 1024.0))
    for half in range(2):
        now = fields[half]
        for side, g, sign in ((0, 0, 1.0), (1, 3, -1.0)):
            rows = slice(4 * side, 4 * side + 4)
            for c, value in enumerate(face([v[g, rows] for v in now], None, faces[side], sign)):
                edges[side, pl.ds(4 * half + c, 4, stride=8), :] = value
    for half in range(2):
        now = fields[half]
        base = [weighted_f[half, c] for c in range(4)]
        for c in range(3):
            base[c] = base[c] - mass[c] if half == 0 else base[c] + mass[c]
        resid = residual(now, nothing, nothing, base, coef[7], coef)
        for c in range(4):
            row = 4 * half + c
            for g in range(4):
                value = resid[c][g]
                if c < 3 and g == 0:
                    value = value - low(faces[0] * now[c][0, 0:4])
                if c < 3 and g == 3:
                    value = value - high(faces[1] * now[c][3, 4:8])
                parts[pl.ds(64 * g + row, 8, stride=8), :] = value

    def tile(ref, row):
        return ref.at[pl.ds(pl.multiple_of(row * 8, 8), 8)]

    def edge_piece(side, y, device):
        return pltpu.make_async_remote_copy(
            edges.at[side, pl.ds(8 * y, 8)], recv_e.at[tb], esend_sem.at[side], erecv_sem,
            device_id=device, device_id_type=MESH,
        )

    pass_on(6)

    @pl.when(has_left)
    def _():
        for y in range(4):
            edge_piece(0, y, {"space": sx - 1, "tm": 28 + y}).start()

    @pl.when(has_right)
    def _():
        for y in range(4):
            edge_piece(1, y, {"space": sx + 1, "tm": y}).start()

    def send(step, carry):
        k = step // 4
        odd = lax.rem(k, 2)
        dz = 4 + (k // 2) * (1 - odd) - ((k + 1) // 2) * odd
        column = lax.rem(lax.rem(tb, 16) + 2 * dz, 16)
        column = column // 2 * 2 + lax.rem(tb + step, 2)
        peer = lax.rem(tb // 16 + 1 + lax.rem(step // 2, 2), 2) * 16 + column

        @pl.when(peer != tb)
        def _():
            pltpu.make_async_remote_copy(
                tile(parts, peer), recv.at[tb], psend_sem, precv_sem,
                device_id={"tm": peer}, device_id_type=MESH,
            ).start()

        return carry

    lax.fori_loop(0, 32, send, 0)
    recv[tb] = tile(parts, tb)[...]

    for condition, _, copy in round_one:
        pl.when(condition)(copy.wait_send)

    def sent_edges(side, device):
        pltpu.make_async_remote_copy(
            edges.at[side], edges.at[side], esend_sem.at[side], erecv_sem,
            device_id=device, device_id_type=MESH,
        ).wait_send()

    pl.when(has_left)(lambda: sent_edges(0, to_left))
    pl.when(has_right)(lambda: sent_edges(1, to_right))
    pieces = pltpu.make_async_remote_copy(
        recv.at[0:31], recv.at[0:31], psend_sem, precv_sem, device_id=to_after, device_id_type=MESH
    )
    pieces.wait_send()
    pieces.wait_recv()

    @pl.when(is_edge)
    def _():
        pltpu.make_async_remote_copy(
            recv_e, recv_e, psend_sem, erecv_sem, device_id=to_after, device_id_type=MESH
        ).wait_recv()

    before = jnp.zeros((4, 128), F32)
    for k in range(8):
        block = (recv[4 * k] + recv[4 * k + 1]) + (recv[4 * k + 2] + recv[4 * k + 3])
        block = block + (
            (recv_e[4 * k] + recv_e[4 * k + 1]) + (recv_e[4 * k + 2] + recv_e[4 * k + 3])
        )
        level = block[0:4] + before
        before = block[4:8]
        for c in range(4):
            coarse[c, k : k + 1, :] = level[c : c + 1]


def per_device(initial_guess, forcing, visc_table, visc_class, inverse_bank, patch_kind):
    hbm = pl.BlockSpec(memory_space=pltpu.HBM)
    vmem = pl.BlockSpec(memory_space=pltpu.VMEM)
    dma = pltpu.SemaphoreType.DMA
    smoothed, coarse = pl.pallas_call(
        kernel,
        out_shape=(
            pltpu.VMEM((4, 8, 4, 8, 128), F32),
            pltpu.VMEM((4, 8, 128), F32),
        ),
        in_specs=[hbm] * 7,
        out_specs=(vmem, vmem),
        scratch_shapes=[
            pltpu.SMEM((8,), F32),
            pltpu.VMEM((4, 8, 128), jnp.int32),
            pltpu.VMEM((4, 32, 32), BF16),
            pltpu.VMEM((4, 2, 64), jnp.int32),
            pltpu.VMEM((4, 8, 4, 8, 128), F32),
            pltpu.VMEM((4, 8, 4, 8, 128), F32),
            pltpu.VMEM((4, 8, 4, 8, 128), F32),
            pltpu.VMEM((4, 8, 4, 8, 128), F32),
            pltpu.VMEM((4, 8, 4, 8, 128), F32),
            pltpu.VMEM((3, 4, 8, 128), F32),
            pltpu.VMEM((3, 4, 8, 128), F32),
            pltpu.VMEM((4, 8, 4, 128), F32),
            pltpu.VMEM((4, 8, 4, 128), F32),
            pltpu.VMEM((4, 8, 4, 128), F32),
            pltpu.VMEM((4, 8, 4, 128), F32),
            pltpu.VMEM((4, 8, 8, 128), F32),
            pltpu.VMEM((4, 8, 8, 128), F32),
            pltpu.VMEM((4, 4, 8, 128), F32),
            pltpu.VMEM((4, 8, 128), F32),
            pltpu.VMEM((4, 8, 128), F32),
            pltpu.VMEM((2, 16, 128), F32),
            pltpu.VMEM((2, 16, 128), F32),
            pltpu.VMEM((2, 4, 128), F32),
            pltpu.VMEM((8, 4, 8, 128), F32),
            pltpu.VMEM((64, 256), BF16),
            pltpu.VMEM((6, 4, 16, 128), BF16),
            pltpu.VMEM((2, 4, 4, 8, 128), F32),
            pltpu.VMEM((256, 128), F32),
            pltpu.VMEM((2, 32, 128), F32),
            pltpu.VMEM((32, 8, 128), F32),
            pltpu.VMEM((32, 8, 128), F32),
            dma((6,)),
            dma((12,)),
            dma((12,)),
            dma,
            dma,
            dma((2,)),
            dma,
            pltpu.SemaphoreType.REGULAR((6,)),
        ],
        compiler_params=pltpu.CompilerParams(
            collective_id=0, has_side_effects=True, vmem_limit_bytes=60 * 1024 * 1024
        ),
    )(
        initial_guess,
        initial_guess.reshape(4, 8, 4, 8, 128),
        forcing.reshape(4, 8, 4, 8, 128),
        visc_table,
        visc_class.reshape(4, 8, 128),
        inverse_bank,
        patch_kind,
    )
    return smoothed.reshape(4, 8, 8, 4, 128), coarse


def solution(mesh):
    return jax.shard_map(
        per_device,
        mesh=mesh,
        in_specs=(
            P(None, "tm", "space", None, None),
            P(None, "tm", "space", None, None),
            P(),
            P("space", None, None),
            P(),
            P("space", None, None),
        ),
        out_specs=(P(None, "tm", "space", None, None), P(None, None, ("space", "tm"))),
        check_vma=False,
    )
```

```python
import functools

import jax
import jax.numpy as jnp
from jax import lax
from jax.experimental import pallas as pl
from jax.experimental.pallas import tpu as pltpu
from jax.sharding import PartitionSpec as P

MESH = pl.DeviceIdType.MESH
F32 = jnp.float32
BF16 = jnp.bfloat16
DAMPING = 0.8
STABILIZE = 0.1


def iota(shape, dim):
    return lax.broadcasted_iota(jnp.int32, shape, dim)


def cell_index(q):
    return (q // 8) * 8 + (q // 4 % 2) * 4 + (q % 2) * 2


def build_bank(bank_ref, lhs_ref):
    j = iota((32, 64), 0)
    q = iota((32, 64), 1)
    spread = (j == cell_index(q % 32) + q // 32).astype(BF16)
    p = iota((64, 32), 0)
    i = iota((64, 32), 1)
    gather = (i == cell_index(p % 32) + p // 32).astype(BF16)
    same = (iota((64, 64), 0) // 2 % 2) == (iota((64, 64), 1) // 2 % 2)
    wide = jnp.dot(bank_ref[...].reshape(128, 32), spread, preferred_element_type=F32).astype(BF16)
    parts = []
    for kind in range(4):
        part = jnp.dot(gather, wide[32 * kind : 32 * kind + 32], preferred_element_type=F32)
        parts.append(jnp.where(same, part, 0.0).astype(BF16))
    lhs_ref[...] = jnp.concatenate(parts, axis=1)


def kind_maps(kind_ref):
    upper = iota((8, 64), 0) // 2 % 2 == 0
    double = (iota((64, 128), 0) == iota((64, 128), 1) // 2).astype(BF16)
    maps = []
    for g in range(4):
        pair = kind_ref[g].astype(F32)
        rows = jnp.where(upper, pair[0:1], pair[1:2]).astype(BF16)
        maps.append(jnp.dot(rows, double, preferred_element_type=F32))
    return maps


def store_mask(kinds, mask_ref, at):
    for kind in range(4):
        mask = (kinds == float(kind)).astype(F32)
        mask_ref[at, kind] = jnp.concatenate([mask, mask], axis=0).astype(BF16)


def shift_x(values, left, right):
    first = jnp.concatenate([left, values[0, 0:4]], axis=0)
    last = jnp.concatenate([values[3, 4:8], right], axis=0)
    low = iota((3, 8, 128), 1) < 4
    inner = pltpu.roll(jnp.where(low, values[1:4], values[0:3]), 4, 1)
    return (
        jnp.concatenate([first[None], inner], axis=0),
        jnp.concatenate([inner, last[None]], axis=0),
    )


def shifts_yz(values):
    return (
        pltpu.roll(values, 1, 1),
        pltpu.roll(values, 7, 1),
        pltpu.roll(values, 1, 2),
        pltpu.roll(values, 127, 2),
    )


def edge_masks():
    y = iota((4, 8, 128), 1) % 4
    z = iota((4, 8, 128), 2)
    return y != 0, y != 3, z != 0, z != 127


def build_coefficients(viscosity, coef_ref):
    none = jnp.zeros((4, 128), F32)
    xm, xp = shift_x(viscosity, none, none)
    ym, yp, zm, zp = shifts_yz(viscosity)
    g, row = iota((4, 8, 128), 0), iota((4, 8, 128), 1)
    has_xm = jnp.logical_or(g > 0, row >= 4)
    has_xp = jnp.logical_or(g < 3, row < 4)
    total = jnp.zeros_like(viscosity)
    for n, (near, mask) in enumerate(zip((xm, xp, ym, yp, zm, zp), (has_xm, has_xp) + edge_masks())):
        near = jnp.where(mask, near, 0.0)
        kappa = 0.5 * (viscosity + near)
        inner = jnp.where(mask, kappa, 0.0)
        total = total + (inner if n < 2 else kappa)
        coef_ref[1 + n] = inner
    coef_ref[0] = total + 1.0
    coef_ref[7] = total


def residual(now, left, right, base, diagonal, coef_ref):
    mym, myp, mzm, mzp = edge_masks()
    pressure = now[3]
    pxm, pxp = shift_x(pressure, left[3], right[3])
    pym, pyp, pzm, pzp = shifts_yz(pressure)
    pym = jnp.where(mym, pym, 0.0)
    pyp = jnp.where(myp, pyp, 0.0)
    pzm = jnp.where(mzm, pzm, 0.0)
    pzp = jnp.where(mzp, pzp, 0.0)
    gradients = (pxp - pxm, pyp - pym, pzp - pzm)
    out = []
    divergence = None
    for c in range(3):
        value = now[c]
        xm, xp = shift_x(value, left[c], right[c])
        ym, yp, zm, zp = shifts_yz(value)
        flow = coef_ref[1] * xm + coef_ref[2] * xp
        flow = flow + (coef_ref[3] * ym + coef_ref[4] * yp)
        flow = flow + (coef_ref[5] * zm + coef_ref[6] * zp)
        out.append(base[c] - diagonal * value + flow - 0.5 * gradients[c])
        if c == 0:
            divergence = xp - xm
        elif c == 1:
            divergence = divergence + (jnp.where(myp, yp, 0.0) - jnp.where(mym, ym, 0.0))
        else:
            divergence = divergence + (jnp.where(mzp, zp, 0.0) - jnp.where(mzm, zm, 0.0))
    around = (pxm + pxp) + (pym + pyp) + (pzm + pzp)
    out.append(base[3] - STABILIZE * (6.0 * pressure - around) + 0.5 * divergence)
    return out


def face(near, own, kappa, sign):
    out = []
    for c in range(3):
        out.append(kappa * (near[c] if own is None else near[c] - own[c]))
    out[0] = out[0] - (0.5 * sign) * near[3]
    out.append(STABILIZE * near[3] + (0.5 * sign) * near[0])
    return out


def low(rows):
    return jnp.concatenate([rows, jnp.zeros((4, 128), F32)], axis=0)


def high(rows):
    return jnp.concatenate([jnp.zeros((4, 128), F32), rows], axis=0)


def corrections(units, at, lhs_ref, mask_ref):
    even = iota((8, 128), 1) % 2 == 0
    columns = []
    for unit, place in zip(units, at):
        evens = [jnp.where(even, v, pltpu.roll(v, 1, 1)) for v in unit]
        odds = [jnp.where(even, pltpu.roll(v, 127, 1), v) for v in unit]
        stack = jnp.concatenate(evens + odds, axis=0).astype(BF16).reshape(4, 16, 128)
        masked = [(stack * mask_ref[place, kind]).reshape(64, 128) for kind in range(4)]
        columns.append(jnp.concatenate(masked, axis=0))
    product = jnp.dot(
        lhs_ref[...], jnp.concatenate(columns, axis=1), preferred_element_type=F32
    )
    out = []
    for n in range(len(units)):
        across = slice(128 * n, 128 * n + 128)
        out.append(
            [
                DAMPING
                * jnp.where(even, product[8 * c : 8 * c + 8, across], product[32 + 8 * c : 40 + 8 * c, across])
                for c in range(4)
            ]
        )
    return out


def time_sums(load):
    plain = load(0)
    ramp = None
    for t in range(1, 8):
        value = load(t)
        plain = plain + value
        ramp = value * float(t) if ramp is None else ramp + value * float(t)
    return plain, ramp


def steps(body):
    def several(i, carry):
        for j in range(4):
            body(4 * i + j, i, j)
        return carry

    lax.fori_loop(0, 2, several, 0)


def kernel(
    init5, init, forc, table_in, vclass_in, bank_in, kind_in,
    smoothed, coarse, table, vclass, bank, kind,
    f0, f1, forcing, part, part2, e0, e1, lp, rp, lp2, rp2, lres, rres, ares, lcor, rcor, vk_out, vk_in,
    faces, fields, mass, coef, lhs, mask, weighted_f, parts, edges, recv, recv_e,
    load_sem, send_sem, recv_sem, psend_sem, precv_sem, esend_sem, erecv_sem, token_sem,
):
    sx = lax.axis_index("space")
    tb = lax.axis_index("tm")
    has_left, has_right = sx > 0, sx < 7
    has_before, has_after = tb > 0, tb < 31
    is_edge = jnp.logical_or(jnp.logical_and(tb < 4, has_left), jnp.logical_and(tb >= 28, has_right))
    to_left, to_right, to_after = {"space": sx - 1}, {"space": sx + 1}, {"tm": tb + 1}
    left_after, right_after = {"space": sx - 1, "tm": tb + 1}, {"space": sx + 1, "tm": tb + 1}
    left_before, right_before = {"space": sx - 1, "tm": tb - 1}, {"space": sx + 1, "tm": tb - 1}
    both = jnp.logical_and

    barrier = pltpu.get_barrier_semaphore()

    def greet(condition, device):
        @pl.when(condition)
        def _():
            pl.semaphore_signal(barrier, inc=1, device_id=device, device_id_type=MESH)

    column, row = lax.rem(tb, 16), tb // 16
    ring = [{"tm": row * 16 + lax.rem(column + step, 16)} for step in (2, 14)]
    far_ring = [{"tm": row * 16 + lax.rem(column + step, 16)} for step in (4, 12)]
    across = {"tm": lax.rem(tb + 16, 32)}
    partner = {"tm": tb + 1 - 2 * lax.rem(tb, 2)}
    greet(has_left, to_left)
    greet(has_right, to_right)
    greet(has_before, {"tm": tb - 1})
    greet(has_after, to_after)
    greet(both(has_left, has_before), left_before)
    greet(both(has_right, has_before), right_before)
    for device in ring + [across]:
        greet(True, device)

    def tell(n, devices):
        for condition, device in devices:

            @pl.when(condition)
            def _(device=device):
                pl.semaphore_signal(token_sem.at[n], inc=1, device_id=device, device_id_type=MESH)

    circles = [
        [(True, partner)],
        [(True, device) for device in ring],
        [(True, device) for device in far_ring],
        [(True, across)],
        [(has_left, to_left), (has_right, to_right)],
    ]
    counts = [1, 2, 2, 1, has_left.astype(jnp.int32) + has_right.astype(jnp.int32)]

    def pass_on(n):
        if n > 0:
            pl.semaphore_wait(token_sem.at[n - 1], counts[n - 1])
        if n < 5:
            tell(n, circles[n])

    loads = [
        pltpu.make_async_copy(table_in, table, load_sem.at[0]),
        pltpu.make_async_copy(vclass_in, vclass, load_sem.at[1]),
        pltpu.make_async_copy(kind_in, kind, load_sem.at[2]),
        pltpu.make_async_copy(init, f0, load_sem.at[3]),
        pltpu.make_async_copy(forc, forcing, load_sem.at[4]),
        pltpu.make_async_copy(bank_in, bank, load_sem.at[5]),
    ]
    for copy in loads:
        copy.start()

    @pl.when(sx == 0)
    def _():
        vk_in[0] = jnp.zeros((16, 128), F32)
        lp[...] = jnp.zeros_like(lp)
        lres[...] = jnp.zeros_like(lres)

    @pl.when(sx == 7)
    def _():
        vk_in[1] = jnp.zeros((16, 128), F32)
        rp[...] = jnp.zeros_like(rp)
        rres[...] = jnp.zeros_like(rres)

    @pl.when(tb == 0)
    def _():
        e0[...] = jnp.zeros_like(e0)
        ares[...] = jnp.zeros_like(ares)

    @pl.when(jnp.logical_or(tb == 0, sx == 0))
    def _():
        lcor[...] = jnp.zeros_like(lcor)

    @pl.when(jnp.logical_or(tb == 0, sx == 7))
    def _():
        rcor[...] = jnp.zeros_like(rcor)

    @pl.when(jnp.logical_not(is_edge))
    def _():
        recv_e[...] = jnp.zeros_like(recv_e)

    loads[0].wait()
    loads[1].wait()
    viscosity = jnp.zeros((4, 8, 128), F32)
    for label in range(8):
        viscosity = jnp.where(vclass[...] == label, table[label], viscosity)
    build_coefficients(viscosity, coef)
    loads[2].wait()
    maps = kind_maps(kind)
    vk_out[0, 0:4] = viscosity[0, 0:4]
    vk_out[1, 0:4] = viscosity[3, 4:8]
    vk_out[0, 4:8] = jnp.zeros((4, 128), F32)
    vk_out[1, 4:8] = jnp.zeros((4, 128), F32)
    vk_out[0, 8:16] = maps[0]
    vk_out[1, 8:16] = maps[3]
    for g in range(4):
        store_mask(maps[g], mask, g + 1)
    loads[3].wait()
    loads[4].wait()

    nothing = [jnp.zeros((4, 128), F32)] * 4

    def local(t, i, j):
        now = [f0[c, t] for c in range(4)]
        base = [forcing[c, t] for c in range(4)]
        for c in range(3):
            base[c] = base[c] + (f0[c, t - 1] if j else jnp.where(i > 0, f0[c, jnp.maximum(t - 1, 0)], 0.0))
        for c, value in enumerate(residual(now, nothing, nothing, base, coef[0], coef)):
            part[c, t] = value

    steps(local)

    one = lambda condition: condition.astype(jnp.int32)
    pl.semaphore_wait(
        barrier,
        3 + one(has_left) + one(has_right) + one(has_before) + one(has_after)
        + one(both(has_left, has_after)) + one(both(has_right, has_after)),
    )

    def remote(condition, awaited, source, target, n, device):
        copy = pltpu.make_async_remote_copy(
            source, target, send_sem.at[n], recv_sem.at[n], device_id=device, device_id_type=MESH
        )
        return condition, awaited, copy

    round_one = [
        remote(has_left, has_right, vk_out.at[0], vk_in.at[1], 0, to_left),
        remote(has_right, has_left, vk_out.at[1], vk_in.at[0], 1, to_right),
        remote(has_left, has_right, init5.at[:, :, 0], rp, 2, to_left),
        remote(has_right, has_left, init5.at[:, :, 7], lp, 3, to_right),
        remote(has_after, has_before, init.at[0:3, 7], e0, 4, to_after),
        remote(has_after, has_before, part.at[:, 7], ares, 5, to_after),
        remote(both(has_left, has_after), both(has_right, has_before), init.at[:, 7, 0], rcor, 6, left_after),
        remote(both(has_right, has_after), both(has_left, has_before), init.at[:, 7, 3], lcor, 7, right_after),
    ]
    for i in range(2):
        pair = slice(4 * i, 4 * i + 4)
        round_one += [
            remote(has_left, has_right, part.at[:, pair, 0], rres.at[:, pair], 8 + 2 * i, to_left),
            remote(has_right, has_left, part.at[:, pair, 3], lres.at[:, pair], 9 + 2 * i, to_right),
        ]
    for condition, _, copy in round_one:
        pl.when(condition)(copy.start)
    pass_on(0)

    def arrive(first, last):
        for _, awaited, copy in round_one[first:last]:
            pl.when(awaited)(copy.wait_recv)

    loads[5].wait()
    build_bank(bank, lhs)
    pass_on(1)
    first = (lax.rem(tb, 4) * 8).astype(F32) * (1.0 / 1024.0)

    def weigh(plain, ramp):
        far = first * plain + ramp * (1.0 / 1024.0)
        return plain * (1.0 / 32.0) - far, far

    for c in range(4):
        near, far = weigh(*time_sums(lambda t, c=c: forcing[c, t]))
        weighted_f[0, c] = near
        weighted_f[1, c] = far


    for pair in ((1, 2), (3, 4), (5, 6), (7,)):
        where = [(t, g) for t in pair for g in (1, 2)]
        units = [[part[c, t, g] for c in range(4)] for t, g in where]
        for (t, g), change in zip(where, corrections(units, [g + 1 for _, g in where], lhs, mask)):
            for c in range(4):
                f1[c, t, g] = f0[c, t, g] + change[c]

    pass_on(2)
    arrive(0, 2)
    faces[0] = 0.5 * (viscosity[0, 0:4] + vk_in[0, 0:4])
    faces[1] = 0.5 * (viscosity[3, 4:8] + vk_in[1, 0:4])
    store_mask(vk_in[0, 8:16], mask, 0)
    store_mask(vk_in[1, 8:16], mask, 5)
    arrive(2, 5)
    pass_on(3)

    units = [[part[c, 0, g] + (e0[c, g] if c < 3 else 0.0) for c in range(4)] for g in (1, 2)]
    for g, change in zip((1, 2), corrections(units, [2, 3], lhs, mask)):
        for c in range(4):
            f1[c, 0, g] = f0[c, 0, g] + change[c]

    def plane(ref, t, side):
        if side == 0:
            return [ref[c, t, 0, 0:4] for c in range(4)]
        return [ref[c, t, 3, 4:8] for c in range(4)]

    def outer(t, i, j):
        units = []
        for side, g, near, sign, place in ((0, 0, lp, -1.0, low), (1, 3, rp, 1.0, high)):
            extra = face([near[c, t] for c in range(4)], plane(f0, t, side), faces[side], sign)
            unit = [part[c, t, g] + place(extra[c]) for c in range(4)]
            if j == 0:
                unit = [unit[c] + jnp.where(i == 0, e0[c, g], 0.0) for c in range(3)] + unit[3:]
            units.append(unit)
        for g, change in zip((0, 3), corrections(units, [1, 4], lhs, mask)):
            for c in range(4):
                f1[c, t, g] = f0[c, t, g] + change[c]

    steps(outer)


    pass_on(4)

    arrive(5, 8)
    units = [[ares[c, g] for c in range(4)] for g in range(4)]
    old = [e0[c, 0, 0:4] for c in range(3)]
    extra = face([lcor[c, 4:8] for c in range(4)], old, faces[0], -1.0)
    units[0] = [units[0][c] + low(extra[c]) for c in range(4)]
    old = [e0[c, 3, 4:8] for c in range(3)]
    extra = face([rcor[c, 0:4] for c in range(4)], old, faces[1], 1.0)
    units[3] = [units[3][c] + high(extra[c]) for c in range(4)]
    for g, change in enumerate(corrections(units, [1, 2, 3, 4], lhs, mask)):
        for c in range(3):
            e1[c, g] = e0[c, g] + change[c]

    def middle(t, i, j):
        now = [f1[c, t] for c in range(4)]
        base = [forcing[c, t] for c in range(4)]
        for c in range(3):
            if j:
                base[c] = base[c] + f1[c, t - 1]
            else:
                base[c] = base[c] + jnp.where(i > 0, f1[c, jnp.maximum(t - 1, 0)], e1[c])
        resid = residual(now, nothing, nothing, base, coef[0], coef)
        for c in range(4):
            part2[c, t] = resid[c]
        units = [[resid[c][g] for c in range(4)] for g in (1, 2)]
        for g, change in zip((1, 2), corrections(units, [2, 3], lhs, mask)):
            for c in range(4):
                smoothed[c, t, g] = now[c][g] + change[c]

    steps(middle)


    def sum_up(rows):
        for c in range(4):
            plain, ramp = time_sums(lambda t: smoothed[c, t, rows])
            near, far = weigh(plain, ramp)
            fields[0, c, rows] = near
            fields[1, c, rows] = far
            mass[c, rows] = plain * (1.0 / 1024.0)

    sum_up(slice(1, 3))

    def beside(pair):
        units = []
        for t in pair:
            extra = face(plane(f0, t, 0), [lp[c, t] for c in range(4)], faces[0], 1.0)
            unit = [lres[c, t] + high(extra[c]) for c in range(4)]
            if t == 0:
                unit = [unit[c] + lcor[c] for c in range(3)] + unit[3:]
            units.append(unit)
            extra = face(plane(f0, t, 1), [rp[c, t] for c in range(4)], faces[1], -1.0)
            unit = [rres[c, t] + low(extra[c]) for c in range(4)]
            if t == 0:
                unit = [unit[c] + rcor[c] for c in range(3)] + unit[3:]
            units.append(unit)
        changes = corrections(units, [0, 5] * 8, lhs, mask)
        for n, t in enumerate(pair):
            for c in range(4):
                lp2[c, t] = jnp.where(has_left, lp[c, t] + changes[2 * n][c][4:8], 0.0)
                rp2[c, t] = jnp.where(has_right, rp[c, t] + changes[2 * n + 1][c][0:4], 0.0)

    def ends(pair):
        units = []
        for t in pair:
            for side, g, near, sign, place in ((0, 0, lp2, -1.0, low), (1, 3, rp2, 1.0, high)):
                extra = face([near[c, t] for c in range(4)], plane(f1, t, side), faces[side], sign)
                units.append([part2[c, t, g] + place(extra[c]) for c in range(4)])
        changes = corrections(units, [1, 4] * 8, lhs, mask)
        for n, t in enumerate(pair):
            for side, g in ((0, 0), (1, 3)):
                for c in range(4):
                    smoothed[c, t, g] = f1[c, t, g] + changes[2 * n + side][c]

    arrive(8, 12)
    beside(range(8))
    ends(range(8))

    for g in (0, 3):
        sum_up(slice(g, g + 1))
    for half in range(2):
        for side, rows, sign in ((0, slice(0, 4), 1.0), (1, slice(4, 8), -1.0)):
            near = [fields[half, c, 3 * side, rows] for c in range(4)]
            for c, value in enumerate(face(near, None, faces[side], sign)):
                edges[side, pl.ds(4 * half + c, 4, stride=8), :] = value

    def edge_piece(side, y, device):
        return pltpu.make_async_remote_copy(
            edges.at[side, pl.ds(8 * y, 8)], recv_e.at[tb], esend_sem.at[side], erecv_sem,
            device_id=device, device_id_type=MESH,
        )

    pass_on(5)

    @pl.when(has_left)
    def _():
        for y in range(4):
            edge_piece(0, y, {"space": sx - 1, "tm": 28 + y}).start()

    @pl.when(has_right)
    def _():
        for y in range(4):
            edge_piece(1, y, {"space": sx + 1, "tm": y}).start()

    for half in range(2):
        now = [fields[half, c] for c in range(4)]
        base = [weighted_f[half, c] for c in range(4)]
        for c in range(3):
            base[c] = base[c] - mass[c] if half == 0 else base[c] + mass[c]
        resid = residual(now, nothing, nothing, base, coef[7], coef)
        for c in range(4):
            row = 4 * half + c
            for g in range(4):
                value = resid[c][g]
                if c < 3 and g == 0:
                    value = value - low(faces[0] * now[c][0, 0:4])
                if c < 3 and g == 3:
                    value = value - high(faces[1] * now[c][3, 4:8])
                parts[pl.ds(64 * g + row, 8, stride=8), :] = value

    def tile(ref, row):
        return ref.at[pl.ds(pl.multiple_of(row * 8, 8), 8)]

    def send(step, carry):
        k = step // 4
        odd = lax.rem(k, 2)
        dz = 4 + (k // 2) * (1 - odd) - ((k + 1) // 2) * odd
        column = lax.rem(lax.rem(tb, 16) + 2 * dz, 16)
        column = column // 2 * 2 + lax.rem(tb + step, 2)
        peer = lax.rem(tb // 16 + 1 + lax.rem(step // 2, 2), 2) * 16 + column

        @pl.when(peer != tb)
        def _():
            pltpu.make_async_remote_copy(
                tile(parts, peer), recv.at[tb], psend_sem, precv_sem,
                device_id={"tm": peer}, device_id_type=MESH,
            ).start()

        return carry

    lax.fori_loop(0, 32, send, 0)
    recv[tb] = tile(parts, tb)[...]

    for condition, _, copy in round_one:
        pl.when(condition)(copy.wait_send)

    def sent_edges(side, device):
        pltpu.make_async_remote_copy(
            edges.at[side], edges.at[side], esend_sem.at[side], erecv_sem,
            device_id=device, device_id_type=MESH,
        ).wait_send()

    pl.when(has_left)(lambda: sent_edges(0, to_left))
    pl.when(has_right)(lambda: sent_edges(1, to_right))
    pieces = pltpu.make_async_remote_copy(
        recv.at[0:31], recv.at[0:31], psend_sem, precv_sem, device_id=to_after, device_id_type=MESH
    )
    pieces.wait_send()
    pieces.wait_recv()

    @pl.when(is_edge)
    def _():
        pltpu.make_async_remote_copy(
            recv_e, recv_e, psend_sem, erecv_sem, device_id=to_after, device_id_type=MESH
        ).wait_recv()

    before = jnp.zeros((4, 128), F32)
    for k in range(8):
        block = (recv[4 * k] + recv[4 * k + 1]) + (recv[4 * k + 2] + recv[4 * k + 3])
        block = block + (
            (recv_e[4 * k] + recv_e[4 * k + 1]) + (recv_e[4 * k + 2] + recv_e[4 * k + 3])
        )
        level = block[0:4] + before
        before = block[4:8]
        for c in range(4):
            coarse[c, k : k + 1, :] = level[c : c + 1]


def store(smoothed_in, coarse_in, smoothed, coarse, sems):
    copies = [
        pltpu.make_async_copy(smoothed_in, smoothed, sems.at[0]),
        pltpu.make_async_copy(coarse_in, coarse, sems.at[1]),
    ]
    for copy in copies:
        copy.start()
    for copy in copies:
        copy.wait()


def per_device(initial_guess, forcing, visc_table, visc_class, inverse_bank, patch_kind):
    hbm = pl.BlockSpec(memory_space=pltpu.HBM)
    vmem = pl.BlockSpec(memory_space=pltpu.VMEM)
    dma = pltpu.SemaphoreType.DMA
    smoothed, coarse = pl.pallas_call(
        kernel,
        out_shape=(
            pltpu.VMEM((4, 8, 4, 8, 128), F32),
            pltpu.VMEM((4, 8, 128), F32),
        ),
        in_specs=[hbm] * 7,
        out_specs=(vmem, vmem),
        scratch_shapes=[
            pltpu.SMEM((8,), F32),
            pltpu.VMEM((4, 8, 128), jnp.int32),
            pltpu.VMEM((4, 32, 32), BF16),
            pltpu.VMEM((4, 2, 64), jnp.int32),
            pltpu.VMEM((4, 8, 4, 8, 128), F32),
            pltpu.VMEM((4, 8, 4, 8, 128), F32),
            pltpu.VMEM((4, 8, 4, 8, 128), F32),
            pltpu.VMEM((4, 8, 4, 8, 128), F32),
            pltpu.VMEM((4, 8, 4, 8, 128), F32),
            pltpu.VMEM((3, 4, 8, 128), F32),
            pltpu.VMEM((3, 4, 8, 128), F32),
            pltpu.VMEM((4, 8, 4, 128), F32),
            pltpu.VMEM((4, 8, 4, 128), F32),
            pltpu.VMEM((4, 8, 4, 128), F32),
            pltpu.VMEM((4, 8, 4, 128), F32),
            pltpu.VMEM((4, 8, 8, 128), F32),
            pltpu.VMEM((4, 8, 8, 128), F32),
            pltpu.VMEM((4, 4, 8, 128), F32),
            pltpu.VMEM((4, 8, 128), F32),
            pltpu.VMEM((4, 8, 128), F32),
            pltpu.VMEM((2, 16, 128), F32),
            pltpu.VMEM((2, 16, 128), F32),
            pltpu.VMEM((2, 4, 128), F32),
            pltpu.VMEM((2, 4, 4, 8, 128), F32),
            pltpu.VMEM((4, 4, 8, 128), F32),
            pltpu.VMEM((8, 4, 8, 128), F32),
            pltpu.VMEM((64, 256), BF16),
            pltpu.VMEM((6, 4, 16, 128), BF16),
            pltpu.VMEM((2, 4, 4, 8, 128), F32),
            pltpu.VMEM((256, 128), F32),
            pltpu.VMEM((2, 32, 128), F32),
            pltpu.VMEM((32, 8, 128), F32),
            pltpu.VMEM((32, 8, 128), F32),
            dma((6,)),
            dma((12,)),
            dma((12,)),
            dma,
            dma,
            dma((2,)),
            dma,
            pltpu.SemaphoreType.REGULAR((5,)),
        ],
        compiler_params=pltpu.CompilerParams(
            collective_id=0, has_side_effects=True, vmem_limit_bytes=60 * 1024 * 1024
        ),
    )(
        initial_guess,
        initial_guess.reshape(4, 8, 4, 8, 128),
        forcing.reshape(4, 8, 4, 8, 128),
        visc_table,
        visc_class.reshape(4, 8, 128),
        inverse_bank,
        patch_kind,
    )
    smoothed, coarse = pl.pallas_call(
        store,
        out_shape=(
            jax.ShapeDtypeStruct((4, 8, 4, 8, 128), F32),
            jax.ShapeDtypeStruct((4, 8, 128), F32),
        ),
        in_specs=[pl.BlockSpec(memory_space=pl.ANY)] * 2,
        out_specs=(pl.BlockSpec(memory_space=pl.ANY),) * 2,
        scratch_shapes=[dma((2,))],
        compiler_params=pltpu.CompilerParams(vmem_limit_bytes=4 * 1024 * 1024),
    )(smoothed, coarse)
    return smoothed.reshape(4, 8, 8, 4, 128), coarse


def solution(mesh):
    return jax.shard_map(
        per_device,
        mesh=mesh,
        in_specs=(
            P(None, "tm", "space", None, None),
            P(None, "tm", "space", None, None),
            P(),
            P("space", None, None),
            P(),
            P("space", None, None),
        ),
        out_specs=(P(None, "tm", "space", None, None), P(None, None, ("space", "tm"))),
        check_vma=False,
    )
```

```python
import functools

import jax
import jax.numpy as jnp
from jax import lax
from jax.experimental import pallas as pl
from jax.experimental.pallas import tpu as pltpu
from jax.sharding import PartitionSpec as P

MESH = pl.DeviceIdType.MESH
F32 = jnp.float32
BF16 = jnp.bfloat16
DAMPING = 0.8
STABILIZE = 0.1


def iota(shape, dim):
    return lax.broadcasted_iota(jnp.int32, shape, dim)


def cell_index(q):
    return (q // 8) * 8 + (q // 4 % 2) * 4 + (q % 2) * 2


def build_bank(bank_ref, lhs_ref):
    j = iota((32, 64), 0)
    q = iota((32, 64), 1)
    spread = (j == cell_index(q % 32) + q // 32).astype(BF16)
    p = iota((64, 32), 0)
    i = iota((64, 32), 1)
    gather = (i == cell_index(p % 32) + p // 32).astype(BF16)
    same = (iota((64, 64), 0) // 2 % 2) == (iota((64, 64), 1) // 2 % 2)
    wide = jnp.dot(bank_ref[...].reshape(128, 32), spread, preferred_element_type=F32).astype(BF16)
    parts = []
    for kind in range(4):
        part = jnp.dot(gather, wide[32 * kind : 32 * kind + 32], preferred_element_type=F32)
        parts.append(jnp.where(same, part, 0.0).astype(BF16))
    lhs_ref[...] = jnp.concatenate(parts, axis=1)


def kind_maps(kind_ref):
    upper = iota((8, 64), 0) // 2 % 2 == 0
    double = (iota((64, 128), 0) == iota((64, 128), 1) // 2).astype(BF16)
    maps = []
    for g in range(4):
        pair = kind_ref[g].astype(F32)
        rows = jnp.where(upper, pair[0:1], pair[1:2]).astype(BF16)
        maps.append(jnp.dot(rows, double, preferred_element_type=F32))
    return maps


def store_mask(kinds, mask_ref, at):
    for kind in range(4):
        mask = (kinds == float(kind)).astype(F32)
        mask_ref[at, kind] = jnp.concatenate([mask, mask], axis=0).astype(BF16)


def shift_x(values, left, right):
    first = jnp.concatenate([left, values[0, 0:4]], axis=0)
    last = jnp.concatenate([values[3, 4:8], right], axis=0)
    low = iota((3, 8, 128), 1) < 4
    inner = pltpu.roll(jnp.where(low, values[1:4], values[0:3]), 4, 1)
    return (
        jnp.concatenate([first[None], inner], axis=0),
        jnp.concatenate([inner, last[None]], axis=0),
    )


def shifts_yz(values):
    return (
        pltpu.roll(values, 1, 1),
        pltpu.roll(values, 7, 1),
        pltpu.roll(values, 1, 2),
        pltpu.roll(values, 127, 2),
    )


def edge_masks():
    y = iota((4, 8, 128), 1) % 4
    z = iota((4, 8, 128), 2)
    return y != 0, y != 3, z != 0, z != 127


def build_coefficients(viscosity, coef_ref):
    none = jnp.zeros((4, 128), F32)
    xm, xp = shift_x(viscosity, none, none)
    ym, yp, zm, zp = shifts_yz(viscosity)
    g, row = iota((4, 8, 128), 0), iota((4, 8, 128), 1)
    has_xm = jnp.logical_or(g > 0, row >= 4)
    has_xp = jnp.logical_or(g < 3, row < 4)
    total = jnp.zeros_like(viscosity)
    for n, (near, mask) in enumerate(zip((xm, xp, ym, yp, zm, zp), (has_xm, has_xp) + edge_masks())):
        near = jnp.where(mask, near, 0.0)
        kappa = 0.5 * (viscosity + near)
        inner = jnp.where(mask, kappa, 0.0)
        total = total + (inner if n < 2 else kappa)
        coef_ref[1 + n] = inner
    coef_ref[0] = total + 1.0
    coef_ref[7] = total


def residual(now, left, right, base, diagonal, coef_ref):
    mym, myp, mzm, mzp = edge_masks()
    pressure = now[3]
    pxm, pxp = shift_x(pressure, left[3], right[3])
    pym, pyp, pzm, pzp = shifts_yz(pressure)
    pym = jnp.where(mym, pym, 0.0)
    pyp = jnp.where(myp, pyp, 0.0)
    pzm = jnp.where(mzm, pzm, 0.0)
    pzp = jnp.where(mzp, pzp, 0.0)
    gradients = (pxp - pxm, pyp - pym, pzp - pzm)
    out = []
    divergence = None
    for c in range(3):
        value = now[c]
        xm, xp = shift_x(value, left[c], right[c])
        ym, yp, zm, zp = shifts_yz(value)
        flow = coef_ref[1] * xm + coef_ref[2] * xp
        flow = flow + (coef_ref[3] * ym + coef_ref[4] * yp)
        flow = flow + (coef_ref[5] * zm + coef_ref[6] * zp)
        out.append(base[c] - diagonal * value + flow - 0.5 * gradients[c])
        if c == 0:
            divergence = xp - xm
        elif c == 1:
            divergence = divergence + (jnp.where(myp, yp, 0.0) - jnp.where(mym, ym, 0.0))
        else:
            divergence = divergence + (jnp.where(mzp, zp, 0.0) - jnp.where(mzm, zm, 0.0))
    around = (pxm + pxp) + (pym + pyp) + (pzm + pzp)
    out.append(base[3] - STABILIZE * (6.0 * pressure - around) + 0.5 * divergence)
    return out


def face(near, own, kappa, sign):
    out = []
    for c in range(3):
        out.append(kappa * (near[c] if own is None else near[c] - own[c]))
    out[0] = out[0] - (0.5 * sign) * near[3]
    out.append(STABILIZE * near[3] + (0.5 * sign) * near[0])
    return out


def low(rows):
    return jnp.concatenate([rows, jnp.zeros((4, 128), F32)], axis=0)


def high(rows):
    return jnp.concatenate([jnp.zeros((4, 128), F32), rows], axis=0)


def corrections(units, at, lhs_ref, mask_ref):
    even = iota((8, 128), 1) % 2 == 0
    columns = []
    for unit, place in zip(units, at):
        evens = [jnp.where(even, v, pltpu.roll(v, 1, 1)) for v in unit]
        odds = [jnp.where(even, pltpu.roll(v, 127, 1), v) for v in unit]
        stack = jnp.concatenate(evens + odds, axis=0).astype(BF16).reshape(4, 16, 128)
        masked = [(stack * mask_ref[place, kind]).reshape(64, 128) for kind in range(4)]
        columns.append(jnp.concatenate(masked, axis=0))
    product = jnp.dot(
        lhs_ref[...], jnp.concatenate(columns, axis=1), preferred_element_type=F32
    )
    out = []
    for n in range(len(units)):
        across = slice(128 * n, 128 * n + 128)
        out.append(
            [
                DAMPING
                * jnp.where(even, product[8 * c : 8 * c + 8, across], product[32 + 8 * c : 40 + 8 * c, across])
                for c in range(4)
            ]
        )
    return out


def time_sums(load):
    plain = load(0)
    ramp = None
    for t in range(1, 8):
        value = load(t)
        plain = plain + value
        ramp = value * float(t) if ramp is None else ramp + value * float(t)
    return plain, ramp


def steps(body):
    def several(i, carry):
        for j in range(4):
            body(4 * i + j, i, j)
        return carry

    lax.fori_loop(0, 2, several, 0)


def kernel(
    init5, init, forc, table_in, vclass_in, bank_in, kind_in,
    smoothed, coarse, table, vclass, bank, kind,
    f0, f1, forcing, part, part2, e0, e1, lp, rp, lp2, rp2, lres, rres, ares, lcor, rcor, vk_out, vk_in,
    faces, fields, mass, coef, lhs, mask, weighted_f, parts, edges, recv, recv_e,
    load_sem, send_sem, recv_sem, psend_sem, precv_sem, esend_sem, erecv_sem, token_sem,
):
    sx = lax.axis_index("space")
    tb = lax.axis_index("tm")
    has_left, has_right = sx > 0, sx < 7
    has_before, has_after = tb > 0, tb < 31
    is_edge = jnp.logical_or(jnp.logical_and(tb < 4, has_left), jnp.logical_and(tb >= 28, has_right))
    to_left, to_right, to_after = {"space": sx - 1}, {"space": sx + 1}, {"tm": tb + 1}
    left_after, right_after = {"space": sx - 1, "tm": tb + 1}, {"space": sx + 1, "tm": tb + 1}
    both = jnp.logical_and

    barrier = pltpu.get_barrier_semaphore()

    def greet(condition, device):
        @pl.when(condition)
        def _():
            pl.semaphore_signal(barrier, inc=1, device_id=device, device_id_type=MESH)

    column, row = lax.rem(tb, 16), tb // 16
    ring = [{"tm": row * 16 + lax.rem(column + step, 16)} for step in (2, 14, 4, 12)]
    far_ring = ring[2:]
    across = {"tm": lax.rem(tb + 16, 32)}
    partner = {"tm": tb + 1 - 2 * lax.rem(tb, 2)}
    greet(has_left, to_left)
    greet(has_right, to_right)
    greet(has_before, {"tm": tb - 1})
    greet(has_after, to_after)
    for device in ring + [across]:
        greet(True, device)

    def tell(n, devices):
        for condition, device in devices:

            @pl.when(condition)
            def _(device=device):
                pl.semaphore_signal(token_sem.at[n], inc=1, device_id=device, device_id_type=MESH)

    circles = [
        [(True, partner)],
        [(True, device) for device in ring],
        [(True, device) for device in far_ring],
        [(True, across)],
    ]
    counts = [1, 4, 2, 1]

    def pass_on(n):
        if n > 0:
            pl.semaphore_wait(token_sem.at[n - 1], counts[n - 1])
        if n < 4:
            tell(n, circles[n])

    loads = [
        pltpu.make_async_copy(table_in, table, load_sem.at[0]),
        pltpu.make_async_copy(vclass_in, vclass, load_sem.at[1]),
        pltpu.make_async_copy(kind_in, kind, load_sem.at[2]),
        pltpu.make_async_copy(init, f0, load_sem.at[3]),
        pltpu.make_async_copy(forc, forcing, load_sem.at[4]),
        pltpu.make_async_copy(bank_in, bank, load_sem.at[5]),
    ]
    for copy in loads:
        copy.start()

    @pl.when(sx == 0)
    def _():
        vk_in[0] = jnp.zeros((16, 128), F32)
        lp[...] = jnp.zeros_like(lp)
        lres[...] = jnp.zeros_like(lres)

    @pl.when(sx == 7)
    def _():
        vk_in[1] = jnp.zeros((16, 128), F32)
        rp[...] = jnp.zeros_like(rp)
        rres[...] = jnp.zeros_like(rres)

    @pl.when(tb == 0)
    def _():
        e0[...] = jnp.zeros_like(e0)
        ares[...] = jnp.zeros_like(ares)

    @pl.when(jnp.logical_or(tb == 0, sx == 0))
    def _():
        lcor[...] = jnp.zeros_like(lcor)

    @pl.when(jnp.logical_or(tb == 0, sx == 7))
    def _():
        rcor[...] = jnp.zeros_like(rcor)

    @pl.when(jnp.logical_not(is_edge))
    def _():
        recv_e[...] = jnp.zeros_like(recv_e)

    loads[0].wait()
    loads[1].wait()
    viscosity = jnp.zeros((4, 8, 128), F32)
    for label in range(8):
        viscosity = jnp.where(vclass[...] == label, table[label], viscosity)
    build_coefficients(viscosity, coef)
    loads[2].wait()
    maps = kind_maps(kind)
    vk_out[0, 0:4] = viscosity[0, 0:4]
    vk_out[1, 0:4] = viscosity[3, 4:8]
    vk_out[0, 4:8] = jnp.zeros((4, 128), F32)
    vk_out[1, 4:8] = jnp.zeros((4, 128), F32)
    vk_out[0, 8:16] = maps[0]
    vk_out[1, 8:16] = maps[3]
    for g in range(4):
        store_mask(maps[g], mask, g + 1)
    loads[3].wait()
    loads[4].wait()

    nothing = [jnp.zeros((4, 128), F32)] * 4

    def local(t, i, j):
        now = [f0[c, t] for c in range(4)]
        base = [forcing[c, t] for c in range(4)]
        for c in range(3):
            base[c] = base[c] + (f0[c, t - 1] if j else jnp.where(i > 0, f0[c, jnp.maximum(t - 1, 0)], 0.0))
        for c, value in enumerate(residual(now, nothing, nothing, base, coef[0], coef)):
            part[c, t] = value

    steps(local)

    one = lambda condition: condition.astype(jnp.int32)
    pl.semaphore_wait(
        barrier,
        5 + one(has_left) + one(has_right) + one(has_before) + one(has_after),
    )

    def remote(condition, awaited, source, target, n, device):
        copy = pltpu.make_async_remote_copy(
            source, target, send_sem.at[n], recv_sem.at[n], device_id=device, device_id_type=MESH
        )
        return condition, awaited, copy

    round_one = [
        remote(has_left, has_right, vk_out.at[0], vk_in.at[1], 0, to_left),
        remote(has_right, has_left, vk_out.at[1], vk_in.at[0], 1, to_right),
        remote(has_left, has_right, init5.at[:, :, 0], rp, 2, to_left),
        remote(has_right, has_left, init5.at[:, :, 7], lp, 3, to_right),
        remote(has_after, has_before, init.at[0:3, 7], e0, 4, to_after),
        remote(has_after, has_before, part.at[:, 7], ares, 5, to_after),
        remote(both(has_left, has_after), both(has_right, has_before), init.at[:, 7, 0], rcor, 6, left_after),
        remote(both(has_right, has_after), both(has_left, has_before), init.at[:, 7, 3], lcor, 7, right_after),
    ]
    for i in range(2):
        pair = slice(4 * i, 4 * i + 4)
        round_one += [
            remote(has_left, has_right, part.at[:, pair, 0], rres.at[:, pair], 8 + 2 * i, to_left),
            remote(has_right, has_left, part.at[:, pair, 3], lres.at[:, pair], 9 + 2 * i, to_right),
        ]
    for condition, _, copy in round_one[:6] + round_one[8:]:
        pl.when(condition)(copy.start)
    tell(4, [(has_before, {"tm": tb - 1})])
    pass_on(0)

    def arrive(first, last):
        for _, awaited, copy in round_one[first:last]:
            pl.when(awaited)(copy.wait_recv)

    loads[5].wait()
    build_bank(bank, lhs)
    pass_on(1)

    @pl.when(has_after)
    def _():
        pl.semaphore_wait(token_sem.at[4], 1)
        for condition, _, copy in round_one[6:8]:
            pl.when(condition)(copy.start)

    first = (lax.rem(tb, 4) * 8).astype(F32) * (1.0 / 1024.0)

    def weigh(plain, ramp):
        far = first * plain + ramp * (1.0 / 1024.0)
        return plain * (1.0 / 32.0) - far, far

    for c in range(4):
        near, far = weigh(*time_sums(lambda t, c=c: forcing[c, t]))
        weighted_f[0, c] = near
        weighted_f[1, c] = far


    for pair in ((1, 2), (3, 4), (5, 6), (7,)):
        where = [(t, g) for t in pair for g in (1, 2)]
        units = [[part[c, t, g] for c in range(4)] for t, g in where]
        for (t, g), change in zip(where, corrections(units, [g + 1 for _, g in where], lhs, mask)):
            for c in range(4):
                f1[c, t, g] = f0[c, t, g] + change[c]

    pass_on(2)
    arrive(0, 2)
    faces[0] = 0.5 * (viscosity[0, 0:4] + vk_in[0, 0:4])
    faces[1] = 0.5 * (viscosity[3, 4:8] + vk_in[1, 0:4])
    store_mask(vk_in[0, 8:16], mask, 0)
    store_mask(vk_in[1, 8:16], mask, 5)
    arrive(2, 5)
    pass_on(3)

    units = [[part[c, 0, g] + (e0[c, g] if c < 3 else 0.0) for c in range(4)] for g in (1, 2)]
    for g, change in zip((1, 2), corrections(units, [2, 3], lhs, mask)):
        for c in range(4):
            f1[c, 0, g] = f0[c, 0, g] + change[c]

    def plane(ref, t, side):
        if side == 0:
            return [ref[c, t, 0, 0:4] for c in range(4)]
        return [ref[c, t, 3, 4:8] for c in range(4)]

    def outer(t, i, j):
        units = []
        for side, g, near, sign, place in ((0, 0, lp, -1.0, low), (1, 3, rp, 1.0, high)):
            extra = face([near[c, t] for c in range(4)], plane(f0, t, side), faces[side], sign)
            unit = [part[c, t, g] + place(extra[c]) for c in range(4)]
            if j == 0:
                unit = [unit[c] + jnp.where(i == 0, e0[c, g], 0.0) for c in range(3)] + unit[3:]
            units.append(unit)
        for g, change in zip((0, 3), corrections(units, [1, 4], lhs, mask)):
            for c in range(4):
                f1[c, t, g] = f0[c, t, g] + change[c]

    steps(outer)


    def middle(pair):
        units = []
        for t in pair:
            now = [f1[c, t] for c in range(4)]
            base = [forcing[c, t] for c in range(4)]
            for c in range(3):
                base[c] = base[c] + (f1[c, t - 1] if t > 0 else e1[c])
            resid = residual(now, nothing, nothing, base, coef[0], coef)
            for c in range(4):
                part2[c, t] = resid[c]
            units += [[resid[c][g] for c in range(4)] for g in (1, 2)]
        changes = corrections(units, [2, 3] * len(pair), lhs, mask)
        for n, t in enumerate(pair):
            for g in (1, 2):
                for c in range(4):
                    smoothed[c, t, g] = f1[c, t, g] + changes[2 * n + g - 1][c]

    middle((1, 2, 3))
    middle((4, 5, 6, 7))

    arrive(5, 8)
    units = [[ares[c, g] for c in range(4)] for g in range(4)]
    old = [e0[c, 0, 0:4] for c in range(3)]
    extra = face([lcor[c, 4:8] for c in range(4)], old, faces[0], -1.0)
    units[0] = [units[0][c] + low(extra[c]) for c in range(4)]
    old = [e0[c, 3, 4:8] for c in range(3)]
    extra = face([rcor[c, 0:4] for c in range(4)], old, faces[1], 1.0)
    units[3] = [units[3][c] + high(extra[c]) for c in range(4)]
    for g, change in enumerate(corrections(units, [1, 2, 3, 4], lhs, mask)):
        for c in range(3):
            e1[c, g] = e0[c, g] + change[c]

    middle((0,))


    def sum_up(rows):
        for c in range(4):
            plain, ramp = time_sums(lambda t: smoothed[c, t, rows])
            near, far = weigh(plain, ramp)
            fields[0, c, rows] = near
            fields[1, c, rows] = far
            mass[c, rows] = plain * (1.0 / 1024.0)

    sum_up(slice(1, 3))

    def beside(pair):
        units = []
        for t in pair:
            extra = face(plane(f0, t, 0), [lp[c, t] for c in range(4)], faces[0], 1.0)
            unit = [lres[c, t] + high(extra[c]) for c in range(4)]
            if t == 0:
                unit = [unit[c] + lcor[c] for c in range(3)] + unit[3:]
            units.append(unit)
            extra = face(plane(f0, t, 1), [rp[c, t] for c in range(4)], faces[1], -1.0)
            unit = [rres[c, t] + low(extra[c]) for c in range(4)]
            if t == 0:
                unit = [unit[c] + rcor[c] for c in range(3)] + unit[3:]
            units.append(unit)
        changes = corrections(units, [0, 5] * 8, lhs, mask)
        for n, t in enumerate(pair):
            for c in range(4):
                lp2[c, t] = jnp.where(has_left, lp[c, t] + changes[2 * n][c][4:8], 0.0)
                rp2[c, t] = jnp.where(has_right, rp[c, t] + changes[2 * n + 1][c][0:4], 0.0)

    def ends(pair):
        units = []
        for t in pair:
            for side, g, near, sign, place in ((0, 0, lp2, -1.0, low), (1, 3, rp2, 1.0, high)):
                extra = face([near[c, t] for c in range(4)], plane(f1, t, side), faces[side], sign)
                units.append([part2[c, t, g] + place(extra[c]) for c in range(4)])
        changes = corrections(units, [1, 4] * 8, lhs, mask)
        for n, t in enumerate(pair):
            for side, g in ((0, 0), (1, 3)):
                for c in range(4):
                    smoothed[c, t, g] = f1[c, t, g] + changes[2 * n + side][c]

    arrive(8, 12)
    beside(range(8))
    ends(range(8))

    for g in (0, 3):
        sum_up(slice(g, g + 1))
    for half in range(2):
        for side, rows, sign in ((0, slice(0, 4), 1.0), (1, slice(4, 8), -1.0)):
            near = [fields[half, c, 3 * side, rows] for c in range(4)]
            for c, value in enumerate(face(near, None, faces[side], sign)):
                edges[side, pl.ds(4 * half + c, 4, stride=8), :] = value

    def edge_piece(side, y, device):
        return pltpu.make_async_remote_copy(
            edges.at[side, pl.ds(8 * y, 8)], recv_e.at[tb], esend_sem.at[side], erecv_sem,
            device_id=device, device_id_type=MESH,
        )


    pass_on(4)

    @pl.when(has_left)
    def _():
        for y in range(4):
            edge_piece(0, y, {"space": sx - 1, "tm": 28 + y}).start()

    @pl.when(has_right)
    def _():
        for y in range(4):
            edge_piece(1, y, {"space": sx + 1, "tm": y}).start()

    for half in range(2):
        now = [fields[half, c] for c in range(4)]
        base = [weighted_f[half, c] for c in range(4)]
        for c in range(3):
            base[c] = base[c] - mass[c] if half == 0 else base[c] + mass[c]
        resid = residual(now, nothing, nothing, base, coef[7], coef)
        for c in range(4):
            row = 4 * half + c
            for g in range(4):
                value = resid[c][g]
                if c < 3 and g == 0:
                    value = value - low(faces[0] * now[c][0, 0:4])
                if c < 3 and g == 3:
                    value = value - high(faces[1] * now[c][3, 4:8])
                parts[pl.ds(64 * g + row, 8, stride=8), :] = value

    def tile(ref, row):
        return ref.at[pl.ds(pl.multiple_of(row * 8, 8), 8)]

    def send(step, carry):
        k = step // 4
        odd = lax.rem(k, 2)
        dz = 4 + (k // 2) * (1 - odd) - ((k + 1) // 2) * odd
        column = lax.rem(lax.rem(tb, 16) + 2 * dz, 16)
        column = column // 2 * 2 + lax.rem(tb + step, 2)
        peer = lax.rem(tb // 16 + 1 + lax.rem(step // 2, 2), 2) * 16 + column

        @pl.when(peer != tb)
        def _():
            pltpu.make_async_remote_copy(
                tile(parts, peer), recv.at[tb], psend_sem, precv_sem,
                device_id={"tm": peer}, device_id_type=MESH,
            ).start()

        return carry

    lax.fori_loop(0, 32, send, 0)
    recv[tb] = tile(parts, tb)[...]

    for condition, _, copy in round_one:
        pl.when(condition)(copy.wait_send)

    def sent_edges(side, device):
        pltpu.make_async_remote_copy(
            edges.at[side], edges.at[side], esend_sem.at[side], erecv_sem,
            device_id=device, device_id_type=MESH,
        ).wait_send()

    pl.when(has_left)(lambda: sent_edges(0, to_left))
    pl.when(has_right)(lambda: sent_edges(1, to_right))
    pieces = pltpu.make_async_remote_copy(
        recv.at[0:31], recv.at[0:31], psend_sem, precv_sem, device_id=to_after, device_id_type=MESH
    )
    pieces.wait_send()
    pieces.wait_recv()

    @pl.when(is_edge)
    def _():
        pltpu.make_async_remote_copy(
            recv_e, recv_e, psend_sem, erecv_sem, device_id=to_after, device_id_type=MESH
        ).wait_recv()

    before = jnp.zeros((4, 128), F32)
    for k in range(8):
        block = (recv[4 * k] + recv[4 * k + 1]) + (recv[4 * k + 2] + recv[4 * k + 3])
        block = block + (
            (recv_e[4 * k] + recv_e[4 * k + 1]) + (recv_e[4 * k + 2] + recv_e[4 * k + 3])
        )
        level = block[0:4] + before
        before = block[4:8]
        for c in range(4):
            coarse[c, k : k + 1, :] = level[c : c + 1]


def store(smoothed_in, coarse_in, smoothed, coarse, sems):
    copies = [
        pltpu.make_async_copy(smoothed_in, smoothed, sems.at[0]),
        pltpu.make_async_copy(coarse_in, coarse, sems.at[1]),
    ]
    for copy in copies:
        copy.start()
    for copy in copies:
        copy.wait()


def per_device(initial_guess, forcing, visc_table, visc_class, inverse_bank, patch_kind):
    hbm = pl.BlockSpec(memory_space=pltpu.HBM)
    vmem = pl.BlockSpec(memory_space=pltpu.VMEM)
    dma = pltpu.SemaphoreType.DMA
    smoothed, coarse = pl.pallas_call(
        kernel,
        out_shape=(
            pltpu.VMEM((4, 8, 4, 8, 128), F32),
            pltpu.VMEM((4, 8, 128), F32),
        ),
        in_specs=[hbm] * 7,
        out_specs=(vmem, vmem),
        scratch_shapes=[
            pltpu.SMEM((8,), F32),
            pltpu.VMEM((4, 8, 128), jnp.int32),
            pltpu.VMEM((4, 32, 32), BF16),
            pltpu.VMEM((4, 2, 64), jnp.int32),
            pltpu.VMEM((4, 8, 4, 8, 128), F32),
            pltpu.VMEM((4, 8, 4, 8, 128), F32),
            pltpu.VMEM((4, 8, 4, 8, 128), F32),
            pltpu.VMEM((4, 8, 4, 8, 128), F32),
            pltpu.VMEM((4, 8, 4, 8, 128), F32),
            pltpu.VMEM((3, 4, 8, 128), F32),
            pltpu.VMEM((3, 4, 8, 128), F32),
            pltpu.VMEM((4, 8, 4, 128), F32),
            pltpu.VMEM((4, 8, 4, 128), F32),
            pltpu.VMEM((4, 8, 4, 128), F32),
            pltpu.VMEM((4, 8, 4, 128), F32),
            pltpu.VMEM((4, 8, 8, 128), F32),
            pltpu.VMEM((4, 8, 8, 128), F32),
            pltpu.VMEM((4, 4, 8, 128), F32),
            pltpu.VMEM((4, 8, 128), F32),
            pltpu.VMEM((4, 8, 128), F32),
            pltpu.VMEM((2, 16, 128), F32),
            pltpu.VMEM((2, 16, 128), F32),
            pltpu.VMEM((2, 4, 128), F32),
            pltpu.VMEM((2, 4, 4, 8, 128), F32),
            pltpu.VMEM((4, 4, 8, 128), F32),
            pltpu.VMEM((8, 4, 8, 128), F32),
            pltpu.VMEM((64, 256), BF16),
            pltpu.VMEM((6, 4, 16, 128), BF16),
            pltpu.VMEM((2, 4, 4, 8, 128), F32),
            pltpu.VMEM((256, 128), F32),
            pltpu.VMEM((2, 32, 128), F32),
            pltpu.VMEM((32, 8, 128), F32),
            pltpu.VMEM((32, 8, 128), F32),
            dma((6,)),
            dma((12,)),
            dma((12,)),
            dma,
            dma,
            dma((2,)),
            dma,
            pltpu.SemaphoreType.REGULAR((5,)),
        ],
        compiler_params=pltpu.CompilerParams(
            collective_id=0, has_side_effects=True, vmem_limit_bytes=60 * 1024 * 1024
        ),
    )(
        initial_guess,
        initial_guess.reshape(4, 8, 4, 8, 128),
        forcing.reshape(4, 8, 4, 8, 128),
        visc_table,
        visc_class.reshape(4, 8, 128),
        inverse_bank,
        patch_kind,
    )
    smoothed, coarse = pl.pallas_call(
        store,
        out_shape=(
            jax.ShapeDtypeStruct((4, 8, 4, 8, 128), F32),
            jax.ShapeDtypeStruct((4, 8, 128), F32),
        ),
        in_specs=[pl.BlockSpec(memory_space=pl.ANY)] * 2,
        out_specs=(pl.BlockSpec(memory_space=pl.ANY),) * 2,
        scratch_shapes=[dma((2,))],
        compiler_params=pltpu.CompilerParams(vmem_limit_bytes=4 * 1024 * 1024),
    )(smoothed, coarse)
    return smoothed.reshape(4, 8, 8, 4, 128), coarse


def solution(mesh):
    return jax.shard_map(
        per_device,
        mesh=mesh,
        in_specs=(
            P(None, "tm", "space", None, None),
            P(None, "tm", "space", None, None),
            P(),
            P("space", None, None),
            P(),
            P("space", None, None),
        ),
        out_specs=(P(None, "tm", "space", None, None), P(None, None, ("space", "tm"))),
        check_vma=False,
    )
```

```python
import functools

import jax
import jax.numpy as jnp
from jax import lax
from jax.experimental import pallas as pl
from jax.experimental.pallas import tpu as pltpu
from jax.sharding import PartitionSpec as P

MESH = pl.DeviceIdType.MESH
F32 = jnp.float32
BF16 = jnp.bfloat16
DAMPING = 0.8
STABILIZE = 0.1


def iota(shape, dim):
    return lax.broadcasted_iota(jnp.int32, shape, dim)


def cell_index(q):
    return (q // 8) * 8 + (q // 4 % 2) * 4 + (q % 2) * 2


def build_bank(bank_ref, lhs_ref):
    j = iota((32, 64), 0)
    q = iota((32, 64), 1)
    spread = (j == cell_index(q % 32) + q // 32).astype(BF16)
    p = iota((64, 32), 0)
    i = iota((64, 32), 1)
    gather = (i == cell_index(p % 32) + p // 32).astype(BF16)
    same = (iota((64, 64), 0) // 2 % 2) == (iota((64, 64), 1) // 2 % 2)
    wide = jnp.dot(bank_ref[...].reshape(128, 32), spread, preferred_element_type=F32).astype(BF16)
    parts = []
    for kind in range(4):
        part = jnp.dot(gather, wide[32 * kind : 32 * kind + 32], preferred_element_type=F32)
        parts.append(jnp.where(same, part, 0.0).astype(BF16))
    lhs_ref[...] = jnp.concatenate(parts, axis=1)


def kind_maps(kind_ref):
    upper = iota((8, 64), 0) // 2 % 2 == 0
    double = (iota((64, 128), 0) == iota((64, 128), 1) // 2).astype(BF16)
    maps = []
    for g in range(4):
        pair = kind_ref[g].astype(F32)
        rows = jnp.where(upper, pair[0:1], pair[1:2]).astype(BF16)
        maps.append(jnp.dot(rows, double, preferred_element_type=F32))
    return maps


def store_mask(kinds, mask_ref, at):
    for kind in range(4):
        mask = (kinds == float(kind)).astype(F32)
        mask_ref[at, kind] = jnp.concatenate([mask, mask], axis=0).astype(BF16)


def shift_x(values, left, right):
    first = jnp.concatenate([left, values[0, 0:4]], axis=0)
    last = jnp.concatenate([values[3, 4:8], right], axis=0)
    low = iota((3, 8, 128), 1) < 4
    inner = pltpu.roll(jnp.where(low, values[1:4], values[0:3]), 4, 1)
    return (
        jnp.concatenate([first[None], inner], axis=0),
        jnp.concatenate([inner, last[None]], axis=0),
    )


def shifts_yz(values):
    return (
        pltpu.roll(values, 1, 1),
        pltpu.roll(values, 7, 1),
        pltpu.roll(values, 1, 2),
        pltpu.roll(values, 127, 2),
    )


def edge_masks():
    y = iota((4, 8, 128), 1) % 4
    z = iota((4, 8, 128), 2)
    return y != 0, y != 3, z != 0, z != 127


def build_coefficients(viscosity, coef_ref):
    none = jnp.zeros((4, 128), F32)
    xm, xp = shift_x(viscosity, none, none)
    ym, yp, zm, zp = shifts_yz(viscosity)
    g, row = iota((4, 8, 128), 0), iota((4, 8, 128), 1)
    has_xm = jnp.logical_or(g > 0, row >= 4)
    has_xp = jnp.logical_or(g < 3, row < 4)
    total = jnp.zeros_like(viscosity)
    for n, (near, mask) in enumerate(zip((xm, xp, ym, yp, zm, zp), (has_xm, has_xp) + edge_masks())):
        near = jnp.where(mask, near, 0.0)
        kappa = 0.5 * (viscosity + near)
        inner = jnp.where(mask, kappa, 0.0)
        total = total + (inner if n < 2 else kappa)
        coef_ref[1 + n] = inner
    coef_ref[0] = total + 1.0
    coef_ref[7] = total


def residual(now, left, right, base, diagonal, coef_ref):
    mym, myp, mzm, mzp = edge_masks()
    pressure = now[3]
    pxm, pxp = shift_x(pressure, left[3], right[3])
    pym, pyp, pzm, pzp = shifts_yz(pressure)
    pym = jnp.where(mym, pym, 0.0)
    pyp = jnp.where(myp, pyp, 0.0)
    pzm = jnp.where(mzm, pzm, 0.0)
    pzp = jnp.where(mzp, pzp, 0.0)
    gradients = (pxp - pxm, pyp - pym, pzp - pzm)
    out = []
    divergence = None
    for c in range(3):
        value = now[c]
        xm, xp = shift_x(value, left[c], right[c])
        ym, yp, zm, zp = shifts_yz(value)
        flow = coef_ref[1] * xm + coef_ref[2] * xp
        flow = flow + (coef_ref[3] * ym + coef_ref[4] * yp)
        flow = flow + (coef_ref[5] * zm + coef_ref[6] * zp)
        out.append(base[c] - diagonal * value + flow - 0.5 * gradients[c])
        if c == 0:
            divergence = xp - xm
        elif c == 1:
            divergence = divergence + (jnp.where(myp, yp, 0.0) - jnp.where(mym, ym, 0.0))
        else:
            divergence = divergence + (jnp.where(mzp, zp, 0.0) - jnp.where(mzm, zm, 0.0))
    around = (pxm + pxp) + (pym + pyp) + (pzm + pzp)
    out.append(base[3] - STABILIZE * (6.0 * pressure - around) + 0.5 * divergence)
    return out


def face(near, own, kappa, sign):
    out = []
    for c in range(3):
        out.append(kappa * (near[c] if own is None else near[c] - own[c]))
    out[0] = out[0] - (0.5 * sign) * near[3]
    out.append(STABILIZE * near[3] + (0.5 * sign) * near[0])
    return out


def low(rows):
    return jnp.concatenate([rows, jnp.zeros((4, 128), F32)], axis=0)


def high(rows):
    return jnp.concatenate([jnp.zeros((4, 128), F32), rows], axis=0)


def corrections(units, at, lhs_ref, mask_ref):
    even = iota((8, 128), 1) % 2 == 0
    columns = []
    for unit, place in zip(units, at):
        evens = [jnp.where(even, v, pltpu.roll(v, 1, 1)) for v in unit]
        odds = [jnp.where(even, pltpu.roll(v, 127, 1), v) for v in unit]
        stack = jnp.concatenate(evens + odds, axis=0).astype(BF16).reshape(4, 16, 128)
        masked = [(stack * mask_ref[place, kind]).reshape(64, 128) for kind in range(4)]
        columns.append(jnp.concatenate(masked, axis=0))
    product = jnp.dot(
        lhs_ref[...], jnp.concatenate(columns, axis=1), preferred_element_type=F32
    )
    out = []
    for n in range(len(units)):
        across = slice(128 * n, 128 * n + 128)
        out.append(
            [
                DAMPING
                * jnp.where(even, product[8 * c : 8 * c + 8, across], product[32 + 8 * c : 40 + 8 * c, across])
                for c in range(4)
            ]
        )
    return out


def time_sums(load):
    plain = load(0)
    ramp = None
    for t in range(1, 8):
        value = load(t)
        plain = plain + value
        ramp = value * float(t) if ramp is None else ramp + value * float(t)
    return plain, ramp


def steps(body):
    def several(i, carry):
        for j in range(4):
            body(4 * i + j, i, j)
        return carry

    lax.fori_loop(0, 2, several, 0)


def kernel(
    init5, init, forc, table_in, vclass_in, bank_in, kind_in,
    smoothed, coarse, table, vclass, bank, kind,
    f0, f1, forcing, part, part2, e0, e1, lp, rp, lp2, rp2, lres, rres, ares, lcor, rcor, vk_out, vk_in,
    faces, fields, mass, coef, lhs, mask, weighted_f, parts, edges, parts_in, edges_in, sums, edge_sums, recv, recv_e,
    load_sem, send_sem, recv_sem, psend_sem, precv_sem, esend_sem, erecv_sem, token_sem, pair_send, pair_recv,
):
    sx = lax.axis_index("space")
    tb = lax.axis_index("tm")
    has_left, has_right = sx > 0, sx < 7
    has_before, has_after = tb > 0, tb < 31
    is_edge = jnp.logical_or(jnp.logical_and(tb < 4, has_left), jnp.logical_and(tb >= 28, has_right))
    to_left, to_right, to_after = {"space": sx - 1}, {"space": sx + 1}, {"tm": tb + 1}
    left_after, right_after = {"space": sx - 1, "tm": tb + 1}, {"space": sx + 1, "tm": tb + 1}
    both = jnp.logical_and

    barrier = pltpu.get_barrier_semaphore()

    def greet(condition, device):
        @pl.when(condition)
        def _():
            pl.semaphore_signal(barrier, inc=1, device_id=device, device_id_type=MESH)

    column, row = lax.rem(tb, 16), tb // 16
    ring = [{"tm": row * 16 + lax.rem(column + step, 16)} for step in (2, 14, 4, 12)]
    far_ring = ring[2:]
    across = {"tm": lax.rem(tb + 16, 32)}
    partner = {"tm": tb + 1 - 2 * lax.rem(tb, 2)}
    greet(has_left, to_left)
    greet(has_right, to_right)
    greet(has_before, {"tm": tb - 1})
    greet(has_after, to_after)
    for device in ring + [across]:
        greet(True, device)

    def tell(n, devices):
        for condition, device in devices:

            @pl.when(condition)
            def _(device=device):
                pl.semaphore_signal(token_sem.at[n], inc=1, device_id=device, device_id_type=MESH)

    circles = [
        [(True, partner)],
        [(True, device) for device in ring],
        [(True, device) for device in far_ring],
        [(True, across)],
    ]
    counts = [1, 4, 2, 1]

    def pass_on(n):
        if n > 0:
            pl.semaphore_wait(token_sem.at[n - 1], counts[n - 1])
        if n < 4:
            tell(n, circles[n])

    loads = [
        pltpu.make_async_copy(table_in, table, load_sem.at[0]),
        pltpu.make_async_copy(vclass_in, vclass, load_sem.at[1]),
        pltpu.make_async_copy(kind_in, kind, load_sem.at[2]),
        pltpu.make_async_copy(init, f0, load_sem.at[3]),
        pltpu.make_async_copy(forc, forcing, load_sem.at[4]),
        pltpu.make_async_copy(bank_in, bank, load_sem.at[5]),
    ]
    for copy in loads:
        copy.start()

    @pl.when(sx == 0)
    def _():
        vk_in[0] = jnp.zeros((16, 128), F32)
        lp[...] = jnp.zeros_like(lp)
        lres[...] = jnp.zeros_like(lres)

    @pl.when(sx == 7)
    def _():
        vk_in[1] = jnp.zeros((16, 128), F32)
        rp[...] = jnp.zeros_like(rp)
        rres[...] = jnp.zeros_like(rres)

    @pl.when(tb == 0)
    def _():
        e0[...] = jnp.zeros_like(e0)
        ares[...] = jnp.zeros_like(ares)

    @pl.when(jnp.logical_or(tb == 0, sx == 0))
    def _():
        lcor[...] = jnp.zeros_like(lcor)

    @pl.when(jnp.logical_or(tb == 0, sx == 7))
    def _():
        rcor[...] = jnp.zeros_like(rcor)

    @pl.when(jnp.logical_not(is_edge))
    def _():
        recv_e[...] = jnp.zeros_like(recv_e)

    one = lambda condition: condition.astype(jnp.int32)
    pl.semaphore_wait(
        barrier,
        5 + one(has_left) + one(has_right) + one(has_before) + one(has_after),
    )

    def remote(condition, awaited, source, target, n, device):
        copy = pltpu.make_async_remote_copy(
            source, target, send_sem.at[n], recv_sem.at[n], device_id=device, device_id_type=MESH
        )
        return condition, awaited, copy

    round_one = [
        remote(has_left, has_right, vk_out.at[0], vk_in.at[1], 0, to_left),
        remote(has_right, has_left, vk_out.at[1], vk_in.at[0], 1, to_right),
        remote(has_left, has_right, init5.at[:, :, 0], rp, 2, to_left),
        remote(has_right, has_left, init5.at[:, :, 7], lp, 3, to_right),
        remote(has_after, has_before, init.at[0:3, 7], e0, 4, to_after),
        remote(has_after, has_before, part.at[:, 7], ares, 5, to_after),
        remote(both(has_left, has_after), both(has_right, has_before), init.at[:, 7, 0], rcor, 6, left_after),
        remote(both(has_right, has_after), both(has_left, has_before), init.at[:, 7, 3], lcor, 7, right_after),
    ]
    for i in range(2):
        pair = slice(4 * i, 4 * i + 4)
        round_one += [
            remote(has_left, has_right, part.at[:, pair, 0], rres.at[:, pair], 8 + 2 * i, to_left),
            remote(has_right, has_left, part.at[:, pair, 3], lres.at[:, pair], 9 + 2 * i, to_right),
        ]
    def begin(*places):
        for place in places:
            condition, _, copy = round_one[place]
            pl.when(condition)(copy.start)

    begin(2, 3, 4)
    tell(4, [(has_before, {"tm": tb - 1})])
    pass_on(0)

    loads[0].wait()
    loads[1].wait()
    viscosity = jnp.zeros((4, 8, 128), F32)
    for label in range(8):
        viscosity = jnp.where(vclass[...] == label, table[label], viscosity)
    build_coefficients(viscosity, coef)
    loads[2].wait()
    maps = kind_maps(kind)
    vk_out[0, 0:4] = viscosity[0, 0:4]
    vk_out[1, 0:4] = viscosity[3, 4:8]
    vk_out[0, 4:8] = jnp.zeros((4, 128), F32)
    vk_out[1, 4:8] = jnp.zeros((4, 128), F32)
    vk_out[0, 8:16] = maps[0]
    vk_out[1, 8:16] = maps[3]
    begin(0, 1)
    for g in range(4):
        store_mask(maps[g], mask, g + 1)
    loads[3].wait()
    loads[4].wait()

    nothing = [jnp.zeros((4, 128), F32)] * 4

    def local(t):
        now = [f0[c, t] for c in range(4)]
        base = [forcing[c, t] for c in range(4)]
        if t > 0:
            base = [base[c] + f0[c, t - 1] for c in range(3)] + base[3:]
        for c, value in enumerate(residual(now, nothing, nothing, base, coef[0], coef)):
            part[c, t] = value

    for t in range(4):
        local(t)
    begin(8, 9)
    for t in range(4, 8):
        local(t)
    @pl.when(has_after)
    def _():
        pl.semaphore_wait(token_sem.at[4], 1)
        begin(6, 7)

    begin(10, 11, 5)

    def arrive(first, last):
        for _, awaited, copy in round_one[first:last]:
            pl.when(awaited)(copy.wait_recv)

    loads[5].wait()
    build_bank(bank, lhs)
    pass_on(1)

    first = (lax.rem(tb, 4) * 8).astype(F32) * (1.0 / 1024.0)

    def weigh(plain, ramp):
        far = first * plain + ramp * (1.0 / 1024.0)
        return plain * (1.0 / 32.0) - far, far

    for c in range(4):
        near, far = weigh(*time_sums(lambda t, c=c: forcing[c, t]))
        weighted_f[0, c] = near
        weighted_f[1, c] = far


    for pair in ((1, 2), (3, 4), (5, 6), (7,)):
        where = [(t, g) for t in pair for g in (1, 2)]
        units = [[part[c, t, g] for c in range(4)] for t, g in where]
        for (t, g), change in zip(where, corrections(units, [g + 1 for _, g in where], lhs, mask)):
            for c in range(4):
                f1[c, t, g] = f0[c, t, g] + change[c]

    pass_on(2)
    arrive(0, 2)
    faces[0] = 0.5 * (viscosity[0, 0:4] + vk_in[0, 0:4])
    faces[1] = 0.5 * (viscosity[3, 4:8] + vk_in[1, 0:4])
    store_mask(vk_in[0, 8:16], mask, 0)
    store_mask(vk_in[1, 8:16], mask, 5)
    arrive(2, 5)
    pass_on(3)

    units = [[part[c, 0, g] + (e0[c, g] if c < 3 else 0.0) for c in range(4)] for g in (1, 2)]
    for g, change in zip((1, 2), corrections(units, [2, 3], lhs, mask)):
        for c in range(4):
            f1[c, 0, g] = f0[c, 0, g] + change[c]

    def plane(ref, t, side):
        if side == 0:
            return [ref[c, t, 0, 0:4] for c in range(4)]
        return [ref[c, t, 3, 4:8] for c in range(4)]

    def outer(t, i, j):
        units = []
        for side, g, near, sign, place in ((0, 0, lp, -1.0, low), (1, 3, rp, 1.0, high)):
            extra = face([near[c, t] for c in range(4)], plane(f0, t, side), faces[side], sign)
            unit = [part[c, t, g] + place(extra[c]) for c in range(4)]
            if j == 0:
                unit = [unit[c] + jnp.where(i == 0, e0[c, g], 0.0) for c in range(3)] + unit[3:]
            units.append(unit)
        for g, change in zip((0, 3), corrections(units, [1, 4], lhs, mask)):
            for c in range(4):
                f1[c, t, g] = f0[c, t, g] + change[c]

    steps(outer)


    def middle(pair):
        units = []
        for t in pair:
            now = [f1[c, t] for c in range(4)]
            base = [forcing[c, t] for c in range(4)]
            for c in range(3):
                base[c] = base[c] + (f1[c, t - 1] if t > 0 else e1[c])
            resid = residual(now, nothing, nothing, base, coef[0], coef)
            for c in range(4):
                part2[c, t] = resid[c]
            units += [[resid[c][g] for c in range(4)] for g in (1, 2)]
        changes = corrections(units, [2, 3] * len(pair), lhs, mask)
        for n, t in enumerate(pair):
            for g in (1, 2):
                for c in range(4):
                    smoothed[c, t, g] = f1[c, t, g] + changes[2 * n + g - 1][c]

    middle((1, 2, 3))
    middle((4, 5, 6, 7))


    def sum_up(rows):
        for c in range(4):
            plain, ramp = time_sums(lambda t: smoothed[c, t, rows])
            near, far = weigh(plain, ramp)
            fields[0, c, rows] = near
            fields[1, c, rows] = far
            mass[c, rows] = plain * (1.0 / 1024.0)

    def beside(pair):
        units = []
        for t in pair:
            extra = face(plane(f0, t, 0), [lp[c, t] for c in range(4)], faces[0], 1.0)
            unit = [lres[c, t] + high(extra[c]) for c in range(4)]
            if t == 0:
                unit = [unit[c] + lcor[c] for c in range(3)] + unit[3:]
            units.append(unit)
            extra = face(plane(f0, t, 1), [rp[c, t] for c in range(4)], faces[1], -1.0)
            unit = [rres[c, t] + low(extra[c]) for c in range(4)]
            if t == 0:
                unit = [unit[c] + rcor[c] for c in range(3)] + unit[3:]
            units.append(unit)
        changes = corrections(units, [0, 5] * 8, lhs, mask)
        for n, t in enumerate(pair):
            for c in range(4):
                lp2[c, t] = jnp.where(has_left, lp[c, t] + changes[2 * n][c][4:8], 0.0)
                rp2[c, t] = jnp.where(has_right, rp[c, t] + changes[2 * n + 1][c][0:4], 0.0)

    def ends(pair):
        units = []
        for t in pair:
            for side, g, near, sign, place in ((0, 0, lp2, -1.0, low), (1, 3, rp2, 1.0, high)):
                extra = face([near[c, t] for c in range(4)], plane(f1, t, side), faces[side], sign)
                units.append([part2[c, t, g] + place(extra[c]) for c in range(4)])
        changes = corrections(units, [1, 4] * 8, lhs, mask)
        for n, t in enumerate(pair):
            for side, g in ((0, 0), (1, 3)):
                for c in range(4):
                    smoothed[c, t, g] = f1[c, t, g] + changes[2 * n + side][c]

    arrive(5, 12)
    beside(range(8))

    units = [[ares[c, g] for c in range(4)] for g in range(4)]
    old = [e0[c, 0, 0:4] for c in range(3)]
    extra = face([lcor[c, 4:8] for c in range(4)], old, faces[0], -1.0)
    units[0] = [units[0][c] + low(extra[c]) for c in range(4)]
    old = [e0[c, 3, 4:8] for c in range(3)]
    extra = face([rcor[c, 0:4] for c in range(4)], old, faces[1], 1.0)
    units[3] = [units[3][c] + high(extra[c]) for c in range(4)]
    for g, change in enumerate(corrections(units, [1, 2, 3, 4], lhs, mask)):
        for c in range(3):
            e1[c, g] = e0[c, g] + change[c]

    middle((0,))
    sum_up(slice(1, 3))
    ends(range(8))

    for g in (0, 3):
        sum_up(slice(g, g + 1))
    for half in range(2):
        for side, rows, sign in ((0, slice(0, 4), 1.0), (1, slice(4, 8), -1.0)):
            near = [fields[half, c, 3 * side, rows] for c in range(4)]
            for c, value in enumerate(face(near, None, faces[side], sign)):
                edges[side, pl.ds(4 * half + c, 4, stride=8), :] = value

    core = lax.rem(tb, 2)

    def swap(source, target, n):
        return pltpu.make_async_remote_copy(
            source, target, pair_send.at[n], pair_recv.at[n], device_id=partner, device_id_type=MESH
        )

    swaps = [
        swap(edges.at[1 - core], edges_in, 0),
        swap(parts.at[pl.ds(pl.multiple_of(128 * (1 - core), 128), 128)], parts_in, 1),
    ]
    swaps[0].start()

    for half in range(2):
        now = [fields[half, c] for c in range(4)]
        base = [weighted_f[half, c] for c in range(4)]
        for c in range(3):
            base[c] = base[c] - mass[c] if half == 0 else base[c] + mass[c]
        resid = residual(now, nothing, nothing, base, coef[7], coef)
        for c in range(4):
            row = 4 * half + c
            for g in range(4):
                value = resid[c][g]
                if c < 3 and g == 0:
                    value = value - low(faces[0] * now[c][0, 0:4])
                if c < 3 and g == 3:
                    value = value - high(faces[1] * now[c][3, 4:8])
                parts[pl.ds(64 * g + row, 8, stride=8), :] = value

    swaps[1].start()

    def tile(ref, row):
        return ref.at[pl.ds(pl.multiple_of(row * 8, 8), 8)]

    pass_on(4)
    swaps[0].wait_recv()
    edge_sums[...] = edges[core] + edges_in[...]
    sends_left, sends_right = both(core == 0, has_left), both(core == 1, has_right)

    def edge_piece(y, device):
        return pltpu.make_async_remote_copy(
            edge_sums.at[pl.ds(8 * y, 8)], recv_e.at[tb // 2], esend_sem, erecv_sem,
            device_id=device, device_id_type=MESH,
        )

    @pl.when(sends_left)
    def _():
        for y in range(4):
            edge_piece(y, {"space": sx - 1, "tm": 28 + y}).start()

    @pl.when(sends_right)
    def _():
        for y in range(4):
            edge_piece(y, {"space": sx + 1, "tm": y}).start()

    swaps[1].wait_recv()
    sums[...] = parts[pl.ds(pl.multiple_of(128 * core, 128), 128), :] + parts_in[...]

    def send(step, carry):
        k = step // 2
        odd = lax.rem(k, 2)
        dz = 4 + (k // 2) * (1 - odd) - ((k + 1) // 2) * odd
        place = lax.rem(column // 2 * 2 + 2 * dz, 16) + lax.rem(step, 2)
        peer = 16 * core + place

        @pl.when(peer != tb)
        def _():
            pltpu.make_async_remote_copy(
                tile(sums, place), recv.at[tb // 2], psend_sem, precv_sem,
                device_id={"tm": peer}, device_id_type=MESH,
            ).start()

        return carry

    lax.fori_loop(0, 16, send, 0)
    keeps = tb // 16 == core

    @pl.when(keeps)
    def _():
        recv[tb // 2] = tile(sums, column)[...]

    for condition, _, copy in round_one:
        pl.when(condition)(copy.wait_send)

    for copy in swaps:
        copy.wait_send()

    @pl.when(jnp.logical_or(sends_left, sends_right))
    def _():
        pltpu.make_async_remote_copy(
            edge_sums, edge_sums, esend_sem, erecv_sem, device_id=partner, device_id_type=MESH
        ).wait_send()

    def settle(number):
        pieces = pltpu.make_async_remote_copy(
            recv.at[0:number], recv.at[0:number], psend_sem, precv_sem, device_id=partner, device_id_type=MESH
        )
        pieces.wait_send()
        pieces.wait_recv()

    pl.when(keeps)(lambda: settle(15))
    pl.when(jnp.logical_not(keeps))(lambda: settle(16))

    @pl.when(is_edge)
    def _():
        pltpu.make_async_remote_copy(
            recv_e, recv_e, psend_sem, erecv_sem, device_id=partner, device_id_type=MESH
        ).wait_recv()

    before = jnp.zeros((4, 128), F32)
    for k in range(8):
        block = (recv[2 * k] + recv[2 * k + 1]) + (recv_e[2 * k] + recv_e[2 * k + 1])
        level = block[0:4] + before
        before = block[4:8]
        for c in range(4):
            coarse[c, k : k + 1, :] = level[c : c + 1]


def store(smoothed_in, coarse_in, smoothed, coarse, sems):
    copies = [
        pltpu.make_async_copy(smoothed_in, smoothed, sems.at[0]),
        pltpu.make_async_copy(coarse_in, coarse, sems.at[1]),
    ]
    for copy in copies:
        copy.start()
    for copy in copies:
        copy.wait()


def per_device(initial_guess, forcing, visc_table, visc_class, inverse_bank, patch_kind):
    hbm = pl.BlockSpec(memory_space=pltpu.HBM)
    vmem = pl.BlockSpec(memory_space=pltpu.VMEM)
    dma = pltpu.SemaphoreType.DMA
    smoothed, coarse = pl.pallas_call(
        kernel,
        out_shape=(
            pltpu.VMEM((4, 8, 4, 8, 128), F32),
            pltpu.VMEM((4, 8, 128), F32),
        ),
        in_specs=[hbm] * 7,
        out_specs=(vmem, vmem),
        scratch_shapes=[
            pltpu.SMEM((8,), F32),
            pltpu.VMEM((4, 8, 128), jnp.int32),
            pltpu.VMEM((4, 32, 32), BF16),
            pltpu.VMEM((4, 2, 64), jnp.int32),
            pltpu.VMEM((4, 8, 4, 8, 128), F32),
            pltpu.VMEM((4, 8, 4, 8, 128), F32),
            pltpu.VMEM((4, 8, 4, 8, 128), F32),
            pltpu.VMEM((4, 8, 4, 8, 128), F32),
            pltpu.VMEM((4, 8, 4, 8, 128), F32),
            pltpu.VMEM((3, 4, 8, 128), F32),
            pltpu.VMEM((3, 4, 8, 128), F32),
            pltpu.VMEM((4, 8, 4, 128), F32),
            pltpu.VMEM((4, 8, 4, 128), F32),
            pltpu.VMEM((4, 8, 4, 128), F32),
            pltpu.VMEM((4, 8, 4, 128), F32),
            pltpu.VMEM((4, 8, 8, 128), F32),
            pltpu.VMEM((4, 8, 8, 128), F32),
            pltpu.VMEM((4, 4, 8, 128), F32),
            pltpu.VMEM((4, 8, 128), F32),
            pltpu.VMEM((4, 8, 128), F32),
            pltpu.VMEM((2, 16, 128), F32),
            pltpu.VMEM((2, 16, 128), F32),
            pltpu.VMEM((2, 4, 128), F32),
            pltpu.VMEM((2, 4, 4, 8, 128), F32),
            pltpu.VMEM((4, 4, 8, 128), F32),
            pltpu.VMEM((8, 4, 8, 128), F32),
            pltpu.VMEM((64, 256), BF16),
            pltpu.VMEM((6, 4, 16, 128), BF16),
            pltpu.VMEM((2, 4, 4, 8, 128), F32),
            pltpu.VMEM((256, 128), F32),
            pltpu.VMEM((2, 32, 128), F32),
            pltpu.VMEM((128, 128), F32),
            pltpu.VMEM((32, 128), F32),
            pltpu.VMEM((128, 128), F32),
            pltpu.VMEM((32, 128), F32),
            pltpu.VMEM((16, 8, 128), F32),
            pltpu.VMEM((16, 8, 128), F32),
            dma((6,)),
            dma((12,)),
            dma((12,)),
            dma,
            dma,
            dma,
            dma,
            pltpu.SemaphoreType.REGULAR((5,)),
            dma((2,)),
            dma((2,)),
        ],
        compiler_params=pltpu.CompilerParams(
            collective_id=0, has_side_effects=True, vmem_limit_bytes=60 * 1024 * 1024
        ),
    )(
        initial_guess,
        initial_guess.reshape(4, 8, 4, 8, 128),
        forcing.reshape(4, 8, 4, 8, 128),
        visc_table,
        visc_class.reshape(4, 8, 128),
        inverse_bank,
        patch_kind,
    )
    smoothed, coarse = pl.pallas_call(
        store,
        out_shape=(
            jax.ShapeDtypeStruct((4, 8, 4, 8, 128), F32),
            jax.ShapeDtypeStruct((4, 8, 128), F32),
        ),
        in_specs=[pl.BlockSpec(memory_space=pl.ANY)] * 2,
        out_specs=(pl.BlockSpec(memory_space=pl.ANY),) * 2,
        scratch_shapes=[dma((2,))],
        compiler_params=pltpu.CompilerParams(vmem_limit_bytes=4 * 1024 * 1024),
    )(smoothed, coarse)
    return smoothed.reshape(4, 8, 8, 4, 128), coarse


def solution(mesh):
    return jax.shard_map(
        per_device,
        mesh=mesh,
        in_specs=(
            P(None, "tm", "space", None, None),
            P(None, "tm", "space", None, None),
            P(),
            P("space", None, None),
            P(),
            P("space", None, None),
        ),
        out_specs=(P(None, "tm", "space", None, None), P(None, None, ("space", "tm"))),
        check_vma=False,
    )
```

```python
import functools

import jax
import jax.numpy as jnp
from jax import lax
from jax.experimental import pallas as pl
from jax.experimental.pallas import tpu as pltpu
from jax.sharding import PartitionSpec as P

MESH = pl.DeviceIdType.MESH
F32 = jnp.float32
BF16 = jnp.bfloat16
DAMPING = 0.8
STABILIZE = 0.1


def iota(shape, dim):
    return lax.broadcasted_iota(jnp.int32, shape, dim)


def cell_index(q):
    return (q // 8) * 8 + (q // 4 % 2) * 4 + (q % 2) * 2


def build_bank(bank_ref, lhs_ref):
    j = iota((32, 64), 0)
    q = iota((32, 64), 1)
    spread = (j == cell_index(q % 32) + q // 32).astype(BF16)
    p = iota((64, 32), 0)
    i = iota((64, 32), 1)
    gather = (i == cell_index(p % 32) + p // 32).astype(BF16)
    same = (iota((64, 64), 0) // 2 % 2) == (iota((64, 64), 1) // 2 % 2)
    wide = jnp.dot(bank_ref[...].reshape(128, 32), spread, preferred_element_type=F32).astype(BF16)
    parts = []
    for kind in range(4):
        part = jnp.dot(gather, wide[32 * kind : 32 * kind + 32], preferred_element_type=F32)
        parts.append(jnp.where(same, part, 0.0).astype(BF16))
    lhs_ref[...] = jnp.concatenate(parts, axis=1)


def kind_maps(kind_ref):
    upper = iota((8, 64), 0) // 2 % 2 == 0
    double = (iota((64, 128), 0) == iota((64, 128), 1) // 2).astype(BF16)
    maps = []
    for g in range(4):
        pair = kind_ref[g].astype(F32)
        rows = jnp.where(upper, pair[0:1], pair[1:2]).astype(BF16)
        maps.append(jnp.dot(rows, double, preferred_element_type=F32))
    return maps


def store_mask(kinds, mask_ref, at):
    for kind in range(4):
        mask = (kinds == float(kind)).astype(F32)
        mask_ref[at, kind] = jnp.concatenate([mask, mask], axis=0).astype(BF16)


def shift_x(values, left, right):
    first = jnp.concatenate([left, values[0, 0:4]], axis=0)
    last = jnp.concatenate([values[3, 4:8], right], axis=0)
    low = iota((3, 8, 128), 1) < 4
    inner = pltpu.roll(jnp.where(low, values[1:4], values[0:3]), 4, 1)
    return (
        jnp.concatenate([first[None], inner], axis=0),
        jnp.concatenate([inner, last[None]], axis=0),
    )


def shifts_yz(values):
    return (
        pltpu.roll(values, 1, 1),
        pltpu.roll(values, 7, 1),
        pltpu.roll(values, 1, 2),
        pltpu.roll(values, 127, 2),
    )


def edge_masks():
    y = iota((4, 8, 128), 1) % 4
    z = iota((4, 8, 128), 2)
    return y != 0, y != 3, z != 0, z != 127


def build_coefficients(viscosity, coef_ref):
    none = jnp.zeros((4, 128), F32)
    xm, xp = shift_x(viscosity, none, none)
    ym, yp, zm, zp = shifts_yz(viscosity)
    g, row = iota((4, 8, 128), 0), iota((4, 8, 128), 1)
    has_xm = jnp.logical_or(g > 0, row >= 4)
    has_xp = jnp.logical_or(g < 3, row < 4)
    total = jnp.zeros_like(viscosity)
    for n, (near, mask) in enumerate(zip((xm, xp, ym, yp, zm, zp), (has_xm, has_xp) + edge_masks())):
        near = jnp.where(mask, near, 0.0)
        kappa = 0.5 * (viscosity + near)
        inner = jnp.where(mask, kappa, 0.0)
        total = total + (inner if n < 2 else kappa)
        coef_ref[1 + n] = inner
    coef_ref[0] = total + 1.0
    coef_ref[7] = total


def residual(now, left, right, base, diagonal, coef_ref):
    mym, myp, mzm, mzp = edge_masks()
    pressure = now[3]
    pxm, pxp = shift_x(pressure, left[3], right[3])
    pym, pyp, pzm, pzp = shifts_yz(pressure)
    pym = jnp.where(mym, pym, 0.0)
    pyp = jnp.where(myp, pyp, 0.0)
    pzm = jnp.where(mzm, pzm, 0.0)
    pzp = jnp.where(mzp, pzp, 0.0)
    gradients = (pxp - pxm, pyp - pym, pzp - pzm)
    out = []
    divergence = None
    for c in range(3):
        value = now[c]
        xm, xp = shift_x(value, left[c], right[c])
        ym, yp, zm, zp = shifts_yz(value)
        flow = coef_ref[1] * xm + coef_ref[2] * xp
        flow = flow + (coef_ref[3] * ym + coef_ref[4] * yp)
        flow = flow + (coef_ref[5] * zm + coef_ref[6] * zp)
        out.append(base[c] - diagonal * value + flow - 0.5 * gradients[c])
        if c == 0:
            divergence = xp - xm
        elif c == 1:
            divergence = divergence + (jnp.where(myp, yp, 0.0) - jnp.where(mym, ym, 0.0))
        else:
            divergence = divergence + (jnp.where(mzp, zp, 0.0) - jnp.where(mzm, zm, 0.0))
    around = (pxm + pxp) + (pym + pyp) + (pzm + pzp)
    out.append(base[3] - STABILIZE * (6.0 * pressure - around) + 0.5 * divergence)
    return out


def face(near, own, kappa, sign):
    out = []
    for c in range(3):
        out.append(kappa * (near[c] if own is None else near[c] - own[c]))
    out[0] = out[0] - (0.5 * sign) * near[3]
    out.append(STABILIZE * near[3] + (0.5 * sign) * near[0])
    return out


def low(rows):
    return jnp.concatenate([rows, jnp.zeros((4, 128), F32)], axis=0)


def high(rows):
    return jnp.concatenate([jnp.zeros((4, 128), F32), rows], axis=0)


def corrections(units, at, lhs_ref, mask_ref):
    even = iota((8, 128), 1) % 2 == 0
    columns = []
    for unit, place in zip(units, at):
        evens = [jnp.where(even, v, pltpu.roll(v, 1, 1)) for v in unit]
        odds = [jnp.where(even, pltpu.roll(v, 127, 1), v) for v in unit]
        stack = jnp.concatenate(evens + odds, axis=0).astype(BF16).reshape(4, 16, 128)
        masked = [(stack * mask_ref[place, kind]).reshape(64, 128) for kind in range(4)]
        columns.append(jnp.concatenate(masked, axis=0))
    product = jnp.dot(
        lhs_ref[...], jnp.concatenate(columns, axis=1), preferred_element_type=F32
    )
    out = []
    for n in range(len(units)):
        across = slice(128 * n, 128 * n + 128)
        out.append(
            [
                DAMPING
                * jnp.where(even, product[8 * c : 8 * c + 8, across], product[32 + 8 * c : 40 + 8 * c, across])
                for c in range(4)
            ]
        )
    return out


def time_sums(load):
    plain = load(0)
    ramp = None
    for t in range(1, 8):
        value = load(t)
        plain = plain + value
        ramp = value * float(t) if ramp is None else ramp + value * float(t)
    return plain, ramp


def steps(body):
    def several(i, carry):
        for j in range(4):
            body(4 * i + j, i, j)
        return carry

    lax.fori_loop(0, 2, several, 0)


def kernel(
    init5, init, forc, table_in, vclass_in, bank_in, kind_in,
    smoothed, coarse, table, vclass, bank, kind,
    f0, f1, forcing, part, part2, e0, e1, lp, rp, lp2, rp2, lres, rres, ares, lcor, rcor, vk_out, vk_in,
    faces, fields, mass, coef, lhs, mask, weighted_f, parts, edges, parts_in, sums, recv, recv_e,
    load_sem, send_sem, recv_sem, psend_sem, precv_sem, esend_sem, erecv_sem, token_sem, pair_send, pair_recv,
):
    sx = lax.axis_index("space")
    tb = lax.axis_index("tm")
    has_left, has_right = sx > 0, sx < 7
    has_before, has_after = tb > 0, tb < 31
    is_edge = jnp.logical_or(jnp.logical_and(tb < 4, has_left), jnp.logical_and(tb >= 28, has_right))
    to_left, to_right, to_after = {"space": sx - 1}, {"space": sx + 1}, {"tm": tb + 1}
    left_after, right_after = {"space": sx - 1, "tm": tb + 1}, {"space": sx + 1, "tm": tb + 1}
    both = jnp.logical_and

    barrier = pltpu.get_barrier_semaphore()

    def greet(condition, device):
        @pl.when(condition)
        def _():
            pl.semaphore_signal(barrier, inc=1, device_id=device, device_id_type=MESH)

    column, row = lax.rem(tb, 16), tb // 16
    ring = [{"tm": row * 16 + lax.rem(column + step, 16)} for step in (2, 14, 4, 12)]
    far_ring = ring[2:]
    across = {"tm": lax.rem(tb + 16, 32)}
    partner = {"tm": tb + 1 - 2 * lax.rem(tb, 2)}
    greet(has_left, to_left)
    greet(has_right, to_right)
    greet(has_before, {"tm": tb - 1})
    greet(has_after, to_after)
    for device in ring + [across]:
        greet(True, device)

    def tell(n, devices):
        for condition, device in devices:

            @pl.when(condition)
            def _(device=device):
                pl.semaphore_signal(token_sem.at[n], inc=1, device_id=device, device_id_type=MESH)

    circles = [
        [(True, partner)],
        [(True, device) for device in ring],
        [(True, device) for device in far_ring],
        [(True, across)],
    ]
    counts = [1, 4, 2, 1]

    def pass_on(n):
        if n > 0:
            pl.semaphore_wait(token_sem.at[n - 1], counts[n - 1])
        if n < 4:
            tell(n, circles[n])

    loads = [
        pltpu.make_async_copy(table_in, table, load_sem.at[0]),
        pltpu.make_async_copy(vclass_in, vclass, load_sem.at[1]),
        pltpu.make_async_copy(kind_in, kind, load_sem.at[2]),
        pltpu.make_async_copy(init, f0, load_sem.at[3]),
        pltpu.make_async_copy(forc, forcing, load_sem.at[4]),
        pltpu.make_async_copy(bank_in, bank, load_sem.at[5]),
    ]
    for copy in loads:
        copy.start()

    @pl.when(sx == 0)
    def _():
        vk_in[0] = jnp.zeros((16, 128), F32)
        lp[...] = jnp.zeros_like(lp)
        lres[...] = jnp.zeros_like(lres)

    @pl.when(sx == 7)
    def _():
        vk_in[1] = jnp.zeros((16, 128), F32)
        rp[...] = jnp.zeros_like(rp)
        rres[...] = jnp.zeros_like(rres)

    @pl.when(tb == 0)
    def _():
        e0[...] = jnp.zeros_like(e0)
        ares[...] = jnp.zeros_like(ares)

    @pl.when(jnp.logical_or(tb == 0, sx == 0))
    def _():
        lcor[...] = jnp.zeros_like(lcor)

    @pl.when(jnp.logical_or(tb == 0, sx == 7))
    def _():
        rcor[...] = jnp.zeros_like(rcor)

    @pl.when(jnp.logical_not(is_edge))
    def _():
        recv_e[...] = jnp.zeros_like(recv_e)

    one = lambda condition: condition.astype(jnp.int32)
    pl.semaphore_wait(
        barrier,
        5 + one(has_left) + one(has_right) + one(has_before) + one(has_after),
    )

    def remote(condition, awaited, source, target, n, device):
        copy = pltpu.make_async_remote_copy(
            source, target, send_sem.at[n], recv_sem.at[n], device_id=device, device_id_type=MESH
        )
        return condition, awaited, copy

    round_one = [
        remote(has_left, has_right, vk_out.at[0], vk_in.at[1], 0, to_left),
        remote(has_right, has_left, vk_out.at[1], vk_in.at[0], 1, to_right),
        remote(has_left, has_right, init5.at[:, :, 0], rp, 2, to_left),
        remote(has_right, has_left, init5.at[:, :, 7], lp, 3, to_right),
        remote(has_after, has_before, init.at[0:3, 7], e0, 4, to_after),
        remote(has_after, has_before, part.at[:, 7], ares, 5, to_after),
        remote(both(has_left, has_after), both(has_right, has_before), init.at[:, 7, 0], rcor, 6, left_after),
        remote(both(has_right, has_after), both(has_left, has_before), init.at[:, 7, 3], lcor, 7, right_after),
    ]
    for i in range(2):
        pair = slice(4 * i, 4 * i + 4)
        round_one += [
            remote(has_left, has_right, part.at[:, pair, 0], rres.at[:, pair], 8 + 2 * i, to_left),
            remote(has_right, has_left, part.at[:, pair, 3], lres.at[:, pair], 9 + 2 * i, to_right),
        ]
    def begin(*places):
        for place in places:
            condition, _, copy = round_one[place]
            pl.when(condition)(copy.start)

    begin(2, 3, 4)
    tell(4, [(has_before, {"tm": tb - 1})])
    pass_on(0)

    loads[0].wait()
    loads[1].wait()
    viscosity = jnp.zeros((4, 8, 128), F32)
    for label in range(8):
        viscosity = jnp.where(vclass[...] == label, table[label], viscosity)
    build_coefficients(viscosity, coef)
    loads[2].wait()
    maps = kind_maps(kind)
    vk_out[0, 0:4] = viscosity[0, 0:4]
    vk_out[1, 0:4] = viscosity[3, 4:8]
    vk_out[0, 4:8] = jnp.zeros((4, 128), F32)
    vk_out[1, 4:8] = jnp.zeros((4, 128), F32)
    vk_out[0, 8:16] = maps[0]
    vk_out[1, 8:16] = maps[3]
    begin(0, 1)
    for g in range(4):
        store_mask(maps[g], mask, g + 1)
    loads[3].wait()
    loads[4].wait()

    nothing = [jnp.zeros((4, 128), F32)] * 4

    def local(t):
        now = [f0[c, t] for c in range(4)]
        base = [forcing[c, t] for c in range(4)]
        if t > 0:
            base = [base[c] + f0[c, t - 1] for c in range(3)] + base[3:]
        for c, value in enumerate(residual(now, nothing, nothing, base, coef[0], coef)):
            part[c, t] = value

    for t in range(4):
        local(t)
    begin(8, 9)
    for t in range(4, 8):
        local(t)
    @pl.when(has_after)
    def _():
        pl.semaphore_wait(token_sem.at[4], 1)
        begin(6, 7)

    begin(10, 11, 5)

    def arrive(first, last):
        for _, awaited, copy in round_one[first:last]:
            pl.when(awaited)(copy.wait_recv)

    loads[5].wait()
    build_bank(bank, lhs)
    pass_on(1)

    first = (lax.rem(tb, 4) * 8).astype(F32) * (1.0 / 1024.0)

    def weigh(plain, ramp):
        far = first * plain + ramp * (1.0 / 1024.0)
        return plain * (1.0 / 32.0) - far, far

    for c in range(4):
        near, far = weigh(*time_sums(lambda t, c=c: forcing[c, t]))
        weighted_f[0, c] = near
        weighted_f[1, c] = far


    for pair in ((1, 2), (3, 4), (5, 6), (7,)):
        where = [(t, g) for t in pair for g in (1, 2)]
        units = [[part[c, t, g] for c in range(4)] for t, g in where]
        for (t, g), change in zip(where, corrections(units, [g + 1 for _, g in where], lhs, mask)):
            for c in range(4):
                f1[c, t, g] = f0[c, t, g] + change[c]

    pass_on(2)
    arrive(0, 2)
    faces[0] = 0.5 * (viscosity[0, 0:4] + vk_in[0, 0:4])
    faces[1] = 0.5 * (viscosity[3, 4:8] + vk_in[1, 0:4])
    store_mask(vk_in[0, 8:16], mask, 0)
    store_mask(vk_in[1, 8:16], mask, 5)
    arrive(2, 5)
    pass_on(3)

    units = [[part[c, 0, g] + (e0[c, g] if c < 3 else 0.0) for c in range(4)] for g in (1, 2)]
    for g, change in zip((1, 2), corrections(units, [2, 3], lhs, mask)):
        for c in range(4):
            f1[c, 0, g] = f0[c, 0, g] + change[c]

    def plane(ref, t, side):
        if side == 0:
            return [ref[c, t, 0, 0:4] for c in range(4)]
        return [ref[c, t, 3, 4:8] for c in range(4)]

    def outer(t, i, j):
        units = []
        for side, g, near, sign, place in ((0, 0, lp, -1.0, low), (1, 3, rp, 1.0, high)):
            extra = face([near[c, t] for c in range(4)], plane(f0, t, side), faces[side], sign)
            unit = [part[c, t, g] + place(extra[c]) for c in range(4)]
            if j == 0:
                unit = [unit[c] + jnp.where(i == 0, e0[c, g], 0.0) for c in range(3)] + unit[3:]
            units.append(unit)
        for g, change in zip((0, 3), corrections(units, [1, 4], lhs, mask)):
            for c in range(4):
                f1[c, t, g] = f0[c, t, g] + change[c]

    steps(outer)


    def middle(pair):
        units = []
        for t in pair:
            now = [f1[c, t] for c in range(4)]
            base = [forcing[c, t] for c in range(4)]
            for c in range(3):
                base[c] = base[c] + (f1[c, t - 1] if t > 0 else e1[c])
            resid = residual(now, nothing, nothing, base, coef[0], coef)
            for c in range(4):
                part2[c, t] = resid[c]
            units += [[resid[c][g] for c in range(4)] for g in (1, 2)]
        changes = corrections(units, [2, 3] * len(pair), lhs, mask)
        for n, t in enumerate(pair):
            for g in (1, 2):
                for c in range(4):
                    smoothed[c, t, g] = f1[c, t, g] + changes[2 * n + g - 1][c]

    middle((1, 2, 3))
    middle((4, 5, 6, 7))


    def sum_up(rows):
        for c in range(4):
            plain, ramp = time_sums(lambda t: smoothed[c, t, rows])
            near, far = weigh(plain, ramp)
            fields[0, c, rows] = near
            fields[1, c, rows] = far
            mass[c, rows] = plain * (1.0 / 1024.0)

    def beside(pair):
        units = []
        for t in pair:
            extra = face(plane(f0, t, 0), [lp[c, t] for c in range(4)], faces[0], 1.0)
            unit = [lres[c, t] + high(extra[c]) for c in range(4)]
            if t == 0:
                unit = [unit[c] + lcor[c] for c in range(3)] + unit[3:]
            units.append(unit)
            extra = face(plane(f0, t, 1), [rp[c, t] for c in range(4)], faces[1], -1.0)
            unit = [rres[c, t] + low(extra[c]) for c in range(4)]
            if t == 0:
                unit = [unit[c] + rcor[c] for c in range(3)] + unit[3:]
            units.append(unit)
        changes = corrections(units, [0, 5] * 8, lhs, mask)
        for n, t in enumerate(pair):
            for c in range(4):
                lp2[c, t] = jnp.where(has_left, lp[c, t] + changes[2 * n][c][4:8], 0.0)
                rp2[c, t] = jnp.where(has_right, rp[c, t] + changes[2 * n + 1][c][0:4], 0.0)

    def ends(pair):
        units = []
        for t in pair:
            for side, g, near, sign, place in ((0, 0, lp2, -1.0, low), (1, 3, rp2, 1.0, high)):
                extra = face([near[c, t] for c in range(4)], plane(f1, t, side), faces[side], sign)
                units.append([part2[c, t, g] + place(extra[c]) for c in range(4)])
        changes = corrections(units, [1, 4] * 8, lhs, mask)
        for n, t in enumerate(pair):
            for side, g in ((0, 0), (1, 3)):
                for c in range(4):
                    smoothed[c, t, g] = f1[c, t, g] + changes[2 * n + side][c]

    arrive(5, 12)
    beside(range(8))

    units = [[ares[c, g] for c in range(4)] for g in range(4)]
    old = [e0[c, 0, 0:4] for c in range(3)]
    extra = face([lcor[c, 4:8] for c in range(4)], old, faces[0], -1.0)
    units[0] = [units[0][c] + low(extra[c]) for c in range(4)]
    old = [e0[c, 3, 4:8] for c in range(3)]
    extra = face([rcor[c, 0:4] for c in range(4)], old, faces[1], 1.0)
    units[3] = [units[3][c] + high(extra[c]) for c in range(4)]
    for g, change in enumerate(corrections(units, [1, 2, 3, 4], lhs, mask)):
        for c in range(3):
            e1[c, g] = e0[c, g] + change[c]

    middle((0,))
    sum_up(slice(1, 3))
    ends(range(8))

    for g in (0, 3):
        sum_up(slice(g, g + 1))
    for half in range(2):
        for side, rows, sign in ((0, slice(0, 4), 1.0), (1, slice(4, 8), -1.0)):
            near = [fields[half, c, 3 * side, rows] for c in range(4)]
            for c, value in enumerate(face(near, None, faces[side], sign)):
                edges[side, pl.ds(4 * half + c, 4, stride=8), :] = value

    def edge_piece(side, y, device):
        return pltpu.make_async_remote_copy(
            edges.at[side, pl.ds(8 * y, 8)], recv_e.at[tb], esend_sem.at[side], erecv_sem,
            device_id=device, device_id_type=MESH,
        )

    pass_on(4)

    @pl.when(has_left)
    def _():
        for y in range(4):
            edge_piece(0, y, {"space": sx - 1, "tm": 28 + y}).start()

    @pl.when(has_right)
    def _():
        for y in range(4):
            edge_piece(1, y, {"space": sx + 1, "tm": y}).start()

    for half in range(2):
        now = [fields[half, c] for c in range(4)]
        base = [weighted_f[half, c] for c in range(4)]
        for c in range(3):
            base[c] = base[c] - mass[c] if half == 0 else base[c] + mass[c]
        resid = residual(now, nothing, nothing, base, coef[7], coef)
        for c in range(4):
            row = 4 * half + c
            for g in range(4):
                value = resid[c][g]
                if c < 3 and g == 0:
                    value = value - low(faces[0] * now[c][0, 0:4])
                if c < 3 and g == 3:
                    value = value - high(faces[1] * now[c][3, 4:8])
                parts[pl.ds(64 * g + row, 8, stride=8), :] = value

    core = lax.rem(tb, 2)
    swap = pltpu.make_async_remote_copy(
        parts.at[pl.ds(pl.multiple_of(128 * (1 - core), 128), 128)], parts_in, pair_send, pair_recv,
        device_id=partner, device_id_type=MESH,
    )
    swap.start()

    def tile(ref, row):
        return ref.at[pl.ds(pl.multiple_of(row * 8, 8), 8)]

    swap.wait_recv()
    sums[...] = parts[pl.ds(pl.multiple_of(128 * core, 128), 128), :] + parts_in[...]

    def send(step, carry, hot):
        k = step // 2
        odd = lax.rem(k, 2)
        dz = 4 + (k // 2) * (1 - odd) - ((k + 1) // 2) * odd
        place = lax.rem(column // 2 * 2 + 2 * dz, 16) + lax.rem(step, 2)
        peer = 16 * core + place

        is_hot = jnp.logical_or(peer < 4, peer >= 28)

        @pl.when(both(peer != tb, is_hot if hot else jnp.logical_not(is_hot)))
        def _():
            pltpu.make_async_remote_copy(
                tile(sums, place), recv.at[tb // 2], psend_sem, precv_sem,
                device_id={"tm": peer}, device_id_type=MESH,
            ).start()

        return carry

    lax.fori_loop(0, 16, functools.partial(send, hot=True), 0)
    lax.fori_loop(0, 16, functools.partial(send, hot=False), 0)
    keeps = tb // 16 == core

    @pl.when(keeps)
    def _():
        recv[tb // 2] = tile(sums, column)[...]

    for condition, _, copy in round_one:
        pl.when(condition)(copy.wait_send)

    swap.wait_send()

    def sent_edges(side):
        pltpu.make_async_remote_copy(
            edges.at[side], edges.at[side], esend_sem.at[side], erecv_sem, device_id=partner, device_id_type=MESH
        ).wait_send()

    pl.when(has_left)(lambda: sent_edges(0))
    pl.when(has_right)(lambda: sent_edges(1))

    def settle(number):
        pieces = pltpu.make_async_remote_copy(
            recv.at[0:number], recv.at[0:number], psend_sem, precv_sem, device_id=partner, device_id_type=MESH
        )
        pieces.wait_send()
        pieces.wait_recv()

    pl.when(keeps)(lambda: settle(15))
    pl.when(jnp.logical_not(keeps))(lambda: settle(16))

    @pl.when(is_edge)
    def _():
        pltpu.make_async_remote_copy(
            recv_e, recv_e, psend_sem, erecv_sem, device_id=partner, device_id_type=MESH
        ).wait_recv()

    before = jnp.zeros((4, 128), F32)
    for k in range(8):
        block = recv[2 * k] + recv[2 * k + 1]
        block = block + (
            (recv_e[4 * k] + recv_e[4 * k + 1]) + (recv_e[4 * k + 2] + recv_e[4 * k + 3])
        )
        level = block[0:4] + before
        before = block[4:8]
        for c in range(4):
            coarse[c, k : k + 1, :] = level[c : c + 1]


def store(smoothed_in, coarse_in, smoothed, coarse, sems):
    copies = [
        pltpu.make_async_copy(smoothed_in, smoothed, sems.at[0]),
        pltpu.make_async_copy(coarse_in, coarse, sems.at[1]),
    ]
    for copy in copies:
        copy.start()
    for copy in copies:
        copy.wait()


def per_device(initial_guess, forcing, visc_table, visc_class, inverse_bank, patch_kind):
    hbm = pl.BlockSpec(memory_space=pltpu.HBM)
    vmem = pl.BlockSpec(memory_space=pltpu.VMEM)
    dma = pltpu.SemaphoreType.DMA
    smoothed, coarse = pl.pallas_call(
        kernel,
        out_shape=(
            pltpu.VMEM((4, 8, 4, 8, 128), F32),
            pltpu.VMEM((4, 8, 128), F32),
        ),
        in_specs=[hbm] * 7,
        out_specs=(vmem, vmem),
        scratch_shapes=[
            pltpu.SMEM((8,), F32),
            pltpu.VMEM((4, 8, 128), jnp.int32),
            pltpu.VMEM((4, 32, 32), BF16),
            pltpu.VMEM((4, 2, 64), jnp.int32),
            pltpu.VMEM((4, 8, 4, 8, 128), F32),
            pltpu.VMEM((4, 8, 4, 8, 128), F32),
            pltpu.VMEM((4, 8, 4, 8, 128), F32),
            pltpu.VMEM((4, 8, 4, 8, 128), F32),
            pltpu.VMEM((4, 8, 4, 8, 128), F32),
            pltpu.VMEM((3, 4, 8, 128), F32),
            pltpu.VMEM((3, 4, 8, 128), F32),
            pltpu.VMEM((4, 8, 4, 128), F32),
            pltpu.VMEM((4, 8, 4, 128), F32),
            pltpu.VMEM((4, 8, 4, 128), F32),
            pltpu.VMEM((4, 8, 4, 128), F32),
            pltpu.VMEM((4, 8, 8, 128), F32),
            pltpu.VMEM((4, 8, 8, 128), F32),
            pltpu.VMEM((4, 4, 8, 128), F32),
            pltpu.VMEM((4, 8, 128), F32),
            pltpu.VMEM((4, 8, 128), F32),
            pltpu.VMEM((2, 16, 128), F32),
            pltpu.VMEM((2, 16, 128), F32),
            pltpu.VMEM((2, 4, 128), F32),
            pltpu.VMEM((2, 4, 4, 8, 128), F32),
            pltpu.VMEM((4, 4, 8, 128), F32),
            pltpu.VMEM((8, 4, 8, 128), F32),
            pltpu.VMEM((64, 256), BF16),
            pltpu.VMEM((6, 4, 16, 128), BF16),
            pltpu.VMEM((2, 4, 4, 8, 128), F32),
            pltpu.VMEM((256, 128), F32),
            pltpu.VMEM((2, 32, 128), F32),
            pltpu.VMEM((128, 128), F32),
            pltpu.VMEM((128, 128), F32),
            pltpu.VMEM((16, 8, 128), F32),
            pltpu.VMEM((32, 8, 128), F32),
            dma((6,)),
            dma((12,)),
            dma((12,)),
            dma,
            dma,
            dma((2,)),
            dma,
            pltpu.SemaphoreType.REGULAR((5,)),
            dma,
            dma,
        ],
        compiler_params=pltpu.CompilerParams(
            collective_id=0, has_side_effects=True, vmem_limit_bytes=60 * 1024 * 1024
        ),
    )(
        initial_guess,
        initial_guess.reshape(4, 8, 4, 8, 128),
        forcing.reshape(4, 8, 4, 8, 128),
        visc_table,
        visc_class.reshape(4, 8, 128),
        inverse_bank,
        patch_kind,
    )
    smoothed, coarse = pl.pallas_call(
        store,
        out_shape=(
            jax.ShapeDtypeStruct((4, 8, 4, 8, 128), F32),
            jax.ShapeDtypeStruct((4, 8, 128), F32),
        ),
        in_specs=[pl.BlockSpec(memory_space=pl.ANY)] * 2,
        out_specs=(pl.BlockSpec(memory_space=pl.ANY),) * 2,
        scratch_shapes=[dma((2,))],
        compiler_params=pltpu.CompilerParams(vmem_limit_bytes=4 * 1024 * 1024),
    )(smoothed, coarse)
    return smoothed.reshape(4, 8, 8, 4, 128), coarse


def solution(mesh):
    return jax.shard_map(
        per_device,
        mesh=mesh,
        in_specs=(
            P(None, "tm", "space", None, None),
            P(None, "tm", "space", None, None),
            P(),
            P("space", None, None),
            P(),
            P("space", None, None),
        ),
        out_specs=(P(None, "tm", "space", None, None), P(None, None, ("space", "tm"))),
        check_vma=False,
    )
```

```python
import functools

import jax
import jax.numpy as jnp
from jax import lax
from jax.experimental import pallas as pl
from jax.experimental.pallas import tpu as pltpu
from jax.sharding import PartitionSpec as P

MESH = pl.DeviceIdType.MESH
F32 = jnp.float32
BF16 = jnp.bfloat16
DAMPING = 0.8
STABILIZE = 0.1


def iota(shape, dim):
    return lax.broadcasted_iota(jnp.int32, shape, dim)


def cell_index(q):
    return (q // 8) * 8 + (q // 4 % 2) * 4 + (q % 2) * 2


def build_bank(bank_ref, lhs_ref):
    j = iota((32, 64), 0)
    q = iota((32, 64), 1)
    spread = (j == cell_index(q % 32) + q // 32).astype(BF16)
    p = iota((64, 32), 0)
    i = iota((64, 32), 1)
    gather = (i == cell_index(p % 32) + p // 32).astype(BF16)
    same = (iota((64, 64), 0) // 2 % 2) == (iota((64, 64), 1) // 2 % 2)
    wide = jnp.dot(bank_ref[...].reshape(128, 32), spread, preferred_element_type=F32).astype(BF16)
    parts = []
    for kind in range(4):
        part = jnp.dot(gather, wide[32 * kind : 32 * kind + 32], preferred_element_type=F32)
        parts.append(jnp.where(same, part, 0.0).astype(BF16))
    lhs_ref[...] = jnp.concatenate(parts, axis=1)


def kind_maps(kind_ref):
    upper = iota((8, 64), 0) // 2 % 2 == 0
    double = (iota((64, 128), 0) == iota((64, 128), 1) // 2).astype(BF16)
    maps = []
    for g in range(4):
        pair = kind_ref[g].astype(F32)
        rows = jnp.where(upper, pair[0:1], pair[1:2]).astype(BF16)
        maps.append(jnp.dot(rows, double, preferred_element_type=F32))
    return maps


def store_mask(kinds, mask_ref, at):
    for kind in range(4):
        mask = (kinds == float(kind)).astype(F32)
        mask_ref[at, kind] = jnp.concatenate([mask, mask], axis=0).astype(BF16)


def shift_x(values, left, right):
    first = jnp.concatenate([left, values[0, 0:4]], axis=0)
    last = jnp.concatenate([values[3, 4:8], right], axis=0)
    low = iota((3, 8, 128), 1) < 4
    inner = pltpu.roll(jnp.where(low, values[1:4], values[0:3]), 4, 1)
    return (
        jnp.concatenate([first[None], inner], axis=0),
        jnp.concatenate([inner, last[None]], axis=0),
    )


def shifts_yz(values):
    return (
        pltpu.roll(values, 1, 1),
        pltpu.roll(values, 7, 1),
        pltpu.roll(values, 1, 2),
        pltpu.roll(values, 127, 2),
    )


def edge_masks():
    y = iota((4, 8, 128), 1) % 4
    z = iota((4, 8, 128), 2)
    return y != 0, y != 3, z != 0, z != 127


def build_coefficients(viscosity, coef_ref):
    none = jnp.zeros((4, 128), F32)
    xm, xp = shift_x(viscosity, none, none)
    ym, yp, zm, zp = shifts_yz(viscosity)
    g, row = iota((4, 8, 128), 0), iota((4, 8, 128), 1)
    has_xm = jnp.logical_or(g > 0, row >= 4)
    has_xp = jnp.logical_or(g < 3, row < 4)
    total = jnp.zeros_like(viscosity)
    for n, (near, mask) in enumerate(zip((xm, xp, ym, yp, zm, zp), (has_xm, has_xp) + edge_masks())):
        near = jnp.where(mask, near, 0.0)
        kappa = 0.5 * (viscosity + near)
        inner = jnp.where(mask, kappa, 0.0)
        total = total + (inner if n < 2 else kappa)
        coef_ref[1 + n] = inner
    coef_ref[0] = total + 1.0
    coef_ref[7] = total


def residual(now, left, right, base, diagonal, coef_ref):
    mym, myp, mzm, mzp = edge_masks()
    pressure = now[3]
    pxm, pxp = shift_x(pressure, left[3], right[3])
    pym, pyp, pzm, pzp = shifts_yz(pressure)
    pym = jnp.where(mym, pym, 0.0)
    pyp = jnp.where(myp, pyp, 0.0)
    pzm = jnp.where(mzm, pzm, 0.0)
    pzp = jnp.where(mzp, pzp, 0.0)
    gradients = (pxp - pxm, pyp - pym, pzp - pzm)
    out = []
    divergence = None
    for c in range(3):
        value = now[c]
        xm, xp = shift_x(value, left[c], right[c])
        ym, yp, zm, zp = shifts_yz(value)
        flow = coef_ref[1] * xm + coef_ref[2] * xp
        flow = flow + (coef_ref[3] * ym + coef_ref[4] * yp)
        flow = flow + (coef_ref[5] * zm + coef_ref[6] * zp)
        out.append(base[c] - diagonal * value + flow - 0.5 * gradients[c])
        if c == 0:
            divergence = xp - xm
        elif c == 1:
            divergence = divergence + (jnp.where(myp, yp, 0.0) - jnp.where(mym, ym, 0.0))
        else:
            divergence = divergence + (jnp.where(mzp, zp, 0.0) - jnp.where(mzm, zm, 0.0))
    around = (pxm + pxp) + (pym + pyp) + (pzm + pzp)
    out.append(base[3] - STABILIZE * (6.0 * pressure - around) + 0.5 * divergence)
    return out


def face(near, own, kappa, sign):
    out = []
    for c in range(3):
        out.append(kappa * (near[c] if own is None else near[c] - own[c]))
    out[0] = out[0] - (0.5 * sign) * near[3]
    out.append(STABILIZE * near[3] + (0.5 * sign) * near[0])
    return out


def low(rows):
    return jnp.concatenate([rows, jnp.zeros((4, 128), F32)], axis=0)


def high(rows):
    return jnp.concatenate([jnp.zeros((4, 128), F32), rows], axis=0)


def corrections(units, at, lhs_ref, mask_ref):
    even = iota((8, 128), 1) % 2 == 0
    columns = []
    for unit, place in zip(units, at):
        evens = [jnp.where(even, v, pltpu.roll(v, 1, 1)) for v in unit]
        odds = [jnp.where(even, pltpu.roll(v, 127, 1), v) for v in unit]
        stack = jnp.concatenate(evens + odds, axis=0).astype(BF16).reshape(4, 16, 128)
        masked = [(stack * mask_ref[place, kind]).reshape(64, 128) for kind in range(4)]
        columns.append(jnp.concatenate(masked, axis=0))
    product = jnp.dot(
        lhs_ref[...], jnp.concatenate(columns, axis=1), preferred_element_type=F32
    )
    out = []
    for n in range(len(units)):
        across = slice(128 * n, 128 * n + 128)
        out.append(
            [
                DAMPING
                * jnp.where(even, product[8 * c : 8 * c + 8, across], product[32 + 8 * c : 40 + 8 * c, across])
                for c in range(4)
            ]
        )
    return out


def time_sums(load):
    plain = load(0)
    ramp = None
    for t in range(1, 8):
        value = load(t)
        plain = plain + value
        ramp = value * float(t) if ramp is None else ramp + value * float(t)
    return plain, ramp


def steps(body):
    def several(i, carry):
        for j in range(4):
            body(4 * i + j, i, j)
        return carry

    lax.fori_loop(0, 2, several, 0)


def kernel(
    init5, init, forc, table_in, vclass_in, bank_in, kind_in,
    smoothed, coarse, table, vclass, bank, kind,
    f0, f1, forcing, part, part2, e0, e1, lp, rp, lp2, rp2, lres, rres, ares, lcor, rcor, vk_out, vk_in,
    faces, fields, mass, coef, lhs, mask, weighted_f, parts, edges, parts_in, sums, recv, recv_e,
    load_sem, send_sem, recv_sem, psend_sem, precv_sem, esend_sem, erecv_sem, token_sem, pair_send, pair_recv,
):
    sx = lax.axis_index("space")
    tb = lax.axis_index("tm")
    has_left, has_right = sx > 0, sx < 7
    has_before, has_after = tb > 0, tb < 31
    is_edge = jnp.logical_or(jnp.logical_and(tb < 4, has_left), jnp.logical_and(tb >= 28, has_right))
    to_left, to_right, to_after = {"space": sx - 1}, {"space": sx + 1}, {"tm": tb + 1}
    left_after, right_after = {"space": sx - 1, "tm": tb + 1}, {"space": sx + 1, "tm": tb + 1}
    both = jnp.logical_and

    barrier = pltpu.get_barrier_semaphore()

    def greet(condition, device):
        @pl.when(condition)
        def _():
            pl.semaphore_signal(barrier, inc=1, device_id=device, device_id_type=MESH)

    column, row = lax.rem(tb, 16), tb // 16
    ring = [{"tm": row * 16 + lax.rem(column + step, 16)} for step in (2, 14, 4, 12)]
    far_ring = ring[2:]
    across = {"tm": lax.rem(tb + 16, 32)}
    partner = {"tm": tb + 1 - 2 * lax.rem(tb, 2)}
    greet(has_left, to_left)
    greet(has_right, to_right)
    greet(has_before, {"tm": tb - 1})
    greet(has_after, to_after)
    for device in ring + [across]:
        greet(True, device)

    def tell(n, devices):
        for condition, device in devices:

            @pl.when(condition)
            def _(device=device):
                pl.semaphore_signal(token_sem.at[n], inc=1, device_id=device, device_id_type=MESH)

    circles = [
        [(True, partner)],
        [(True, device) for device in ring],
        [(True, device) for device in far_ring],
        [(True, across)],
    ]
    counts = [1, 4, 2, 1]

    def pass_on(n):
        if n > 0:
            pl.semaphore_wait(token_sem.at[n - 1], counts[n - 1])
        if n < 4:
            tell(n, circles[n])

    loads = [
        pltpu.make_async_copy(table_in, table, load_sem.at[0]),
        pltpu.make_async_copy(vclass_in, vclass, load_sem.at[1]),
        pltpu.make_async_copy(kind_in, kind, load_sem.at[2]),
        pltpu.make_async_copy(init, f0, load_sem.at[3]),
        pltpu.make_async_copy(forc, forcing, load_sem.at[4]),
        pltpu.make_async_copy(bank_in, bank, load_sem.at[5]),
    ]
    for copy in loads[:3] + loads[5:]:
        copy.start()
    for c in range(4):
        pltpu.make_async_copy(init.at[c], f0.at[c], load_sem.at[3]).start()
        pltpu.make_async_copy(forc.at[c], forcing.at[c], load_sem.at[4]).start()

    @pl.when(sx == 0)
    def _():
        vk_in[0] = jnp.zeros((16, 128), F32)
        lp[...] = jnp.zeros_like(lp)
        lres[...] = jnp.zeros_like(lres)

    @pl.when(sx == 7)
    def _():
        vk_in[1] = jnp.zeros((16, 128), F32)
        rp[...] = jnp.zeros_like(rp)
        rres[...] = jnp.zeros_like(rres)

    @pl.when(tb == 0)
    def _():
        e0[...] = jnp.zeros_like(e0)
        ares[...] = jnp.zeros_like(ares)

    @pl.when(jnp.logical_or(tb == 0, sx == 0))
    def _():
        lcor[...] = jnp.zeros_like(lcor)

    @pl.when(jnp.logical_or(tb == 0, sx == 7))
    def _():
        rcor[...] = jnp.zeros_like(rcor)

    @pl.when(jnp.logical_not(is_edge))
    def _():
        recv_e[...] = jnp.zeros_like(recv_e)

    one = lambda condition: condition.astype(jnp.int32)
    pl.semaphore_wait(
        barrier,
        5 + one(has_left) + one(has_right) + one(has_before) + one(has_after),
    )

    def remote(condition, awaited, source, target, n, device):
        copy = pltpu.make_async_remote_copy(
            source, target, send_sem.at[n], recv_sem.at[n], device_id=device, device_id_type=MESH
        )
        return condition, awaited, copy

    round_one = [
        remote(has_left, has_right, vk_out.at[0], vk_in.at[1], 0, to_left),
        remote(has_right, has_left, vk_out.at[1], vk_in.at[0], 1, to_right),
        remote(has_left, has_right, init5.at[:, :, 0], rp, 2, to_left),
        remote(has_right, has_left, init5.at[:, :, 7], lp, 3, to_right),
        remote(has_after, has_before, init.at[0:3, 7], e0, 4, to_after),
        remote(has_after, has_before, part.at[:, 7], ares, 5, to_after),
        remote(both(has_left, has_after), both(has_right, has_before), init.at[:, 7, 0], rcor, 6, left_after),
        remote(both(has_right, has_after), both(has_left, has_before), init.at[:, 7, 3], lcor, 7, right_after),
    ]
    for i in range(2):
        pair = slice(4 * i, 4 * i + 4)
        round_one += [
            remote(has_left, has_right, part.at[:, pair, 0], rres.at[:, pair], 8 + 2 * i, to_left),
            remote(has_right, has_left, part.at[:, pair, 3], lres.at[:, pair], 9 + 2 * i, to_right),
        ]
    def begin(*places):
        for place in places:
            condition, _, copy = round_one[place]
            pl.when(condition)(copy.start)

    begin(2, 3, 4)
    tell(4, [(has_before, {"tm": tb - 1})])
    pass_on(0)

    loads[0].wait()
    loads[1].wait()
    viscosity = jnp.zeros((4, 8, 128), F32)
    for label in range(8):
        viscosity = jnp.where(vclass[...] == label, table[label], viscosity)
    build_coefficients(viscosity, coef)
    loads[2].wait()
    maps = kind_maps(kind)
    vk_out[0, 0:4] = viscosity[0, 0:4]
    vk_out[1, 0:4] = viscosity[3, 4:8]
    vk_out[0, 4:8] = jnp.zeros((4, 128), F32)
    vk_out[1, 4:8] = jnp.zeros((4, 128), F32)
    vk_out[0, 8:16] = maps[0]
    vk_out[1, 8:16] = maps[3]
    begin(0, 1)
    for g in range(4):
        store_mask(maps[g], mask, g + 1)
    loads[3].wait()
    loads[4].wait()

    nothing = [jnp.zeros((4, 128), F32)] * 4

    def local(t):
        now = [f0[c, t] for c in range(4)]
        base = [forcing[c, t] for c in range(4)]
        if t > 0:
            base = [base[c] + f0[c, t - 1] for c in range(3)] + base[3:]
        for c, value in enumerate(residual(now, nothing, nothing, base, coef[0], coef)):
            part[c, t] = value

    for t in range(4):
        local(t)
    begin(8, 9)
    for t in range(4, 8):
        local(t)
    begin(5)
    @pl.when(has_after)
    def _():
        pl.semaphore_wait(token_sem.at[4], 1)
        begin(6, 7)

    begin(10, 11)

    def arrive(first, last):
        for _, awaited, copy in round_one[first:last]:
            pl.when(awaited)(copy.wait_recv)

    loads[5].wait()
    build_bank(bank, lhs)
    pass_on(1)

    first = (lax.rem(tb, 4) * 8).astype(F32) * (1.0 / 1024.0)

    def weigh(plain, ramp):
        far = first * plain + ramp * (1.0 / 1024.0)
        return plain * (1.0 / 32.0) - far, far

    for c in range(4):
        near, far = weigh(*time_sums(lambda t, c=c: forcing[c, t]))
        weighted_f[0, c] = near
        weighted_f[1, c] = far


    for pair in ((1, 2), (3, 4), (5, 6), (7,)):
        where = [(t, g) for t in pair for g in (1, 2)]
        units = [[part[c, t, g] for c in range(4)] for t, g in where]
        for (t, g), change in zip(where, corrections(units, [g + 1 for _, g in where], lhs, mask)):
            for c in range(4):
                f1[c, t, g] = f0[c, t, g] + change[c]

    pass_on(2)
    arrive(0, 2)
    faces[0] = 0.5 * (viscosity[0, 0:4] + vk_in[0, 0:4])
    faces[1] = 0.5 * (viscosity[3, 4:8] + vk_in[1, 0:4])
    store_mask(vk_in[0, 8:16], mask, 0)
    store_mask(vk_in[1, 8:16], mask, 5)
    arrive(2, 5)
    pass_on(3)

    units = [[part[c, 0, g] + (e0[c, g] if c < 3 else 0.0) for c in range(4)] for g in (1, 2)]
    for g, change in zip((1, 2), corrections(units, [2, 3], lhs, mask)):
        for c in range(4):
            f1[c, 0, g] = f0[c, 0, g] + change[c]

    def plane(ref, t, side):
        if side == 0:
            return [ref[c, t, 0, 0:4] for c in range(4)]
        return [ref[c, t, 3, 4:8] for c in range(4)]

    def outer(t, i, j):
        units = []
        for side, g, near, sign, place in ((0, 0, lp, -1.0, low), (1, 3, rp, 1.0, high)):
            extra = face([near[c, t] for c in range(4)], plane(f0, t, side), faces[side], sign)
            unit = [part[c, t, g] + place(extra[c]) for c in range(4)]
            if j == 0:
                unit = [unit[c] + jnp.where(i == 0, e0[c, g], 0.0) for c in range(3)] + unit[3:]
            units.append(unit)
        for g, change in zip((0, 3), corrections(units, [1, 4], lhs, mask)):
            for c in range(4):
                f1[c, t, g] = f0[c, t, g] + change[c]

    steps(outer)


    def middle(pair):
        units = []
        for t in pair:
            now = [f1[c, t] for c in range(4)]
            base = [forcing[c, t] for c in range(4)]
            for c in range(3):
                base[c] = base[c] + (f1[c, t - 1] if t > 0 else e1[c])
            resid = residual(now, nothing, nothing, base, coef[0], coef)
            for c in range(4):
                part2[c, t] = resid[c]
            units += [[resid[c][g] for c in range(4)] for g in (1, 2)]
        changes = corrections(units, [2, 3] * len(pair), lhs, mask)
        for n, t in enumerate(pair):
            for g in (1, 2):
                for c in range(4):
                    smoothed[c, t, g] = f1[c, t, g] + changes[2 * n + g - 1][c]

    middle((1, 2, 3))
    middle((4, 5, 6, 7))


    def sum_up(rows):
        for c in range(4):
            plain, ramp = time_sums(lambda t: smoothed[c, t, rows])
            near, far = weigh(plain, ramp)
            fields[0, c, rows] = near
            fields[1, c, rows] = far
            mass[c, rows] = plain * (1.0 / 1024.0)

    def beside(pair):
        units = []
        for t in pair:
            extra = face(plane(f0, t, 0), [lp[c, t] for c in range(4)], faces[0], 1.0)
            unit = [lres[c, t] + high(extra[c]) for c in range(4)]
            if t == 0:
                unit = [unit[c] + lcor[c] for c in range(3)] + unit[3:]
            units.append(unit)
            extra = face(plane(f0, t, 1), [rp[c, t] for c in range(4)], faces[1], -1.0)
            unit = [rres[c, t] + low(extra[c]) for c in range(4)]
            if t == 0:
                unit = [unit[c] + rcor[c] for c in range(3)] + unit[3:]
            units.append(unit)
        changes = corrections(units, [0, 5] * 8, lhs, mask)
        for n, t in enumerate(pair):
            for c in range(4):
                lp2[c, t] = jnp.where(has_left, lp[c, t] + changes[2 * n][c][4:8], 0.0)
                rp2[c, t] = jnp.where(has_right, rp[c, t] + changes[2 * n + 1][c][0:4], 0.0)

    def ends(pair):
        units = []
        for t in pair:
            for side, g, near, sign, place in ((0, 0, lp2, -1.0, low), (1, 3, rp2, 1.0, high)):
                extra = face([near[c, t] for c in range(4)], plane(f1, t, side), faces[side], sign)
                units.append([part2[c, t, g] + place(extra[c]) for c in range(4)])
        changes = corrections(units, [1, 4] * 8, lhs, mask)
        for n, t in enumerate(pair):
            for side, g in ((0, 0), (1, 3)):
                for c in range(4):
                    smoothed[c, t, g] = f1[c, t, g] + changes[2 * n + side][c]

    arrive(5, 12)
    beside(range(8))

    units = [[ares[c, g] for c in range(4)] for g in range(4)]
    old = [e0[c, 0, 0:4] for c in range(3)]
    extra = face([lcor[c, 4:8] for c in range(4)], old, faces[0], -1.0)
    units[0] = [units[0][c] + low(extra[c]) for c in range(4)]
    old = [e0[c, 3, 4:8] for c in range(3)]
    extra = face([rcor[c, 0:4] for c in range(4)], old, faces[1], 1.0)
    units[3] = [units[3][c] + high(extra[c]) for c in range(4)]
    for g, change in enumerate(corrections(units, [1, 2, 3, 4], lhs, mask)):
        for c in range(3):
            e1[c, g] = e0[c, g] + change[c]

    middle((0,))
    sum_up(slice(1, 3))
    ends(range(8))

    for g in (0, 3):
        sum_up(slice(g, g + 1))
    for half in range(2):
        for side, rows, sign in ((0, slice(0, 4), 1.0), (1, slice(4, 8), -1.0)):
            near = [fields[half, c, 3 * side, rows] for c in range(4)]
            for c, value in enumerate(face(near, None, faces[side], sign)):
                edges[side, pl.ds(4 * half + c, 4, stride=8), :] = value

    def edge_piece(side, y, device):
        return pltpu.make_async_remote_copy(
            edges.at[side, pl.ds(8 * y, 8)], recv_e.at[tb], esend_sem.at[side], erecv_sem,
            device_id=device, device_id_type=MESH,
        )

    pass_on(4)

    @pl.when(has_left)
    def _():
        for y in range(4):
            edge_piece(0, y, {"space": sx - 1, "tm": 28 + y}).start()

    @pl.when(has_right)
    def _():
        for y in range(4):
            edge_piece(1, y, {"space": sx + 1, "tm": y}).start()

    for half in range(2):
        now = [fields[half, c] for c in range(4)]
        base = [weighted_f[half, c] for c in range(4)]
        for c in range(3):
            base[c] = base[c] - mass[c] if half == 0 else base[c] + mass[c]
        resid = residual(now, nothing, nothing, base, coef[7], coef)
        for c in range(4):
            row = 4 * half + c
            for g in range(4):
                value = resid[c][g]
                if c < 3 and g == 0:
                    value = value - low(faces[0] * now[c][0, 0:4])
                if c < 3 and g == 3:
                    value = value - high(faces[1] * now[c][3, 4:8])
                parts[pl.ds(64 * g + row, 8, stride=8), :] = value

    core = lax.rem(tb, 2)
    swap = pltpu.make_async_remote_copy(
        parts.at[pl.ds(pl.multiple_of(128 * (1 - core), 128), 128)], parts_in, pair_send, pair_recv,
        device_id=partner, device_id_type=MESH,
    )
    swap.start()

    def tile(ref, row):
        return ref.at[pl.ds(pl.multiple_of(row * 8, 8), 8)]

    swap.wait_recv()
    sums[...] = parts[pl.ds(pl.multiple_of(128 * core, 128), 128), :] + parts_in[...]

    def send(step, carry, hot):
        k = step // 2
        odd = lax.rem(k, 2)
        dz = 4 + (k // 2) * (1 - odd) - ((k + 1) // 2) * odd
        place = lax.rem(column // 2 * 2 + 2 * dz, 16) + lax.rem(step, 2)
        peer = 16 * core + place

        is_hot = jnp.logical_or(peer < 4, peer >= 28)

        @pl.when(both(peer != tb, is_hot if hot else jnp.logical_not(is_hot)))
        def _():
            pltpu.make_async_remote_copy(
                tile(sums, place), recv.at[tb // 2], psend_sem, precv_sem,
                device_id={"tm": peer}, device_id_type=MESH,
            ).start()

        return carry

    lax.fori_loop(0, 16, functools.partial(send, hot=True), 0)
    lax.fori_loop(0, 16, functools.partial(send, hot=False), 0)
    keeps = tb // 16 == core

    @pl.when(keeps)
    def _():
        recv[tb // 2] = tile(sums, column)[...]

    for condition, _, copy in round_one:
        pl.when(condition)(copy.wait_send)

    swap.wait_send()

    def sent_edges(side):
        pltpu.make_async_remote_copy(
            edges.at[side], edges.at[side], esend_sem.at[side], erecv_sem, device_id=partner, device_id_type=MESH
        ).wait_send()

    pl.when(has_left)(lambda: sent_edges(0))
    pl.when(has_right)(lambda: sent_edges(1))

    def settle(number):
        pieces = pltpu.make_async_remote_copy(
            recv.at[0:number], recv.at[0:number], psend_sem, precv_sem, device_id=partner, device_id_type=MESH
        )
        pieces.wait_send()
        pieces.wait_recv()

    pl.when(keeps)(lambda: settle(15))
    pl.when(jnp.logical_not(keeps))(lambda: settle(16))

    @pl.when(is_edge)
    def _():
        pltpu.make_async_remote_copy(
            recv_e, recv_e, psend_sem, erecv_sem, device_id=partner, device_id_type=MESH
        ).wait_recv()

    before = jnp.zeros((4, 128), F32)
    for k in range(8):
        block = recv[2 * k] + recv[2 * k + 1]
        block = block + (
            (recv_e[4 * k] + recv_e[4 * k + 1]) + (recv_e[4 * k + 2] + recv_e[4 * k + 3])
        )
        level = block[0:4] + before
        before = block[4:8]
        for c in range(4):
            coarse[c, k : k + 1, :] = level[c : c + 1]


def store(smoothed_in, coarse_in, smoothed, coarse, sems):
    copies = [
        pltpu.make_async_copy(smoothed_in, smoothed, sems.at[0]),
        pltpu.make_async_copy(coarse_in, coarse, sems.at[1]),
    ]
    for copy in copies:
        copy.start()
    for copy in copies:
        copy.wait()


def per_device(initial_guess, forcing, visc_table, visc_class, inverse_bank, patch_kind):
    hbm = pl.BlockSpec(memory_space=pltpu.HBM)
    vmem = pl.BlockSpec(memory_space=pltpu.VMEM)
    dma = pltpu.SemaphoreType.DMA
    smoothed, coarse = pl.pallas_call(
        kernel,
        out_shape=(
            pltpu.VMEM((4, 8, 4, 8, 128), F32),
            pltpu.VMEM((4, 8, 128), F32),
        ),
        in_specs=[hbm] * 7,
        out_specs=(vmem, vmem),
        scratch_shapes=[
            pltpu.SMEM((8,), F32),
            pltpu.VMEM((4, 8, 128), jnp.int32),
            pltpu.VMEM((4, 32, 32), BF16),
            pltpu.VMEM((4, 2, 64), jnp.int32),
            pltpu.VMEM((4, 8, 4, 8, 128), F32),
            pltpu.VMEM((4, 8, 4, 8, 128), F32),
            pltpu.VMEM((4, 8, 4, 8, 128), F32),
            pltpu.VMEM((4, 8, 4, 8, 128), F32),
            pltpu.VMEM((4, 8, 4, 8, 128), F32),
            pltpu.VMEM((3, 4, 8, 128), F32),
            pltpu.VMEM((3, 4, 8, 128), F32),
            pltpu.VMEM((4, 8, 4, 128), F32),
            pltpu.VMEM((4, 8, 4, 128), F32),
            pltpu.VMEM((4, 8, 4, 128), F32),
            pltpu.VMEM((4, 8, 4, 128), F32),
            pltpu.VMEM((4, 8, 8, 128), F32),
            pltpu.VMEM((4, 8, 8, 128), F32),
            pltpu.VMEM((4, 4, 8, 128), F32),
            pltpu.VMEM((4, 8, 128), F32),
            pltpu.VMEM((4, 8, 128), F32),
            pltpu.VMEM((2, 16, 128), F32),
            pltpu.VMEM((2, 16, 128), F32),
            pltpu.VMEM((2, 4, 128), F32),
            pltpu.VMEM((2, 4, 4, 8, 128), F32),
            pltpu.VMEM((4, 4, 8, 128), F32),
            pltpu.VMEM((8, 4, 8, 128), F32),
            pltpu.VMEM((64, 256), BF16),
            pltpu.VMEM((6, 4, 16, 128), BF16),
            pltpu.VMEM((2, 4, 4, 8, 128), F32),
            pltpu.VMEM((256, 128), F32),
            pltpu.VMEM((2, 32, 128), F32),
            pltpu.VMEM((128, 128), F32),
            pltpu.VMEM((128, 128), F32),
            pltpu.VMEM((16, 8, 128), F32),
            pltpu.VMEM((32, 8, 128), F32),
            dma((6,)),
            dma((12,)),
            dma((12,)),
            dma,
            dma,
            dma((2,)),
            dma,
            pltpu.SemaphoreType.REGULAR((5,)),
            dma,
            dma,
        ],
        compiler_params=pltpu.CompilerParams(
            collective_id=0, has_side_effects=True, vmem_limit_bytes=60 * 1024 * 1024
        ),
    )(
        initial_guess,
        initial_guess.reshape(4, 8, 4, 8, 128),
        forcing.reshape(4, 8, 4, 8, 128),
        visc_table,
        visc_class.reshape(4, 8, 128),
        inverse_bank,
        patch_kind,
    )
    smoothed, coarse = pl.pallas_call(
        store,
        out_shape=(
            jax.ShapeDtypeStruct((4, 8, 4, 8, 128), F32),
            jax.ShapeDtypeStruct((4, 8, 128), F32),
        ),
        in_specs=[pl.BlockSpec(memory_space=pl.ANY)] * 2,
        out_specs=(pl.BlockSpec(memory_space=pl.ANY),) * 2,
        scratch_shapes=[dma((2,))],
        compiler_params=pltpu.CompilerParams(vmem_limit_bytes=4 * 1024 * 1024),
    )(smoothed, coarse)
    return smoothed.reshape(4, 8, 8, 4, 128), coarse


def solution(mesh):
    return jax.shard_map(
        per_device,
        mesh=mesh,
        in_specs=(
            P(None, "tm", "space", None, None),
            P(None, "tm", "space", None, None),
            P(),
            P("space", None, None),
            P(),
            P("space", None, None),
        ),
        out_specs=(P(None, "tm", "space", None, None), P(None, None, ("space", "tm"))),
        check_vma=False,
    )
```

```python
import functools

import jax
import jax.numpy as jnp
from jax import lax
from jax.experimental import pallas as pl
from jax.experimental.pallas import tpu as pltpu
from jax.sharding import PartitionSpec as P

MESH = pl.DeviceIdType.MESH
F32 = jnp.float32
BF16 = jnp.bfloat16
DAMPING = 0.8
STABILIZE = 0.1


def iota(shape, dim):
    return lax.broadcasted_iota(jnp.int32, shape, dim)


def cell_index(q):
    return (q // 8) * 8 + (q // 4 % 2) * 4 + (q % 2) * 2


def build_bank(bank_ref, lhs_ref):
    j = iota((32, 64), 0)
    q = iota((32, 64), 1)
    spread = (j == cell_index(q % 32) + q // 32).astype(BF16)
    p = iota((64, 32), 0)
    i = iota((64, 32), 1)
    gather = (i == cell_index(p % 32) + p // 32).astype(BF16)
    same = (iota((64, 64), 0) // 2 % 2) == (iota((64, 64), 1) // 2 % 2)
    wide = jnp.dot(bank_ref[...].reshape(128, 32), spread, preferred_element_type=F32).astype(BF16)
    parts = []
    for kind in range(4):
        part = jnp.dot(gather, wide[32 * kind : 32 * kind + 32], preferred_element_type=F32)
        parts.append(jnp.where(same, part, 0.0).astype(BF16))
    lhs_ref[...] = jnp.concatenate(parts, axis=1)


def kind_maps(kind_ref):
    upper = iota((8, 64), 0) // 2 % 2 == 0
    double = (iota((64, 128), 0) == iota((64, 128), 1) // 2).astype(BF16)
    maps = []
    for g in range(4):
        pair = kind_ref[g].astype(F32)
        rows = jnp.where(upper, pair[0:1], pair[1:2]).astype(BF16)
        maps.append(jnp.dot(rows, double, preferred_element_type=F32))
    return maps


def store_mask(kinds, mask_ref, at):
    for kind in range(4):
        mask = (kinds == float(kind)).astype(F32)
        mask_ref[at, kind] = jnp.concatenate([mask, mask], axis=0).astype(BF16)


def shift_x(values, left, right):
    first = jnp.concatenate([left, values[0, 0:4]], axis=0)
    last = jnp.concatenate([values[3, 4:8], right], axis=0)
    low = iota((3, 8, 128), 1) < 4
    inner = pltpu.roll(jnp.where(low, values[1:4], values[0:3]), 4, 1)
    return (
        jnp.concatenate([first[None], inner], axis=0),
        jnp.concatenate([inner, last[None]], axis=0),
    )


def shifts_yz(values):
    return (
        pltpu.roll(values, 1, 1),
        pltpu.roll(values, 7, 1),
        pltpu.roll(values, 1, 2),
        pltpu.roll(values, 127, 2),
    )


def edge_masks():
    y = iota((4, 8, 128), 1) % 4
    z = iota((4, 8, 128), 2)
    return y != 0, y != 3, z != 0, z != 127


def build_coefficients(viscosity, coef_ref):
    none = jnp.zeros((4, 128), F32)
    xm, xp = shift_x(viscosity, none, none)
    ym, yp, zm, zp = shifts_yz(viscosity)
    g, row = iota((4, 8, 128), 0), iota((4, 8, 128), 1)
    has_xm = jnp.logical_or(g > 0, row >= 4)
    has_xp = jnp.logical_or(g < 3, row < 4)
    total = jnp.zeros_like(viscosity)
    for n, (near, mask) in enumerate(zip((xm, xp, ym, yp, zm, zp), (has_xm, has_xp) + edge_masks())):
        near = jnp.where(mask, near, 0.0)
        kappa = 0.5 * (viscosity + near)
        inner = jnp.where(mask, kappa, 0.0)
        total = total + (inner if n < 2 else kappa)
        coef_ref[1 + n] = inner
    coef_ref[0] = total + 1.0
    coef_ref[7] = total


def residual(now, left, right, base, diagonal, coef_ref):
    mym, myp, mzm, mzp = edge_masks()
    pressure = now[3]
    pxm, pxp = shift_x(pressure, left[3], right[3])
    pym, pyp, pzm, pzp = shifts_yz(pressure)
    pym = jnp.where(mym, pym, 0.0)
    pyp = jnp.where(myp, pyp, 0.0)
    pzm = jnp.where(mzm, pzm, 0.0)
    pzp = jnp.where(mzp, pzp, 0.0)
    gradients = (pxp - pxm, pyp - pym, pzp - pzm)
    out = []
    divergence = None
    for c in range(3):
        value = now[c]
        xm, xp = shift_x(value, left[c], right[c])
        ym, yp, zm, zp = shifts_yz(value)
        flow = coef_ref[1] * xm + coef_ref[2] * xp
        flow = flow + (coef_ref[3] * ym + coef_ref[4] * yp)
        flow = flow + (coef_ref[5] * zm + coef_ref[6] * zp)
        out.append(base[c] - diagonal * value + flow - 0.5 * gradients[c])
        if c == 0:
            divergence = xp - xm
        elif c == 1:
            divergence = divergence + (jnp.where(myp, yp, 0.0) - jnp.where(mym, ym, 0.0))
        else:
            divergence = divergence + (jnp.where(mzp, zp, 0.0) - jnp.where(mzm, zm, 0.0))
    around = (pxm + pxp) + (pym + pyp) + (pzm + pzp)
    out.append(base[3] - STABILIZE * (6.0 * pressure - around) + 0.5 * divergence)
    return out


def face(near, own, kappa, sign):
    out = []
    for c in range(3):
        out.append(kappa * (near[c] if own is None else near[c] - own[c]))
    out[0] = out[0] - (0.5 * sign) * near[3]
    out.append(STABILIZE * near[3] + (0.5 * sign) * near[0])
    return out


def low(rows):
    return jnp.concatenate([rows, jnp.zeros((4, 128), F32)], axis=0)


def high(rows):
    return jnp.concatenate([jnp.zeros((4, 128), F32), rows], axis=0)


def corrections(units, at, lhs_ref, mask_ref):
    even = iota((8, 128), 1) % 2 == 0
    columns = []
    for unit, place in zip(units, at):
        evens = [jnp.where(even, v, pltpu.roll(v, 1, 1)) for v in unit]
        odds = [jnp.where(even, pltpu.roll(v, 127, 1), v) for v in unit]
        stack = jnp.concatenate(evens + odds, axis=0).astype(BF16).reshape(4, 16, 128)
        masked = [(stack * mask_ref[place, kind]).reshape(64, 128) for kind in range(4)]
        columns.append(jnp.concatenate(masked, axis=0))
    product = jnp.dot(
        lhs_ref[...], jnp.concatenate(columns, axis=1), preferred_element_type=F32
    )
    out = []
    for n in range(len(units)):
        across = slice(128 * n, 128 * n + 128)
        out.append(
            [
                DAMPING
                * jnp.where(even, product[8 * c : 8 * c + 8, across], product[32 + 8 * c : 40 + 8 * c, across])
                for c in range(4)
            ]
        )
    return out


def time_sums(load):
    plain = load(0)
    ramp = None
    for t in range(1, 8):
        value = load(t)
        plain = plain + value
        ramp = value * float(t) if ramp is None else ramp + value * float(t)
    return plain, ramp


def steps(body):
    def several(i, carry):
        for j in range(4):
            body(4 * i + j, i, j)
        return carry

    lax.fori_loop(0, 2, several, 0)


def kernel(
    init5, init, forc, table_in, vclass_in, bank_in, kind_in,
    smoothed, coarse, table, vclass, bank, kind,
    f0, f1, forcing, part, part2, e0, e1, lp, rp, lp2, rp2, lres, rres, ares, lcor, rcor, vk_out, vk_in,
    faces, fields, mass, coef, lhs, mask, weighted_f, parts, edges, parts_in, sums, recv, recv_e,
    load_sem, send_sem, recv_sem, psend_sem, precv_sem, esend_sem, erecv_sem, token_sem, pair_send, pair_recv,
):
    sx = lax.axis_index("space")
    tb = lax.axis_index("tm")
    has_left, has_right = sx > 0, sx < 7
    has_before, has_after = tb > 0, tb < 31
    is_edge = jnp.logical_or(jnp.logical_and(tb < 4, has_left), jnp.logical_and(tb >= 28, has_right))
    to_left, to_right, to_after = {"space": sx - 1}, {"space": sx + 1}, {"tm": tb + 1}
    left_after, right_after = {"space": sx - 1, "tm": tb + 1}, {"space": sx + 1, "tm": tb + 1}
    both = jnp.logical_and

    barrier = pltpu.get_barrier_semaphore()

    def greet(condition, device):
        @pl.when(condition)
        def _():
            pl.semaphore_signal(barrier, inc=1, device_id=device, device_id_type=MESH)

    column, row = lax.rem(tb, 16), tb // 16
    ring = [{"tm": row * 16 + lax.rem(column + step, 16)} for step in (2, 14, 4, 12)]
    far_ring = ring[2:]
    across = {"tm": lax.rem(tb + 16, 32)}
    partner = {"tm": tb + 1 - 2 * lax.rem(tb, 2)}
    greet(has_left, to_left)
    greet(has_right, to_right)
    greet(has_before, {"tm": tb - 1})
    greet(has_after, to_after)
    for device in ring + [across]:
        greet(True, device)

    def tell(n, devices):
        for condition, device in devices:

            @pl.when(condition)
            def _(device=device):
                pl.semaphore_signal(token_sem.at[n], inc=1, device_id=device, device_id_type=MESH)

    circles = [
        [(True, partner)],
        [(True, device) for device in ring],
        [(True, device) for device in far_ring],
        [(True, across)],
    ]
    counts = [1, 4, 2, 1]

    def pass_on(n):
        if n > 0:
            pl.semaphore_wait(token_sem.at[n - 1], counts[n - 1])
        if n < 4:
            tell(n, circles[n])

    loads = [
        pltpu.make_async_copy(table_in, table, load_sem.at[0]),
        pltpu.make_async_copy(vclass_in, vclass, load_sem.at[1]),
        pltpu.make_async_copy(kind_in, kind, load_sem.at[2]),
        pltpu.make_async_copy(init, f0, load_sem.at[3]),
        pltpu.make_async_copy(forc, forcing, load_sem.at[4]),
        pltpu.make_async_copy(bank_in, bank, load_sem.at[5]),
    ]
    for copy in loads[:3] + loads[5:]:
        copy.start()
    for c in range(4):
        pltpu.make_async_copy(init.at[c], f0.at[c], load_sem.at[3]).start()
        pltpu.make_async_copy(forc.at[c], forcing.at[c], load_sem.at[4]).start()

    @pl.when(sx == 0)
    def _():
        vk_in[0] = jnp.zeros((16, 128), F32)
        lp[...] = jnp.zeros_like(lp)
        lres[...] = jnp.zeros_like(lres)

    @pl.when(sx == 7)
    def _():
        vk_in[1] = jnp.zeros((16, 128), F32)
        rp[...] = jnp.zeros_like(rp)
        rres[...] = jnp.zeros_like(rres)

    @pl.when(tb == 0)
    def _():
        e0[...] = jnp.zeros_like(e0)
        ares[...] = jnp.zeros_like(ares)

    @pl.when(jnp.logical_or(tb == 0, sx == 0))
    def _():
        lcor[...] = jnp.zeros_like(lcor)

    @pl.when(jnp.logical_or(tb == 0, sx == 7))
    def _():
        rcor[...] = jnp.zeros_like(rcor)

    @pl.when(jnp.logical_not(is_edge))
    def _():
        recv_e[...] = jnp.zeros_like(recv_e)

    one = lambda condition: condition.astype(jnp.int32)
    pl.semaphore_wait(
        barrier,
        5 + one(has_left) + one(has_right) + one(has_before) + one(has_after),
    )

    def remote(condition, awaited, source, target, n, device):
        copy = pltpu.make_async_remote_copy(
            source, target, send_sem.at[n], recv_sem.at[n], device_id=device, device_id_type=MESH
        )
        return condition, awaited, copy

    round_one = [
        remote(has_left, has_right, vk_out.at[0], vk_in.at[1], 0, to_left),
        remote(has_right, has_left, vk_out.at[1], vk_in.at[0], 1, to_right),
        remote(has_left, has_right, init5.at[:, :, 0], rp, 2, to_left),
        remote(has_right, has_left, init5.at[:, :, 7], lp, 3, to_right),
        remote(has_after, has_before, init.at[0:3, 7], e0, 4, to_after),
        remote(has_after, has_before, part.at[:, 7], ares, 5, to_after),
        remote(both(has_left, has_after), both(has_right, has_before), init.at[:, 7, 0], rcor, 6, left_after),
        remote(both(has_right, has_after), both(has_left, has_before), init.at[:, 7, 3], lcor, 7, right_after),
    ]
    for i in range(2):
        pair = slice(4 * i, 4 * i + 4)
        round_one += [
            remote(has_left, has_right, part.at[:, pair, 0], rres.at[:, pair], 8 + 2 * i, to_left),
            remote(has_right, has_left, part.at[:, pair, 3], lres.at[:, pair], 9 + 2 * i, to_right),
        ]
    def begin(*places):
        for place in places:
            condition, _, copy = round_one[place]
            pl.when(condition)(copy.start)

    begin(2, 3, 4)
    tell(4, [(has_before, {"tm": tb - 1})])
    pass_on(0)

    loads[0].wait()
    loads[1].wait()
    viscosity = jnp.zeros((4, 8, 128), F32)
    for label in range(8):
        viscosity = jnp.where(vclass[...] == label, table[label], viscosity)
    build_coefficients(viscosity, coef)
    loads[2].wait()
    maps = kind_maps(kind)
    vk_out[0, 0:4] = viscosity[0, 0:4]
    vk_out[1, 0:4] = viscosity[3, 4:8]
    vk_out[0, 4:8] = jnp.zeros((4, 128), F32)
    vk_out[1, 4:8] = jnp.zeros((4, 128), F32)
    vk_out[0, 8:16] = maps[0]
    vk_out[1, 8:16] = maps[3]
    begin(0, 1)
    loads[3].wait()
    loads[4].wait()

    nothing = [jnp.zeros((4, 128), F32)] * 4

    def local(t):
        now = [f0[c, t] for c in range(4)]
        base = [forcing[c, t] for c in range(4)]
        if t > 0:
            base = [base[c] + f0[c, t - 1] for c in range(3)] + base[3:]
        for c, value in enumerate(residual(now, nothing, nothing, base, coef[0], coef)):
            part[c, t] = value

    for t in range(4):
        local(t)
    begin(8, 9)
    for t in range(4, 8):
        local(t)
    begin(5)
    @pl.when(has_after)
    def _():
        pl.semaphore_wait(token_sem.at[4], 1)
        begin(6, 7)

    begin(10, 11)
    for g in range(4):
        store_mask(maps[g], mask, g + 1)

    def arrive(first, last):
        for _, awaited, copy in round_one[first:last]:
            pl.when(awaited)(copy.wait_recv)

    loads[5].wait()
    build_bank(bank, lhs)
    pass_on(1)

    first = (lax.rem(tb, 4) * 8).astype(F32) * (1.0 / 1024.0)

    def weigh(plain, ramp):
        far = first * plain + ramp * (1.0 / 1024.0)
        return plain * (1.0 / 32.0) - far, far

    for c in range(4):
        near, far = weigh(*time_sums(lambda t, c=c: forcing[c, t]))
        weighted_f[0, c] = near
        weighted_f[1, c] = far


    for pair in ((1, 2), (3, 4), (5, 6), (7,)):
        where = [(t, g) for t in pair for g in (1, 2)]
        units = [[part[c, t, g] for c in range(4)] for t, g in where]
        for (t, g), change in zip(where, corrections(units, [g + 1 for _, g in where], lhs, mask)):
            for c in range(4):
                f1[c, t, g] = f0[c, t, g] + change[c]

    pass_on(2)
    arrive(0, 2)
    faces[0] = 0.5 * (viscosity[0, 0:4] + vk_in[0, 0:4])
    faces[1] = 0.5 * (viscosity[3, 4:8] + vk_in[1, 0:4])
    store_mask(vk_in[0, 8:16], mask, 0)
    store_mask(vk_in[1, 8:16], mask, 5)
    arrive(2, 5)
    pass_on(3)

    units = [[part[c, 0, g] + (e0[c, g] if c < 3 else 0.0) for c in range(4)] for g in (1, 2)]
    for g, change in zip((1, 2), corrections(units, [2, 3], lhs, mask)):
        for c in range(4):
            f1[c, 0, g] = f0[c, 0, g] + change[c]

    def plane(ref, t, side):
        if side == 0:
            return [ref[c, t, 0, 0:4] for c in range(4)]
        return [ref[c, t, 3, 4:8] for c in range(4)]

    def outer(t, i, j):
        units = []
        for side, g, near, sign, place in ((0, 0, lp, -1.0, low), (1, 3, rp, 1.0, high)):
            extra = face([near[c, t] for c in range(4)], plane(f0, t, side), faces[side], sign)
            unit = [part[c, t, g] + place(extra[c]) for c in range(4)]
            if j == 0:
                unit = [unit[c] + jnp.where(i == 0, e0[c, g], 0.0) for c in range(3)] + unit[3:]
            units.append(unit)
        for g, change in zip((0, 3), corrections(units, [1, 4], lhs, mask)):
            for c in range(4):
                f1[c, t, g] = f0[c, t, g] + change[c]

    steps(outer)


    def middle(pair):
        units = []
        for t in pair:
            now = [f1[c, t] for c in range(4)]
            base = [forcing[c, t] for c in range(4)]
            for c in range(3):
                base[c] = base[c] + (f1[c, t - 1] if t > 0 else e1[c])
            resid = residual(now, nothing, nothing, base, coef[0], coef)
            for c in range(4):
                part2[c, t] = resid[c]
            units += [[resid[c][g] for c in range(4)] for g in (1, 2)]
        changes = corrections(units, [2, 3] * len(pair), lhs, mask)
        for n, t in enumerate(pair):
            for g in (1, 2):
                for c in range(4):
                    smoothed[c, t, g] = f1[c, t, g] + changes[2 * n + g - 1][c]

    middle((1, 2, 3))
    middle((4, 5, 6, 7))


    def sum_up(rows):
        for c in range(4):
            plain, ramp = time_sums(lambda t: smoothed[c, t, rows])
            near, far = weigh(plain, ramp)
            fields[0, c, rows] = near
            fields[1, c, rows] = far
            mass[c, rows] = plain * (1.0 / 1024.0)

    def beside(pair):
        units = []
        for t in pair:
            extra = face(plane(f0, t, 0), [lp[c, t] for c in range(4)], faces[0], 1.0)
            unit = [lres[c, t] + high(extra[c]) for c in range(4)]
            if t == 0:
                unit = [unit[c] + lcor[c] for c in range(3)] + unit[3:]
            units.append(unit)
            extra = face(plane(f0, t, 1), [rp[c, t] for c in range(4)], faces[1], -1.0)
            unit = [rres[c, t] + low(extra[c]) for c in range(4)]
            if t == 0:
                unit = [unit[c] + rcor[c] for c in range(3)] + unit[3:]
            units.append(unit)
        changes = corrections(units, [0, 5] * 8, lhs, mask)
        for n, t in enumerate(pair):
            for c in range(4):
                lp2[c, t] = jnp.where(has_left, lp[c, t] + changes[2 * n][c][4:8], 0.0)
                rp2[c, t] = jnp.where(has_right, rp[c, t] + changes[2 * n + 1][c][0:4], 0.0)

    def ends(pair):
        units = []
        for t in pair:
            for side, g, near, sign, place in ((0, 0, lp2, -1.0, low), (1, 3, rp2, 1.0, high)):
                extra = face([near[c, t] for c in range(4)], plane(f1, t, side), faces[side], sign)
                units.append([part2[c, t, g] + place(extra[c]) for c in range(4)])
        changes = corrections(units, [1, 4] * 8, lhs, mask)
        for n, t in enumerate(pair):
            for side, g in ((0, 0), (1, 3)):
                for c in range(4):
                    smoothed[c, t, g] = f1[c, t, g] + changes[2 * n + side][c]

    arrive(5, 12)
    beside(range(8))

    units = [[ares[c, g] for c in range(4)] for g in range(4)]
    old = [e0[c, 0, 0:4] for c in range(3)]
    extra = face([lcor[c, 4:8] for c in range(4)], old, faces[0], -1.0)
    units[0] = [units[0][c] + low(extra[c]) for c in range(4)]
    old = [e0[c, 3, 4:8] for c in range(3)]
    extra = face([rcor[c, 0:4] for c in range(4)], old, faces[1], 1.0)
    units[3] = [units[3][c] + high(extra[c]) for c in range(4)]
    for g, change in enumerate(corrections(units, [1, 2, 3, 4], lhs, mask)):
        for c in range(3):
            e1[c, g] = e0[c, g] + change[c]

    middle((0,))
    sum_up(slice(1, 3))
    ends(range(8))

    for g in (0, 3):
        sum_up(slice(g, g + 1))
    for half in range(2):
        for side, rows, sign in ((0, slice(0, 4), 1.0), (1, slice(4, 8), -1.0)):
            near = [fields[half, c, 3 * side, rows] for c in range(4)]
            for c, value in enumerate(face(near, None, faces[side], sign)):
                edges[side, pl.ds(4 * half + c, 4, stride=8), :] = value

    def edge_piece(side, y, device):
        return pltpu.make_async_remote_copy(
            edges.at[side, pl.ds(8 * y, 8)], recv_e.at[tb], esend_sem.at[side], erecv_sem,
            device_id=device, device_id_type=MESH,
        )

    pass_on(4)

    @pl.when(has_left)
    def _():
        for y in range(4):
            edge_piece(0, y, {"space": sx - 1, "tm": 28 + y}).start()

    @pl.when(has_right)
    def _():
        for y in range(4):
            edge_piece(1, y, {"space": sx + 1, "tm": y}).start()

    for half in range(2):
        now = [fields[half, c] for c in range(4)]
        base = [weighted_f[half, c] for c in range(4)]
        for c in range(3):
            base[c] = base[c] - mass[c] if half == 0 else base[c] + mass[c]
        resid = residual(now, nothing, nothing, base, coef[7], coef)
        for c in range(4):
            row = 4 * half + c
            for g in range(4):
                value = resid[c][g]
                if c < 3 and g == 0:
                    value = value - low(faces[0] * now[c][0, 0:4])
                if c < 3 and g == 3:
                    value = value - high(faces[1] * now[c][3, 4:8])
                parts[pl.ds(64 * g + row, 8, stride=8), :] = value

    core = lax.rem(tb, 2)
    swap = pltpu.make_async_remote_copy(
        parts.at[pl.ds(pl.multiple_of(128 * (1 - core), 128), 128)], parts_in, pair_send, pair_recv,
        device_id=partner, device_id_type=MESH,
    )
    swap.start()

    def tile(ref, row):
        return ref.at[pl.ds(pl.multiple_of(row * 8, 8), 8)]

    swap.wait_recv()
    sums[...] = parts[pl.ds(pl.multiple_of(128 * core, 128), 128), :] + parts_in[...]

    def send(step, carry, hot):
        k = step // 2
        odd = lax.rem(k, 2)
        dz = 4 + (k // 2) * (1 - odd) - ((k + 1) // 2) * odd
        place = lax.rem(column // 2 * 2 + 2 * dz, 16) + lax.rem(step, 2)
        peer = 16 * core + place

        is_hot = jnp.logical_or(peer < 4, peer >= 28)

        @pl.when(both(peer != tb, is_hot if hot else jnp.logical_not(is_hot)))
        def _():
            pltpu.make_async_remote_copy(
                tile(sums, place), recv.at[tb // 2], psend_sem, precv_sem,
                device_id={"tm": peer}, device_id_type=MESH,
            ).start()

        return carry

    lax.fori_loop(0, 16, functools.partial(send, hot=True), 0)
    lax.fori_loop(0, 16, functools.partial(send, hot=False), 0)
    keeps = tb // 16 == core

    @pl.when(keeps)
    def _():
        recv[tb // 2] = tile(sums, column)[...]

    for condition, _, copy in round_one:
        pl.when(condition)(copy.wait_send)

    swap.wait_send()

    def sent_edges(side):
        pltpu.make_async_remote_copy(
            edges.at[side], edges.at[side], esend_sem.at[side], erecv_sem, device_id=partner, device_id_type=MESH
        ).wait_send()

    pl.when(has_left)(lambda: sent_edges(0))
    pl.when(has_right)(lambda: sent_edges(1))

    def settle(number):
        pieces = pltpu.make_async_remote_copy(
            recv.at[0:number], recv.at[0:number], psend_sem, precv_sem, device_id=partner, device_id_type=MESH
        )
        pieces.wait_send()
        pieces.wait_recv()

    pl.when(keeps)(lambda: settle(15))
    pl.when(jnp.logical_not(keeps))(lambda: settle(16))

    @pl.when(is_edge)
    def _():
        pltpu.make_async_remote_copy(
            recv_e, recv_e, psend_sem, erecv_sem, device_id=partner, device_id_type=MESH
        ).wait_recv()

    before = jnp.zeros((4, 128), F32)
    for k in range(8):
        block = recv[2 * k] + recv[2 * k + 1]
        block = block + (
            (recv_e[4 * k] + recv_e[4 * k + 1]) + (recv_e[4 * k + 2] + recv_e[4 * k + 3])
        )
        level = block[0:4] + before
        before = block[4:8]
        for c in range(4):
            coarse[c, k : k + 1, :] = level[c : c + 1]


def store(smoothed_in, coarse_in, smoothed, coarse, sems):
    copies = [
        pltpu.make_async_copy(smoothed_in, smoothed, sems.at[0]),
        pltpu.make_async_copy(coarse_in, coarse, sems.at[1]),
    ]
    for copy in copies:
        copy.start()
    for copy in copies:
        copy.wait()


def per_device(initial_guess, forcing, visc_table, visc_class, inverse_bank, patch_kind):
    hbm = pl.BlockSpec(memory_space=pltpu.HBM)
    vmem = pl.BlockSpec(memory_space=pltpu.VMEM)
    dma = pltpu.SemaphoreType.DMA
    smoothed, coarse = pl.pallas_call(
        kernel,
        out_shape=(
            pltpu.VMEM((4, 8, 4, 8, 128), F32),
            pltpu.VMEM((4, 8, 128), F32),
        ),
        in_specs=[hbm] * 7,
        out_specs=(vmem, vmem),
        scratch_shapes=[
            pltpu.SMEM((8,), F32),
            pltpu.VMEM((4, 8, 128), jnp.int32),
            pltpu.VMEM((4, 32, 32), BF16),
            pltpu.VMEM((4, 2, 64), jnp.int32),
            pltpu.VMEM((4, 8, 4, 8, 128), F32),
            pltpu.VMEM((4, 8, 4, 8, 128), F32),
            pltpu.VMEM((4, 8, 4, 8, 128), F32),
            pltpu.VMEM((4, 8, 4, 8, 128), F32),
            pltpu.VMEM((4, 8, 4, 8, 128), F32),
            pltpu.VMEM((3, 4, 8, 128), F32),
            pltpu.VMEM((3, 4, 8, 128), F32),
            pltpu.VMEM((4, 8, 4, 128), F32),
            pltpu.VMEM((4, 8, 4, 128), F32),
            pltpu.VMEM((4, 8, 4, 128), F32),
            pltpu.VMEM((4, 8, 4, 128), F32),
            pltpu.VMEM((4, 8, 8, 128), F32),
            pltpu.VMEM((4, 8, 8, 128), F32),
            pltpu.VMEM((4, 4, 8, 128), F32),
            pltpu.VMEM((4, 8, 128), F32),
            pltpu.VMEM((4, 8, 128), F32),
            pltpu.VMEM((2, 16, 128), F32),
            pltpu.VMEM((2, 16, 128), F32),
            pltpu.VMEM((2, 4, 128), F32),
            pltpu.VMEM((2, 4, 4, 8, 128), F32),
            pltpu.VMEM((4, 4, 8, 128), F32),
            pltpu.VMEM((8, 4, 8, 128), F32),
            pltpu.VMEM((64, 256), BF16),
            pltpu.VMEM((6, 4, 16, 128), BF16),
            pltpu.VMEM((2, 4, 4, 8, 128), F32),
            pltpu.VMEM((256, 128), F32),
            pltpu.VMEM((2, 32, 128), F32),
            pltpu.VMEM((128, 128), F32),
            pltpu.VMEM((128, 128), F32),
            pltpu.VMEM((16, 8, 128), F32),
            pltpu.VMEM((32, 8, 128), F32),
            dma((6,)),
            dma((12,)),
            dma((12,)),
            dma,
            dma,
            dma((2,)),
            dma,
            pltpu.SemaphoreType.REGULAR((5,)),
            dma,
            dma,
        ],
        compiler_params=pltpu.CompilerParams(
            collective_id=0, has_side_effects=True, vmem_limit_bytes=60 * 1024 * 1024
        ),
    )(
        initial_guess,
        initial_guess.reshape(4, 8, 4, 8, 128),
        forcing.reshape(4, 8, 4, 8, 128),
        visc_table,
        visc_class.reshape(4, 8, 128),
        inverse_bank,
        patch_kind,
    )
    smoothed, coarse = pl.pallas_call(
        store,
        out_shape=(
            jax.ShapeDtypeStruct((4, 8, 4, 8, 128), F32),
            jax.ShapeDtypeStruct((4, 8, 128), F32),
        ),
        in_specs=[pl.BlockSpec(memory_space=pl.ANY)] * 2,
        out_specs=(pl.BlockSpec(memory_space=pl.ANY),) * 2,
        scratch_shapes=[dma((2,))],
        compiler_params=pltpu.CompilerParams(vmem_limit_bytes=4 * 1024 * 1024),
    )(smoothed, coarse)
    return smoothed.reshape(4, 8, 8, 4, 128), coarse


def solution(mesh):
    return jax.shard_map(
        per_device,
        mesh=mesh,
        in_specs=(
            P(None, "tm", "space", None, None),
            P(None, "tm", "space", None, None),
            P(),
            P("space", None, None),
            P(),
            P("space", None, None),
        ),
        out_specs=(P(None, "tm", "space", None, None), P(None, None, ("space", "tm"))),
        check_vma=False,
    )
```
